32 devices in a mesh: dp: 8 (over y, x, core), mp: 4 (over z).
Axes of the slice: x: 2, y: 2, z: 4, core: 2. Of those that a mesh axis runs over, the one named last changes fastest.
Arguments:
- tokens: bfloat16 [8192, 2048], P('dp', 'mp'), may hold values from -79.19596 to 79.19596
- seq_lengths: int32 [8, 3], P('dp'), may hold values from 1 to 640, 1024 in all within a row
- gain_first: bfloat16 [2048], replicated, may hold values from 0.5 to 1.5
- lin_query: bfloat16 [2048, 256], P(None, 'mp'), may hold values from -0.125 to 0.125
- lin_key: bfloat16 [2048, 256], P(None, 'mp'), may hold values from -0.125 to 0.125
- lin_value: bfloat16 [2048, 2048], P(None, 'mp'), may hold values from -0.125 to 0.125
- lin_out: bfloat16 [2048, 2048], P('mp'), may hold values from -3 to 3
- gain_second: bfloat16 [2048], replicated, may hold values from 0.5 to 1.5
- win_query: bfloat16 [2048, 2048], P(None, 'mp'), may hold values from -0.125 to 0.125
- win_key: bfloat16 [2048, 2048], P(None, 'mp'), may hold values from -0.125 to 0.125
- win_value: bfloat16 [2048, 2048], P(None, 'mp'), may hold values from -0.125 to 0.125
- win_out: bfloat16 [2048, 2048], P('mp'), may hold values from -0.75 to 0.75
- gain_third: bfloat16 [2048], replicated, may hold values from 0.5 to 1.5
- gate_weight: bfloat16 [2048, 5632], P(None, 'mp'), may hold values from -0.125 to 0.125
- up_weight: bfloat16 [2048, 5632], P(None, 'mp'), may hold values from -0.125 to 0.125
- down_weight: bfloat16 [5632, 2048], P('mp'), may hold values from -0.078125 to 0.078125
- out_cotangent: bfloat16 [8192, 2048], P('dp', 'mp'), may hold values from -6 to 6
Outputs:
- block_out: bfloat16 [8192, 2048], P('dp', 'mp')
- tokens_grad: float32 [8192, 2048], P('dp', 'mp')
- gain_first_grad: float32 [2048], P('mp')
- lin_query_grad: float32 [2048, 256], P(None, 'mp')
- lin_key_grad: float32 [2048, 256], P(None, 'mp')
- lin_value_grad: float32 [2048, 2048], P(None, 'mp')
- lin_out_grad: float32 [2048, 2048], P('mp')
- gain_second_grad: float32 [2048], P('mp')
- win_query_grad: float32 [2048, 2048], P(None, 'mp')
- win_key_grad: float32 [2048, 2048], P(None, 'mp')
- win_value_grad: float32 [2048, 2048], P(None, 'mp')
- win_out_grad: float32 [2048, 2048], P('mp')
- gain_third_grad: float32 [2048], P('mp')
- gate_weight_grad: float32 [2048, 5632], P(None, 'mp')
- up_weight_grad: float32 [2048, 5632], P(None, 'mp')
- down_weight_grad: float32 [5632, 2048], P('mp')
- rms_values: float32 [5], replicated
The draws below stay inside these ranges and needn't reach their ends.
Inputs may be any that keep to these rules, and one draw needn't show every extreme that they name: `seq_lengths`: for each group of 1024 slots: the length of its first sequence, of its second sequence and of its trailing padding, in that order; the three sum to 1024, and the largest of them is exactly five eighths of 1024, rounded down.
All inputs are finite; a program needn't handle non-finite values.
Results may differ from the reference program's by a relative error of at most 0.018.
Values may be sent and summed in bfloat16 or wider, within the bound.
No kernel may reach another device: no remote copies, remote signals or barrier semaphores. Data moves between devices by JAX's collectives and lax.ppermute only.
A program may use at most 320 MiB of HBM per device.

```python
import math
import jax
import jax.numpy as jnp
import numpy as np
from jax import lax

D = 2048
H = 16
FEATURE_SIZE = 16
HEAD_DIM = 128
WINDOW = 64
FF = 5632
TOK_DEV = 1024
GROUPS = 8
TOKENS = 8192


def draw_tokens(key, part):
    base_key, pick_key = jax.random.split(key)
    row_index = jnp.arange(TOKENS, dtype=jnp.int32) // TOK_DEV
    row_frac = row_index.astype(jnp.float32) / max(GROUPS - 1, 1)
    col_frac = jnp.arange(D, dtype=jnp.float32) / D
    outlier_count = max(1, D // 256)
    outlier_boost = float(D // (2 * outlier_count)) ** 0.5
    chosen = jax.random.permutation(pick_key, D)[:outlier_count]
    outlier_mask = jnp.sum((jnp.arange(D, dtype=jnp.int32)[None, :] == chosen[:, None]).astype(jnp.float32), axis=0)
    col_scale = 0.8 * 1.5 ** col_frac * (1.0 + (outlier_boost - 1.0) * outlier_mask)
    base = jnp.clip(jax.random.normal(base_key, (TOKENS, D), jnp.float32), -4.0, 4.0)
    row_scale = 0.7 * 2.0 ** row_frac
    return (base * row_scale[:, None] * col_scale[None, :]).astype(jnp.bfloat16)


def shard_levels(stream_key, extent, shards, smallest, top_value):
    def one(position, parts):
        steps = jax.random.uniform(jax.random.fold_in(jax.random.fold_in(stream_key, 6), position), (parts,), jnp.float32, smallest / len(shards), top_value / len(shards))
        return jnp.repeat(jnp.exp(steps), extent[position] // parts).reshape((-1,) + (1,) * (len(extent) - position - 1))

    loudness = one(*shards[0])
    for cut in shards[1:]:
        loudness = loudness * one(*cut)
    return loudness


def profile(count, total, most, slope):
    loads = [(1 << 20) // math.isqrt(grade ** slope) + 1 for grade in range(2, count + 1)]
    spare, given = total - most - (count - 1), [1] * (count - 1)
    while spare > 0:
        movable = [i for i in range(count - 1) if given[i] < most]
        whole, budget = sum([loads[i] for i in movable]), spare
        for i in movable:
            more = min(most - given[i], max(1, budget * loads[i] // whole), spare)
            given[i] = given[i] + more
            spare = spare - more
    return np.array([most] + given)


def ragged(own_key, count, total, reach, slope):
    if count == 2:
        one = jax.random.randint(own_key, (), max(1, total - reach), min(reach, total - 1) + 1)
        return jnp.stack([one, total - one])
    sizes = jnp.asarray(profile(count, total, reach, slope), jnp.int32)
    couples = (count - 1) // 2
    giver, sink = sizes[1:1 + 2 * couples:2], sizes[2:2 + 2 * couples:2]
    slack = jnp.minimum(giver - 1, reach - sink)
    shifted = jax.random.randint(jax.random.fold_in(own_key, 1), (couples,), 0, 1 << 20) % (slack + 1)
    sizes = sizes.at[1:1 + 2 * couples:2].set(giver - shifted).at[2:2 + 2 * couples:2].set(sink + shifted)
    return sizes[jax.random.permutation(jax.random.fold_in(own_key, 2), count)]


def centred(stream_key, shape, scale, most, cuts=(), held_as=jnp.bfloat16):
    level = shard_levels(stream_key, shape, cuts, -0.22, 0.18) if cuts else 1.0
    entries = jax.random.normal(stream_key, shape, jnp.float32) * scale * level
    return jnp.minimum(jnp.maximum(entries, -most), most).astype(held_as)


def setup_inputs(seed: int = 0) -> dict:
    streams_of = jax.random.split(jax.random.key(seed), 18)
    tokens = draw_tokens(jax.random.fold_in(streams_of[17], 71), 0)
    seq_lengths = jax.vmap(lambda own: ragged(own, 3, TOK_DEV, TOK_DEV * 5 // 8, 2))(jax.random.split(streams_of[1], GROUPS)).reshape((GROUPS, 3)).astype(jnp.int32)
    gain_first = jnp.clip(1.0 + 0.1 * jax.random.normal(streams_of[2], (D,), jnp.float32), 0.5, 1.5).astype(jnp.bfloat16)
    lin_query = centred(streams_of[3], (D, H * FEATURE_SIZE), D ** -0.5, 0.125, ((1, 4),))
    lin_key = centred(streams_of[4], (D, H * FEATURE_SIZE), D ** -0.5, 0.125, ((1, 4),))
    lin_value = centred(streams_of[5], (D, H * HEAD_DIM), D ** -0.5, 0.125, ((1, 4),))
    lin_out = centred(streams_of[6], (H * HEAD_DIM, D), (max(1, H * HEAD_DIM // 512)) ** -0.5, 3.0, ((0, 4),))
    gain_second = jnp.clip(1.0 + 0.1 * jax.random.normal(streams_of[7], (D,), jnp.float32), 0.5, 1.5).astype(jnp.bfloat16)
    win_query = centred(streams_of[8], (D, H * HEAD_DIM), D ** -0.5, 0.125, ((1, 4),))
    win_key = centred(streams_of[9], (D, H * HEAD_DIM), D ** -0.5, 0.125, ((1, 4),))
    win_value = centred(streams_of[10], (D, H * HEAD_DIM), D ** -0.5, 0.125, ((1, 4),))
    win_out = centred(streams_of[11], (H * HEAD_DIM, D), (max(1, H * HEAD_DIM // 32)) ** -0.5, 0.75, ((0, 4),))
    gain_third = jnp.clip(1.0 + 0.1 * jax.random.normal(streams_of[12], (D,), jnp.float32), 0.5, 1.5).astype(jnp.bfloat16)
    gate_weight = centred(streams_of[13], (D, FF), D ** -0.5, 0.125, ((1, 4),))
    up_weight = centred(streams_of[14], (D, FF), D ** -0.5, 0.125, ((1, 4),))
    down_weight = centred(streams_of[15], (FF, D), FF ** -0.5, 0.078125, ((0, 4),))
    out_cotangent = centred(streams_of[16], (TOKENS, D), 1.0, 6.0, ((0, 8), (1, 4)))
    return dict(tokens=tokens, seq_lengths=seq_lengths, gain_first=gain_first, lin_query=lin_query, lin_key=lin_key, lin_value=lin_value, lin_out=lin_out, gain_second=gain_second, win_query=win_query, win_key=win_key, win_value=win_value, win_out=win_out, gain_third=gain_third, gate_weight=gate_weight, up_weight=up_weight, down_weight=down_weight, out_cotangent=out_cotangent)


EPSILON = 1e-05
NEGATIVE = -1e+30
TOP_PRECISION = lax.Precision.HIGHEST

@jax.custom_vjp
def low(v):
    return lax.optimization_barrier(v.astype(jnp.bfloat16)).astype(jnp.float32)

@jax.custom_vjp
def low_back(v):
    return v

def low_keep(v):
    return (low(v), None)

def low_pass(kept, grad):
    return (grad,)

def back_keep(v):
    return (v, None)

def back_low(kept, grad):
    return (low(grad),)
low.defvjp(low_keep, low_pass)
low_back.defvjp(back_keep, back_low)

def matmul(left_side, right_side):
    return jnp.dot(left_side, right_side, precision=TOP_PRECISION, preferred_element_type=jnp.float32)

def rms_norm(values, gain_vector):
    return low(values * lax.rsqrt(lax.optimization_barrier(jnp.mean(values * values, axis=-1, keepdims=True)) + EPSILON) * gain_vector)

def project(normed, weight, head_width):
    return low_back(low(matmul(normed, weight))).reshape(normed.shape[0], -1, head_width)

def linear_attention(queries, key_rows_matrix, value_vectors, segments):
    row_count = queries.shape[0]
    block_rows = min(512, row_count)
    positions = jnp.arange(row_count, dtype=jnp.int32)

    def one_block(begin_row):
        query_tile_rows = lax.dynamic_slice_in_dim(queries, begin_row, block_rows)
        query_segment = lax.dynamic_slice_in_dim(segments, begin_row, block_rows)
        query_place = begin_row + jnp.arange(block_rows, dtype=jnp.int32)
        attention_logits = low_back(jnp.einsum('uao,sao->aus', query_tile_rows, key_rows_matrix, precision=TOP_PRECISION) * FEATURE_SIZE ** (-0.5))
        allowed = (positions[None, :] <= query_place[:, None]) & (segments[None, :] == query_segment[:, None])
        kernel = jnp.where(allowed[None], 1.0 + attention_logits + 0.5 * attention_logits * attention_logits, 0.0)
        totals = lax.optimization_barrier(jnp.sum(kernel, axis=2))
        numerator = low_back(jnp.einsum('hqk,khd->qhd', low(kernel), value_vectors, precision=TOP_PRECISION))
        return low(numerator / jnp.transpose(totals)[:, :, None])
    starts = jnp.arange(row_count // block_rows, dtype=jnp.int32) * block_rows
    return lax.map(jax.checkpoint(one_block), starts).reshape(row_count, -1)

def window_attention(queries, key_rows_matrix, value_vectors, segments):
    row_count, head_count, head_width = queries.shape
    block_rows = min(512, row_count)
    padding = jnp.zeros((WINDOW, head_count, head_width), queries.dtype)
    padded_keys = jnp.concatenate([padding, key_rows_matrix], axis=0)
    padded_values = jnp.concatenate([padding, value_vectors], axis=0)
    padded_segments = jnp.concatenate([jnp.full((WINDOW,), -1, jnp.int32), segments])

    def one_block(begin_row):
        query_tile_rows = lax.dynamic_slice_in_dim(queries, begin_row, block_rows)
        key_block = lax.dynamic_slice_in_dim(padded_keys, begin_row, block_rows + WINDOW)
        value_block = lax.dynamic_slice_in_dim(padded_values, begin_row, block_rows + WINDOW)
        key_segment = lax.dynamic_slice_in_dim(padded_segments, begin_row, block_rows + WINDOW)
        query_segment = lax.dynamic_slice_in_dim(segments, begin_row, block_rows)
        query_place = begin_row + jnp.arange(block_rows, dtype=jnp.int32)
        key_place = begin_row - WINDOW + jnp.arange(block_rows + WINDOW, dtype=jnp.int32)
        allowed = (key_place[None, :] <= query_place[:, None]) & (key_place[None, :] > query_place[:, None] - WINDOW) & (key_segment[None, :] == query_segment[:, None])
        attention_logits = low_back(jnp.einsum('qhd,khd->hqk', query_tile_rows, key_block, precision=TOP_PRECISION) * head_width ** (-0.5))
        weights = jax.nn.softmax(jnp.where(allowed[None], attention_logits, NEGATIVE), axis=-1)
        return low(low_back(jnp.einsum('hqk,khd->qhd', low(weights), value_block, precision=TOP_PRECISION)))
    starts = jnp.arange(row_count // block_rows, dtype=jnp.int32) * block_rows
    return lax.map(jax.checkpoint(one_block), starts).reshape(row_count, -1)

def block_forward(weights, inputs, lengths):
    gain_first, lin_query, lin_key, lin_value, lin_out, gain_second, win_query, win_key, win_value, win_out, gain_third, gate_weight, up_weight, down_weight = weights
    row_count = inputs.shape[0]
    positions = jnp.arange(row_count, dtype=jnp.int32)
    first_end = lengths[0]
    second_end = lengths[0] + lengths[1]
    segments = (positions >= first_end).astype(jnp.int32) + (positions >= second_end).astype(jnp.int32)
    validity = (positions < second_end).astype(inputs.dtype)
    normed_first = rms_norm(inputs, gain_first)
    mixed_first = linear_attention(project(normed_first, lin_query, FEATURE_SIZE), project(normed_first, lin_key, FEATURE_SIZE), project(normed_first, lin_value, HEAD_DIM), segments)
    branch_first = low_back(matmul(mixed_first, lin_out))
    resid_one = inputs + branch_first
    normed_second = rms_norm(resid_one, gain_second)
    mixed_second = window_attention(project(normed_second, win_query, HEAD_DIM), project(normed_second, win_key, HEAD_DIM), project(normed_second, win_value, HEAD_DIM), segments)
    branch_second = low_back(matmul(mixed_second, win_out))
    resid_two = resid_one + branch_second
    normed_third = rms_norm(resid_two, gain_third)
    gate_values = low_back(matmul(normed_third, gate_weight))
    upper_values = low_back(matmul(normed_third, up_weight))
    hidden = low(jax.nn.silu(gate_values) * upper_values)
    branch_third = low_back(matmul(hidden, down_weight))
    output = resid_two + branch_third

    def squares(values):
        return jnp.sum(validity * lax.optimization_barrier(jnp.sum(values * values, axis=1)))
    stats = jnp.stack([squares(inputs), squares(branch_first), squares(branch_second), squares(branch_third), squares(output), jnp.sum(validity)])
    return (output, stats)

def reference(tokens, seq_lengths, gain_first, lin_query, lin_key, lin_value, lin_out, gain_second, win_query, win_key, win_value, win_out, gain_third, gate_weight, up_weight, down_weight, out_cotangent):
    weight_list = [weight.astype(jnp.float32) for weight in (gain_first, lin_query, lin_key, lin_value, lin_out, gain_second, win_query, win_key, win_value, win_out, gain_third, gate_weight, up_weight, down_weight)]
    inputs = tokens.astype(jnp.float32)
    group_count = seq_lengths.shape[0]

    def forward(values, *weights):

        def one_group(pair):
            return block_forward(weights, pair[0], pair[1])
        outputs, stats = lax.map(jax.checkpoint(one_group), (values.reshape(group_count, -1, values.shape[1]), seq_lengths))
        return (outputs.reshape(values.shape), lax.optimization_barrier(jnp.sum(stats, axis=0)))
    output, pullback, stats = jax.vjp(forward, inputs, *weight_list, has_aux=True)
    positions = jnp.arange(TOK_DEV, dtype=jnp.int32)
    validity = (positions[None, :] < (seq_lengths[:, 0] + seq_lengths[:, 1])[:, None]).astype(jnp.float32).reshape(-1)
    cotangent = out_cotangent.astype(jnp.float32) * validity[:, None]
    grads = pullback(cotangent)
    rms = jnp.sqrt(stats[:5] / (stats[5] * D))
    return (output.astype(jnp.bfloat16), grads[0], grads[1], grads[2], grads[3], grads[4], grads[5], grads[6], grads[7], grads[8], grads[9], grads[10], grads[11], grads[12], grads[13], grads[14], rms)
```

```python
import jax
import jax.numpy as jnp
from jax import lax
from jax.sharding import PartitionSpec as P

FEATURE_SIZE = 16
HEAD_DIM = 128
WINDOW = 64


EPSILON = 1e-05
NEGATIVE = -1e30


def segment_info(lengths, row_count):
    positions = jnp.arange(row_count, dtype=jnp.int32)
    first_end = lengths[0, 0]
    second_end = lengths[0, 0] + lengths[0, 1]
    segments = (positions >= first_end).astype(jnp.int32) + (positions >= second_end).astype(
        jnp.int32
    )
    validity = (positions < second_end).astype(jnp.float32)
    return (segments, validity)


def times_transposed(left_side, right_side):
    return lax.dot_general(
        left_side, right_side, (((1,), (1,)), ((), ())), preferred_element_type=jnp.float32
    )


def transposed_times(left_side, right_side):
    return lax.dot_general(
        left_side, right_side, (((0,), (0,)), ((), ())), preferred_element_type=jnp.float32
    )


def gather_stream(shard_part):
    return lax.all_gather(shard_part.astype(jnp.bfloat16), "mp", axis=1, tiled=True).astype(
        jnp.float32
    )


def branch_total(partial_value):
    return lax.psum_scatter(
        partial_value.astype(jnp.bfloat16), "mp", scatter_dimension=1, tiled=True
    ).astype(jnp.float32)


def gather_cotangent(shard_part):
    return lax.all_gather(shard_part, "mp", axis=1, tiled=True)


def sum_groups(values):
    narrow = tuple(v.astype(jnp.bfloat16) if v.ndim == 2 else v for v in values)
    return tuple(v.astype(jnp.float32) for v in lax.psum(narrow, "dp"))


def rms_forward(full_stream, gain_vector):
    inverse = lax.rsqrt(jnp.mean(full_stream * full_stream, axis=1) + EPSILON)
    normed = (full_stream * inverse[:, None] * gain_vector.astype(jnp.float32)).astype(jnp.bfloat16)
    return (normed, inverse)


def norm_backward(partial_value, resid_part, inverse, gain_part, model_width, carried):
    shard_grad = branch_total(partial_value)
    scaled = shard_grad * gain_part
    normed_part = resid_part * inverse[:, None]
    row_dot = lax.psum(jnp.sum(scaled * normed_part, axis=1), "mp")
    input_grad = carried + inverse[:, None] * (
        scaled - normed_part * (row_dot / model_width)[:, None]
    )
    gain_grad = jnp.sum(shard_grad * normed_part, axis=0)
    return (input_grad, gain_grad)


def linear_scores(query_tile_rows, key_rows_matrix, segments, begin_row, score_scale):
    block_rows = query_tile_rows.shape[0]
    attention_logits = (
        jnp.einsum(
            "uao,sao->aus", query_tile_rows, key_rows_matrix, preferred_element_type=jnp.float32
        )
        * score_scale
    )
    query_place = begin_row + jnp.arange(block_rows, dtype=jnp.int32)
    key_place = jnp.arange(key_rows_matrix.shape[0], dtype=jnp.int32)
    query_segment = lax.dynamic_slice_in_dim(segments, begin_row, block_rows)
    allowed = (key_place[None, :] <= query_place[:, None]) & (
        segments[None, :] == query_segment[:, None]
    )
    kernel = jnp.where(
        allowed[None], 1.0 + attention_logits + 0.5 * attention_logits * attention_logits, 0.0
    )
    return (attention_logits, allowed, kernel)


def linear_forward(queries, key_rows_matrix, value_vectors, segments, block_rows, score_scale):
    row_count = queries.shape[0]

    def one_block(begin_row):
        query_tile_rows = lax.dynamic_slice_in_dim(queries, begin_row, block_rows)
        attention_logits, allowed, kernel = linear_scores(
            query_tile_rows, key_rows_matrix, segments, begin_row, score_scale
        )
        totals = jnp.sum(kernel, axis=2)
        numerator = jnp.einsum(
            "hqk,khd->qhd",
            kernel.astype(jnp.bfloat16),
            value_vectors,
            preferred_element_type=jnp.float32,
        )
        return (numerator / jnp.transpose(totals)[:, :, None]).astype(jnp.bfloat16)

    starts = jnp.arange(row_count // block_rows, dtype=jnp.int32) * block_rows
    return lax.map(one_block, starts).reshape(row_count, -1)


def linear_backward(
    queries, key_rows_matrix, value_vectors, segments, out_grad, block_rows, score_scale
):
    row_count = queries.shape[0]

    def one_block(running, begin_row):
        key_total, value_total = running
        query_tile_rows = lax.dynamic_slice_in_dim(queries, begin_row, block_rows)
        grad_block = lax.dynamic_slice_in_dim(out_grad, begin_row, block_rows)
        attention_logits, allowed, kernel = linear_scores(
            query_tile_rows, key_rows_matrix, segments, begin_row, score_scale
        )
        totals = jnp.transpose(jnp.sum(kernel, axis=2))
        kernel_low = kernel.astype(jnp.bfloat16)
        numerator = jnp.einsum(
            "hqk,khd->qhd", kernel_low, value_vectors, preferred_element_type=jnp.float32
        )
        numer_grad = (grad_block / totals[:, :, None]).astype(jnp.bfloat16)
        total_grad = -jnp.sum(grad_block * numerator, axis=2) / (totals * totals)
        kernel_grad = (
            jnp.einsum(
                "qhd,khd->hqk", numer_grad, value_vectors, preferred_element_type=jnp.float32
            )
            + jnp.transpose(total_grad)[:, :, None]
        )
        kernel_grad = jnp.where(allowed[None], kernel_grad, 0.0)
        scores_gradient = (kernel_grad * (1.0 + attention_logits)).astype(jnp.bfloat16)
        value_total = value_total + jnp.einsum(
            "hqk,qhd->khd", kernel_low, numer_grad, preferred_element_type=jnp.float32
        )
        key_total = (
            key_total
            + jnp.einsum(
                "pco,cpu->opu", scores_gradient, query_tile_rows, preferred_element_type=jnp.float32
            )
            * score_scale
        )
        query_grad = (
            jnp.einsum(
                "mwb,bmx->wmx", scores_gradient, key_rows_matrix, preferred_element_type=jnp.float32
            )
            * score_scale
        )
        return ((key_total, value_total), query_grad)

    initial = (
        jnp.zeros(key_rows_matrix.shape, jnp.float32),
        jnp.zeros(value_vectors.shape, jnp.float32),
    )
    starts = jnp.arange(row_count // block_rows, dtype=jnp.int32) * block_rows
    (key_total, value_total), query_grads = lax.scan(one_block, initial, starts)
    return (query_grads.reshape(queries.shape), key_total, value_total)


def pad_front(values, window_rows):
    return jnp.concatenate(
        [jnp.zeros((window_rows,) + values.shape[1:], values.dtype), values], axis=0
    )


def window_scores(
    query_tile_rows, key_block, padded_segments, segments, begin_row, window_rows, score_scale
):
    block_rows = query_tile_rows.shape[0]
    query_segment = lax.dynamic_slice_in_dim(segments, begin_row, block_rows)
    key_segment = lax.dynamic_slice_in_dim(padded_segments, begin_row, block_rows + window_rows)
    query_place = begin_row + jnp.arange(block_rows, dtype=jnp.int32)
    key_place = begin_row - window_rows + jnp.arange(block_rows + window_rows, dtype=jnp.int32)
    allowed = (
        (key_place[None, :] <= query_place[:, None])
        & (key_place[None, :] > query_place[:, None] - window_rows)
        & (key_segment[None, :] == query_segment[:, None])
    )
    attention_logits = (
        jnp.einsum("qhd,khd->hqk", query_tile_rows, key_block, preferred_element_type=jnp.float32)
        * score_scale
    )
    return jnp.where(allowed[None], attention_logits, NEGATIVE)


def window_forward(
    queries, key_rows_matrix, value_vectors, segments, block_rows, window_rows, score_scale
):
    row_count = queries.shape[0]
    padded_keys = pad_front(key_rows_matrix, window_rows)
    padded_values = pad_front(value_vectors, window_rows)
    padded_segments = jnp.concatenate([jnp.full((window_rows,), -1, jnp.int32), segments])

    def one_block(begin_row):
        query_tile_rows = lax.dynamic_slice_in_dim(queries, begin_row, block_rows)
        key_block = lax.dynamic_slice_in_dim(padded_keys, begin_row, block_rows + window_rows)
        value_block = lax.dynamic_slice_in_dim(padded_values, begin_row, block_rows + window_rows)
        masked = window_scores(
            query_tile_rows,
            key_block,
            padded_segments,
            segments,
            begin_row,
            window_rows,
            score_scale,
        )
        row_max = jnp.max(masked, axis=2)
        exponent = jnp.exp(masked - row_max[:, :, None])
        totals = jnp.sum(exponent, axis=2)
        weights = exponent / totals[:, :, None]
        mixed = jnp.einsum(
            "hqk,khd->qhd",
            weights.astype(jnp.bfloat16),
            value_block,
            preferred_element_type=jnp.float32,
        )
        return (mixed.astype(jnp.bfloat16), row_max + jnp.log(totals))

    starts = jnp.arange(row_count // block_rows, dtype=jnp.int32) * block_rows
    mixed, log_totals = lax.map(one_block, starts)
    return (mixed.reshape(row_count, -1), log_totals)


def window_backward(
    queries,
    key_rows_matrix,
    value_vectors,
    segments,
    log_totals,
    out_grad,
    block_rows,
    window_rows,
    score_scale,
):
    row_count = queries.shape[0]
    padded_keys = pad_front(key_rows_matrix, window_rows)
    padded_values = pad_front(value_vectors, window_rows)
    padded_segments = jnp.concatenate([jnp.full((window_rows,), -1, jnp.int32), segments])

    def one_block(running, inputs):
        key_total, value_total = running
        begin_row, log_block = inputs
        query_tile_rows = lax.dynamic_slice_in_dim(queries, begin_row, block_rows)
        grad_block = lax.dynamic_slice_in_dim(out_grad, begin_row, block_rows)
        key_block = lax.dynamic_slice_in_dim(padded_keys, begin_row, block_rows + window_rows)
        value_block = lax.dynamic_slice_in_dim(padded_values, begin_row, block_rows + window_rows)
        masked = window_scores(
            query_tile_rows,
            key_block,
            padded_segments,
            segments,
            begin_row,
            window_rows,
            score_scale,
        )
        weights = jnp.exp(masked - log_block[:, :, None])
        weight_grad = jnp.einsum(
            "qhd,khd->hqk", grad_block, value_block, preferred_element_type=jnp.float32
        )
        row_delta = jnp.sum(weights * weight_grad, axis=2)
        scores_gradient = (weights * (weight_grad - row_delta[:, :, None])).astype(jnp.bfloat16)
        query_grad = (
            jnp.einsum(
                "hqk,khd->qhd", scores_gradient, key_block, preferred_element_type=jnp.float32
            )
            * score_scale
        )
        key_part = (
            jnp.einsum(
                "hqk,qhd->khd", scores_gradient, query_tile_rows, preferred_element_type=jnp.float32
            )
            * score_scale
        )
        value_part = jnp.einsum(
            "hqk,qhd->khd",
            weights.astype(jnp.bfloat16),
            grad_block,
            preferred_element_type=jnp.float32,
        )
        span = block_rows + window_rows
        key_total = lax.dynamic_update_slice_in_dim(
            key_total, lax.dynamic_slice_in_dim(key_total, begin_row, span) + key_part, begin_row, 0
        )
        value_total = lax.dynamic_update_slice_in_dim(
            value_total,
            lax.dynamic_slice_in_dim(value_total, begin_row, span) + value_part,
            begin_row,
            0,
        )
        return ((key_total, value_total), query_grad)

    padded_shape = (row_count + window_rows,) + key_rows_matrix.shape[1:]
    initial = (jnp.zeros(padded_shape, jnp.float32), jnp.zeros(padded_shape, jnp.float32))
    starts = jnp.arange(row_count // block_rows, dtype=jnp.int32) * block_rows
    (key_total, value_total), query_grads = lax.scan(one_block, initial, (starts, log_totals))
    return (query_grads.reshape(queries.shape), key_total[window_rows:], value_total[window_rows:])


def per_device(
    tokens,
    seq_lengths,
    gain_first,
    lin_query,
    lin_key,
    lin_value,
    lin_out,
    gain_second,
    win_query,
    win_key,
    win_value,
    win_out,
    gain_third,
    gate_weight,
    up_weight,
    down_weight,
    out_cotangent,
):
    row_count, shard_width = tokens.shape
    model_width = shard_width * lax.axis_size("mp")
    block_rows = min(512, row_count)
    heads_here = lin_query.shape[1] // FEATURE_SIZE
    offset = lax.axis_index("mp") * shard_width
    segments, validity = segment_info(seq_lengths, row_count)
    lin_scale = FEATURE_SIZE ** (-0.5)
    win_scale = HEAD_DIM ** (-0.5)
    resid_zero = tokens.astype(jnp.float32)
    stream_zero = gather_stream(resid_zero)
    normed_first, inverse_first = rms_forward(stream_zero, gain_first)
    lin_q = (
        jnp.dot(normed_first, lin_query, preferred_element_type=jnp.float32)
        .astype(jnp.bfloat16)
        .reshape(row_count, heads_here, FEATURE_SIZE)
    )
    lin_k = (
        jnp.dot(normed_first, lin_key, preferred_element_type=jnp.float32)
        .astype(jnp.bfloat16)
        .reshape(row_count, heads_here, FEATURE_SIZE)
    )
    lin_v = (
        jnp.dot(normed_first, lin_value, preferred_element_type=jnp.float32)
        .astype(jnp.bfloat16)
        .reshape(row_count, heads_here, HEAD_DIM)
    )
    lin_mixed = linear_forward(lin_q, lin_k, lin_v, segments, block_rows, lin_scale)
    branch_first = branch_total(jnp.dot(lin_mixed, lin_out, preferred_element_type=jnp.float32))
    resid_one = resid_zero + branch_first
    stream_one = gather_stream(resid_one)
    normed_second, inverse_second = rms_forward(stream_one, gain_second)
    win_q = (
        jnp.dot(normed_second, win_query, preferred_element_type=jnp.float32)
        .astype(jnp.bfloat16)
        .reshape(row_count, heads_here, HEAD_DIM)
    )
    win_k = (
        jnp.dot(normed_second, win_key, preferred_element_type=jnp.float32)
        .astype(jnp.bfloat16)
        .reshape(row_count, heads_here, HEAD_DIM)
    )
    win_v = (
        jnp.dot(normed_second, win_value, preferred_element_type=jnp.float32)
        .astype(jnp.bfloat16)
        .reshape(row_count, heads_here, HEAD_DIM)
    )
    win_mixed, log_totals = window_forward(
        win_q, win_k, win_v, segments, block_rows, WINDOW, win_scale
    )
    branch_second = branch_total(jnp.dot(win_mixed, win_out, preferred_element_type=jnp.float32))
    resid_two = resid_one + branch_second
    stream_two = gather_stream(resid_two)
    normed_third, inverse_third = rms_forward(stream_two, gain_third)
    gate_values = jnp.dot(normed_third, gate_weight, preferred_element_type=jnp.float32)
    upper_values = jnp.dot(normed_third, up_weight, preferred_element_type=jnp.float32)
    sigma = jax.nn.sigmoid(gate_values)
    hidden = (gate_values * sigma * upper_values).astype(jnp.bfloat16)
    branch_third = branch_total(jnp.dot(hidden, down_weight, preferred_element_type=jnp.float32))
    output_resid = resid_two + branch_third
    cot_shard = out_cotangent.astype(jnp.float32) * validity[:, None]
    cot_third = gather_cotangent(cot_shard.astype(jnp.bfloat16))
    grad_down = transposed_times(hidden, cot_third)
    hidden_grad = times_transposed(cot_third, down_weight)
    gate_grad = (hidden_grad * upper_values * sigma * (1.0 + gate_values * (1.0 - sigma))).astype(
        jnp.bfloat16
    )
    upper_grad = (hidden_grad * gate_values * sigma).astype(jnp.bfloat16)
    grad_gate = transposed_times(normed_third, gate_grad)
    grad_upper = transposed_times(normed_third, upper_grad)
    normed_third_grad = times_transposed(gate_grad, gate_weight) + times_transposed(
        upper_grad, up_weight
    )
    gain_third_part = lax.dynamic_slice_in_dim(gain_third, offset, shard_width).astype(jnp.float32)
    resid_two_grad, gain_third_grad = norm_backward(
        normed_third_grad, resid_two, inverse_third, gain_third_part, model_width, cot_shard
    )
    ffn_totals = (grad_gate, grad_upper, grad_down, gain_third_grad)
    cot_second = gather_cotangent(resid_two_grad.astype(jnp.bfloat16))
    grad_win_out = transposed_times(win_mixed, cot_second)
    win_mixed_grad = (
        times_transposed(cot_second, win_out)
        .astype(jnp.bfloat16)
        .reshape(row_count, heads_here, HEAD_DIM)
    )
    win_q_grad, win_k_grad, win_v_grad = window_backward(
        win_q, win_k, win_v, segments, log_totals, win_mixed_grad, block_rows, WINDOW, win_scale
    )
    win_q_low = win_q_grad.astype(jnp.bfloat16).reshape(row_count, heads_here * HEAD_DIM)
    win_k_low = win_k_grad.astype(jnp.bfloat16).reshape(row_count, heads_here * HEAD_DIM)
    win_v_low = win_v_grad.astype(jnp.bfloat16).reshape(row_count, heads_here * HEAD_DIM)
    grad_win_query = transposed_times(normed_second, win_q_low)
    grad_win_key = transposed_times(normed_second, win_k_low)
    grad_win_value = transposed_times(normed_second, win_v_low)
    normed_second_grad = (
        times_transposed(win_q_low, win_query)
        + times_transposed(win_k_low, win_key)
        + times_transposed(win_v_low, win_value)
    )
    gain_second_part = lax.dynamic_slice_in_dim(gain_second, offset, shard_width).astype(
        jnp.float32
    )
    resid_one_grad, gain_second_grad = norm_backward(
        normed_second_grad, resid_one, inverse_second, gain_second_part, model_width, resid_two_grad
    )
    window_totals = (grad_win_query, grad_win_key, grad_win_value, grad_win_out, gain_second_grad)
    cot_first = gather_cotangent(resid_one_grad.astype(jnp.bfloat16))
    grad_lin_out = transposed_times(lin_mixed, cot_first)
    lin_mixed_grad = times_transposed(cot_first, lin_out).reshape(row_count, heads_here, HEAD_DIM)
    lin_q_grad, lin_k_grad, lin_v_grad = linear_backward(
        lin_q, lin_k, lin_v, segments, lin_mixed_grad, block_rows, lin_scale
    )
    lin_q_low = lin_q_grad.astype(jnp.bfloat16).reshape(row_count, heads_here * FEATURE_SIZE)
    lin_k_low = lin_k_grad.astype(jnp.bfloat16).reshape(row_count, heads_here * FEATURE_SIZE)
    lin_v_low = lin_v_grad.astype(jnp.bfloat16).reshape(row_count, heads_here * HEAD_DIM)
    grad_lin_query = transposed_times(normed_first, lin_q_low)
    grad_lin_key = transposed_times(normed_first, lin_k_low)
    grad_lin_value = transposed_times(normed_first, lin_v_low)
    normed_first_grad = (
        times_transposed(lin_q_low, lin_query)
        + times_transposed(lin_k_low, lin_key)
        + times_transposed(lin_v_low, lin_value)
    )
    gain_first_part = lax.dynamic_slice_in_dim(gain_first, offset, shard_width).astype(jnp.float32)
    input_grad, gain_first_grad = norm_backward(
        normed_first_grad, resid_zero, inverse_first, gain_first_part, model_width, resid_one_grad
    )
    linear_totals = (grad_lin_query, grad_lin_key, grad_lin_value, grad_lin_out, gain_first_grad)
    every_total = sum_groups(
        (
            linear_totals[0],
            linear_totals[1],
            linear_totals[2],
            linear_totals[3],
            linear_totals[4],
            window_totals[0],
            window_totals[1],
            window_totals[2],
            window_totals[3],
            window_totals[4],
            ffn_totals[0],
            ffn_totals[1],
            ffn_totals[2],
            ffn_totals[3],
        )
    )

    def masked_squares(values):
        return jnp.sum(validity * jnp.sum(values * values, axis=1))

    totals = lax.psum(
        (
            masked_squares(resid_zero),
            masked_squares(branch_first),
            masked_squares(branch_second),
            masked_squares(branch_third),
            masked_squares(output_resid),
            jnp.sum(validity),
        ),
        ("dp", "mp"),
    )
    count = totals[5] / lax.axis_size("mp")
    rms_values = jnp.sqrt(
        jnp.stack([totals[0], totals[1], totals[2], totals[3], totals[4]]) / (count * model_width)
    )
    return (
        output_resid.astype(jnp.bfloat16),
        input_grad,
        every_total[4],
        every_total[0],
        every_total[1],
        every_total[2],
        every_total[3],
        every_total[9],
        every_total[5],
        every_total[6],
        every_total[7],
        every_total[8],
        every_total[13],
        every_total[10],
        every_total[11],
        every_total[12],
        rms_values,
    )


def solution(mesh):
    in_specs = (
        P("dp", "mp"),
        P("dp", None),
        P(),
        P(None, "mp"),
        P(None, "mp"),
        P(None, "mp"),
        P("mp", None),
        P(),
        P(None, "mp"),
        P(None, "mp"),
        P(None, "mp"),
        P("mp", None),
        P(),
        P(None, "mp"),
        P(None, "mp"),
        P("mp", None),
        P("dp", "mp"),
    )
    out_specs = (
        P("dp", "mp"),
        P("dp", "mp"),
        P("mp"),
        P(None, "mp"),
        P(None, "mp"),
        P(None, "mp"),
        P("mp", None),
        P("mp"),
        P(None, "mp"),
        P(None, "mp"),
        P(None, "mp"),
        P("mp", None),
        P("mp"),
        P(None, "mp"),
        P(None, "mp"),
        P("mp", None),
        P(),
    )
    return jax.shard_map(
        per_device, mesh=mesh, in_specs=in_specs, out_specs=out_specs, check_vma=False
    )
```

```python
import functools

import jax
import jax.numpy as jnp
from jax import lax
from jax.experimental import pallas as pl
from jax.experimental.pallas import tpu as pltpu
from jax.sharding import PartitionSpec as P

FEATURE_SIZE = 16
HEAD_DIM = 128
WINDOW = 64
EPSILON = 1e-05
NEGATIVE = -1e30
CHUNKS = 2
LIN_SCALE = FEATURE_SIZE ** (-0.5)
WIN_SCALE = HEAD_DIM ** (-0.5)
F32 = jnp.float32
BF16 = jnp.bfloat16
PAD_ROWS = 16
VMEM_LIMIT = 40 * 1024 * 1024


def nn(left, right):
    return lax.dot_general(left, right, (((1,), (0,)), ((), ())), preferred_element_type=F32)


def nt(left, right):
    return lax.dot_general(left, right, (((1,), (1,)), ((), ())), preferred_element_type=F32)


def tn(left, right):
    return lax.dot_general(left, right, (((0,), (0,)), ((), ())), preferred_element_type=F32)


def segment_start(lens_ref, place):
    first_end = lens_ref[0, 0]
    second_end = first_end + lens_ref[0, 1]
    return jnp.where(place < first_end, 0, jnp.where(place < second_end, first_end, second_end))


def causal_allowed(lens_ref, row_begin, key_begin, rows, keys, window):
    place = row_begin + lax.broadcasted_iota(jnp.int32, (rows, 1), 0)
    key_place = key_begin + lax.broadcasted_iota(jnp.int32, (rows, keys), 1)
    lowest = segment_start(lens_ref, place)
    if window:
        lowest = jnp.maximum(lowest, place - (window - 1))
    allowed = key_place >= lowest
    if key_begin + keys > row_begin:
        allowed = allowed & (key_place <= place)
    return allowed


def head_lanes(values, head):
    lane = lax.broadcasted_iota(jnp.int32, values.shape, 1) // FEATURE_SIZE
    return jnp.where(lane == head, values, jnp.zeros_like(values))


def linear_tile(lens_ref, query, key, row_begin, key_begin):
    logits = nt(query, key) * LIN_SCALE
    allowed = causal_allowed(lens_ref, row_begin, key_begin, query.shape[0], key.shape[0], 0)
    kernel = jnp.where(allowed, 1.0 + logits + 0.5 * logits * logits, 0.0)
    return logits, allowed, kernel


def linear_forward_kernel(chunk, rows, tile, lens_ref, q_ref, *refs):
    count = chunk + 1
    k_refs, v_refs = refs[:count], refs[count : 2 * count]
    low_ref, mixed_ref, total_ref = refs[2 * count :]
    head = pl.program_id(0)
    per = rows // tile
    for i in range(per):
        row_begin = chunk * rows + i * tile
        query = q_ref[pl.ds(i * tile, tile), :]
        total = jnp.zeros((tile, 1), F32)
        number = jnp.zeros((tile, HEAD_DIM), F32)
        for j in range(chunk * per + i + 1):
            span = pl.ds((j % per) * tile, tile)
            key = head_lanes(k_refs[j // per][span, :], head)
            _, _, kernel = linear_tile(lens_ref, query, key, row_begin, j * tile)
            total += jnp.sum(kernel, axis=1, keepdims=True)
            number += nn(kernel.astype(BF16), v_refs[j // per][span, :])
        mixed = number / total
        low_ref[pl.ds(i * tile, tile), :] = mixed.astype(BF16)
        mixed_ref[pl.ds(i * tile, tile), :] = mixed
        total_ref[0, pl.ds(i * tile, tile), :] = total


def linear_backward_kernel(chunk, rows, tile, carried, lens_ref, q_ref, *refs):
    count = chunk + 1
    k_refs, v_refs = refs[:count], refs[count : 2 * count]
    do_ref, mixed_ref, total_ref = refs[2 * count : 2 * count + 3]
    refs = refs[2 * count + 3 :]
    if carried:
        dk_in, dv_in = refs[:2]
        refs = refs[2:]
    dq_out, dk_out, dv_out = refs[:3]
    dk_prev, dv_prev = refs[3 : 3 + chunk], refs[3 + chunk : 3 + 2 * chunk]
    dq_acc, dk_acc, dv_acc = refs[3 + 2 * chunk :]
    head = pl.program_id(0)
    last = pl.num_programs(0) - 1
    per = rows // tile

    @pl.when(head == 0)
    def _():
        dq_acc[...] = jnp.zeros_like(dq_acc)
        dk_acc[...] = jnp.zeros_like(dk_acc)
        if carried:
            dk_acc[pl.ds(chunk * rows, rows), :] = dk_in[...]

    dv_acc[...] = jnp.zeros_like(dv_acc)
    if carried:
        dv_acc[pl.ds(chunk * rows, rows), :] = dv_in[...]
    for i in range(per):
        row_begin = chunk * rows + i * tile
        own = pl.ds(i * tile, tile)
        query = head_lanes(q_ref[own, :], head)
        grad = do_ref[own, :]
        inverse = 1.0 / total_ref[0, own, :]
        number_grad = (grad * inverse).astype(BF16)
        total_grad = -jnp.sum(grad * mixed_ref[own, :], axis=1, keepdims=True) * inverse
        dq = jnp.zeros((tile, q_ref.shape[1]), F32)
        for j in range(chunk * per + i + 1):
            span = pl.ds((j % per) * tile, tile)
            key = head_lanes(k_refs[j // per][span, :], head)
            logits, allowed, kernel = linear_tile(lens_ref, query, key, row_begin, j * tile)
            kernel_grad = nt(number_grad, v_refs[j // per][span, :]) + total_grad
            scores_grad = jnp.where(allowed, kernel_grad * (1.0 + logits), 0.0).astype(BF16)
            dq += nn(scores_grad, key)
            keys = pl.ds(j * tile, tile)
            dk_acc[keys, :] += tn(scores_grad, query) * LIN_SCALE
            dv_acc[keys, :] += tn(kernel.astype(BF16), number_grad)
        dq_acc[own, :] += dq * LIN_SCALE
    dv_out[...] = dv_acc[pl.ds(chunk * rows, rows), :].astype(BF16)
    for c in range(chunk):
        dv_prev[c][...] = dv_acc[pl.ds(c * rows, rows), :]

    @pl.when(head == last)
    def _():
        dq_out[...] = dq_acc[...].astype(BF16)
        dk_out[...] = dk_acc[pl.ds(chunk * rows, rows), :].astype(BF16)
        for c in range(chunk):
            dk_prev[c][...] = dk_acc[pl.ds(c * rows, rows), :]


def window_tile(lens_ref, query, key, row_begin, key_begin):
    logits = nt(query, key) * WIN_SCALE
    allowed = causal_allowed(lens_ref, row_begin, key_begin, query.shape[0], key.shape[0], WINDOW)
    logits = jnp.where(allowed, logits, NEGATIVE)
    exponent = jnp.exp(logits - jnp.max(logits, axis=1, keepdims=True))
    return exponent / jnp.sum(exponent, axis=1, keepdims=True)


def window_keys(current_ref, prev_ref, i, tile):
    if i > 0:
        return current_ref[pl.ds(i * tile - WINDOW, tile + WINDOW), :], i * tile - WINDOW
    if prev_ref is not None:
        return jnp.concatenate([prev_ref[...], current_ref[pl.ds(0, tile), :]], axis=0), -WINDOW
    return current_ref[pl.ds(0, tile), :], 0


def window_forward_kernel(chunk, rows, tile, lens_ref, q_ref, k_ref, v_ref, *refs):
    k_prev, v_prev = refs[:2] if chunk else (None, None)
    out_ref = refs[-1]
    for i in range(rows // tile):
        own = pl.ds(i * tile, tile)
        key, key_begin = window_keys(k_ref, k_prev, i, tile)
        value, _ = window_keys(v_ref, v_prev, i, tile)
        base = chunk * rows
        weights = window_tile(lens_ref, q_ref[own, :], key, base + i * tile, base + key_begin)
        out_ref[own, :] = nn(weights.astype(BF16), value).astype(BF16)


def window_backward_kernel(chunk, rows, tile, carried, lens_ref, q_ref, k_ref, v_ref, *refs):
    k_prev, v_prev = refs[:2] if chunk else (None, None)
    refs = refs[2:] if chunk else refs
    do_ref, refs = refs[0], refs[1:]
    if carried:
        dk_in, dv_in = refs[:2]
        refs = refs[2:]
    dq_out, dk_out, dv_out = refs[:3]
    dk_back, dv_back = refs[3:5] if chunk else (None, None)
    dk_acc, dv_acc = refs[-2:]
    dk_acc[...] = jnp.zeros_like(dk_acc)
    dv_acc[...] = jnp.zeros_like(dv_acc)
    if carried:
        dk_acc[pl.ds(rows, WINDOW), :] = dk_in[...]
        dv_acc[pl.ds(rows, WINDOW), :] = dv_in[...]
    for i in range(rows // tile):
        own = pl.ds(i * tile, tile)
        key, key_begin = window_keys(k_ref, k_prev, i, tile)
        value, _ = window_keys(v_ref, v_prev, i, tile)
        base = chunk * rows
        query = q_ref[own, :]
        grad = do_ref[own, :]
        weights = window_tile(lens_ref, query, key, base + i * tile, base + key_begin)
        weight_grad = nt(grad, value)
        delta = jnp.sum(weights * weight_grad, axis=1, keepdims=True)
        scores_grad = (weights * (weight_grad - delta)).astype(BF16)
        dq_out[own, :] = (nn(scores_grad, key) * WIN_SCALE).astype(BF16)
        keys = pl.ds(WINDOW + key_begin, key.shape[0])
        dk_acc[keys, :] += tn(scores_grad, query) * WIN_SCALE
        dv_acc[keys, :] += tn(weights.astype(BF16), grad)
    dk_out[...] = dk_acc[pl.ds(WINDOW, rows), :].astype(BF16)
    dv_out[...] = dv_acc[pl.ds(WINDOW, rows), :].astype(BF16)
    if chunk:
        dk_back[...] = dk_acc[pl.ds(0, WINDOW), :]
        dv_back[...] = dv_acc[pl.ds(0, WINDOW), :]


SMEM_SPEC = pl.BlockSpec(memory_space=pltpu.SMEM)
PARAMS = pltpu.CompilerParams(
    dimension_semantics=("arbitrary",), vmem_limit_bytes=VMEM_LIMIT
)


def cost(flops, moved):
    return pl.CostEstimate(flops=flops, bytes_accessed=moved, transcendentals=0)


def narrow_spec(rows, width):
    return pl.BlockSpec((rows, width), lambda h: (0, 0))


def head_spec(rows):
    return pl.BlockSpec((rows, HEAD_DIM), lambda h: (0, h))


def total_spec(rows):
    return pl.BlockSpec((1, rows, 1), lambda h: (h, 0, 0))


def linear_forward(chunk, lengths, query, keys, values):
    rows, width = query.shape
    heads = width // FEATURE_SIZE
    tile = min(256, rows)
    count = chunk + 1
    wide = heads * HEAD_DIM
    return pl.pallas_call(
        functools.partial(linear_forward_kernel, chunk, rows, tile),
        grid=(heads,),
        in_specs=[SMEM_SPEC, narrow_spec(rows, width)]
        + [narrow_spec(rows, width)] * count
        + [head_spec(rows)] * count,
        out_specs=[head_spec(rows), head_spec(rows), total_spec(rows)],
        out_shape=[
            jax.ShapeDtypeStruct((rows, wide), BF16),
            jax.ShapeDtypeStruct((rows, wide), F32),
            jax.ShapeDtypeStruct((heads, rows, 1), F32),
        ],
        compiler_params=PARAMS,
        cost_estimate=cost(4 * heads * rows * rows * count * HEAD_DIM, 8 * rows * wide),
        name="linear_forward",
    )(lengths, query, *keys, *values)


def linear_backward(chunk, lengths, query, keys, values, grad, mixed, total, carry):
    rows, width = query.shape
    heads = width // FEATURE_SIZE
    tile = min(256, rows)
    count = chunk + 1
    wide = heads * HEAD_DIM
    carry = list(carry)
    outs = pl.pallas_call(
        functools.partial(linear_backward_kernel, chunk, rows, tile, bool(carry)),
        grid=(heads,),
        in_specs=[SMEM_SPEC, narrow_spec(rows, width)]
        + [narrow_spec(rows, width)] * count
        + [head_spec(rows)] * count
        + [head_spec(rows), head_spec(rows), total_spec(rows)]
        + ([narrow_spec(rows, width), head_spec(rows)] if carry else []),
        out_specs=[narrow_spec(rows, width), narrow_spec(rows, width), head_spec(rows)]
        + [narrow_spec(rows, width)] * chunk
        + [head_spec(rows)] * chunk,
        out_shape=[
            jax.ShapeDtypeStruct((rows, width), BF16),
            jax.ShapeDtypeStruct((rows, width), BF16),
            jax.ShapeDtypeStruct((rows, wide), BF16),
        ]
        + [jax.ShapeDtypeStruct((rows, width), F32)] * chunk
        + [jax.ShapeDtypeStruct((rows, wide), F32)] * chunk,
        scratch_shapes=[
            pltpu.VMEM((rows, width), F32),
            pltpu.VMEM((count * rows, width), F32),
            pltpu.VMEM((count * rows, HEAD_DIM), F32),
        ],
        compiler_params=PARAMS,
        cost_estimate=cost(10 * heads * rows * rows * count * HEAD_DIM, 16 * rows * wide),
        name="linear_backward",
    )(lengths, query, *keys, *values, grad, mixed, total, *carry)
    return outs[:3], list(zip(outs[3 : 3 + chunk], outs[3 + chunk :]))


def prev_spec(rows):
    return pl.BlockSpec((WINDOW, HEAD_DIM), lambda h: (rows // WINDOW - 1, h))


def edge_spec():
    return pl.BlockSpec((WINDOW, HEAD_DIM), lambda h: (0, h))


def window_forward(chunk, lengths, query, key, value, before):
    rows, wide = query.shape
    heads = wide // HEAD_DIM
    tile = min(128, rows)
    return pl.pallas_call(
        functools.partial(window_forward_kernel, chunk, rows, tile),
        grid=(heads,),
        in_specs=[SMEM_SPEC] + [head_spec(rows)] * 3 + [prev_spec(rows)] * len(before),
        out_specs=head_spec(rows),
        out_shape=jax.ShapeDtypeStruct((rows, wide), BF16),
        compiler_params=PARAMS,
        cost_estimate=cost(4 * rows * 4 * HEAD_DIM * wide, 8 * rows * wide),
        name="window_forward",
    )(lengths, query, key, value, *before)


def window_backward(chunk, lengths, query, key, value, before, grad, carry):
    rows, wide = query.shape
    heads = wide // HEAD_DIM
    tile = min(128, rows)
    carry = list(carry)
    edges = 2 if chunk else 0
    outs = pl.pallas_call(
        functools.partial(window_backward_kernel, chunk, rows, tile, bool(carry)),
        grid=(heads,),
        in_specs=[SMEM_SPEC]
        + [head_spec(rows)] * 3
        + [prev_spec(rows)] * len(before)
        + [head_spec(rows)]
        + [edge_spec()] * len(carry),
        out_specs=[head_spec(rows)] * 3 + [edge_spec()] * edges,
        out_shape=[jax.ShapeDtypeStruct((rows, wide), BF16)] * 3
        + [jax.ShapeDtypeStruct((WINDOW, wide), F32)] * edges,
        scratch_shapes=[pltpu.VMEM((WINDOW + rows, HEAD_DIM), F32)] * 2,
        compiler_params=PARAMS,
        cost_estimate=cost(10 * rows * 4 * HEAD_DIM * wide, 16 * rows * wide),
        name="window_backward",
    )(lengths, query, key, value, *before, grad, *carry)
    return outs[:3], outs[3:]


def gather_norm_kernel(count, width, place_ref, own_ref, *refs):
    right, left = refs[: count - 1], refs[count - 1 : 2 * count - 2]
    gain_ref, normed_ref, inverse_ref, held = refs[2 * count - 2 :]
    place = place_ref[0]
    squares = jnp.zeros((own_ref.shape[0], 1), F32)
    for k in range(count):
        if k == 0:
            piece = own_ref[...].astype(F32)
        else:
            piece = jnp.where(place >= k, right[k - 1][...], left[count - k - 1][...]).astype(F32)
        held[k] = piece
        squares += jnp.sum(piece * piece, axis=1, keepdims=True)
    inverse = lax.rsqrt(squares * (1.0 / (count * width)) + EPSILON)
    inverse_ref[...] = inverse
    for k in range(count):
        block = lax.rem(place - k + count, count)
        columns = pl.ds(pl.multiple_of(block * width, width), width)
        gain = gain_ref[:, columns].astype(F32)
        normed_ref[:, columns] = (held[k] * inverse * gain).astype(BF16)


def gather_norm(pieces, gain_vector):
    own, right, left = pieces
    rows, width = own.shape
    count = len(right) + 1
    tile = min(128, rows)
    place = lax.axis_index("mp").astype(jnp.int32).reshape(1)
    piece_spec = pl.BlockSpec((tile, width), lambda t: (t, 0))
    return pl.pallas_call(
        functools.partial(gather_norm_kernel, count, width),
        grid=(rows // tile,),
        in_specs=[SMEM_SPEC]
        + [piece_spec] * (2 * count - 1)
        + [pl.BlockSpec((1, count * width), lambda t: (0, 0))],
        out_specs=[
            pl.BlockSpec((tile, count * width), lambda t: (t, 0)),
            pl.BlockSpec((tile, 1), lambda t: (t, 0)),
        ],
        out_shape=[
            jax.ShapeDtypeStruct((rows, count * width), BF16),
            jax.ShapeDtypeStruct((rows, 1), F32),
        ],
        scratch_shapes=[pltpu.VMEM((count, tile, width), F32)],
        compiler_params=PARAMS,
        cost_estimate=cost(8 * rows * width * count, 6 * rows * width * count),
        name="gather_norm",
    )(place, own, *right, *left, gain_vector.reshape(1, -1))


def gather_join_kernel(count, width, place_ref, own_ref, *refs):
    right, left = refs[: count - 1], refs[count - 1 : 2 * count - 2]
    out_ref = refs[-1]
    place = place_ref[0]
    for k in range(count):
        if k == 0:
            piece = own_ref[...]
        else:
            piece = jnp.where(place >= k, right[k - 1][...], left[count - k - 1][...])
        block = lax.rem(place - k + count, count)
        out_ref[:, pl.ds(pl.multiple_of(block * width, width), width)] = piece


def gather_join(pieces):
    own, right, left = pieces
    rows, width = own.shape
    count = len(right) + 1
    tile = min(128, rows)
    place = lax.axis_index("mp").astype(jnp.int32).reshape(1)
    piece_spec = pl.BlockSpec((tile, width), lambda t: (t, 0))
    return pl.pallas_call(
        functools.partial(gather_join_kernel, count, width),
        grid=(rows // tile,),
        in_specs=[SMEM_SPEC] + [piece_spec] * (2 * count - 1),
        out_specs=pl.BlockSpec((tile, count * width), lambda t: (t, 0)),
        out_shape=jax.ShapeDtypeStruct((rows, count * width), BF16),
        compiler_params=PARAMS,
        cost_estimate=cost(rows * width * count, 6 * rows * width * count),
        name="gather_join",
    )(place, own, *right, *left)


def hidden_kernel(gate_ref, upper_ref, after_ref, hidden_ref):
    gate = gate_ref[...]
    hidden_ref[...] = (gate * jax.nn.sigmoid(gate) * upper_ref[...]).astype(BF16)


def hidden_backward_kernel(gate_ref, upper_ref, grad_ref, dg_ref, du_ref, row_ref):
    gate, upper, grad = gate_ref[...], upper_ref[...], grad_ref[...]
    sigma = jax.nn.sigmoid(gate)
    gate_grad = (grad * upper * sigma * (1.0 + gate * (1.0 - sigma))).astype(BF16)
    upper_grad = (grad * gate * sigma).astype(BF16)
    dg_ref[...] = gate_grad
    du_ref[...] = upper_grad
    row_ref[...] = jnp.sum(
        gate_grad.astype(F32) * gate + upper_grad.astype(F32) * upper, axis=1, keepdims=True
    )


def row_tiles(rows, most):
    return max(t for t in range(16, most + 1, 16) if rows % t == 0)


def hidden_forward(gate, upper, after):
    rows, width = gate.shape
    tile = row_tiles(rows, 128)
    spec = pl.BlockSpec((tile, width), lambda t: (t, 0))
    return pl.pallas_call(
        hidden_kernel,
        grid=(rows // tile,),
        in_specs=[spec, spec, pl.BlockSpec(memory_space=pl.ANY)],
        out_specs=spec,
        out_shape=jax.ShapeDtypeStruct((rows, width), BF16),
        compiler_params=PARAMS,
        cost_estimate=cost(8 * rows * width, 10 * rows * width),
        name="hidden_forward",
    )(gate, upper, after)


def hidden_backward(gate, upper, grad):
    rows, width = gate.shape
    tile = row_tiles(rows, 128)
    spec = pl.BlockSpec((tile, width), lambda t: (t, 0))
    return pl.pallas_call(
        hidden_backward_kernel,
        grid=(rows // tile,),
        in_specs=[spec] * 3,
        out_specs=[spec, spec, pl.BlockSpec((tile, 1), lambda t: (t, 0))],
        out_shape=[jax.ShapeDtypeStruct((rows, width), BF16)] * 2
        + [jax.ShapeDtypeStruct((rows, 1), F32)],
        compiler_params=PARAMS,
        cost_estimate=cost(20 * rows * width, 16 * rows * width),
        name="hidden_backward",
    )(gate, upper, grad)


def pack_kernel(count, tile, grad_ref, normed_ref, extra_ref, out_ref, sum_ref):
    step = pl.program_id(0)
    rows = out_ref.shape[1] - PAD_ROWS
    width = out_ref.shape[2]
    grad = grad_ref[...]

    @pl.when(step == 0)
    def _():
        sum_ref[...] = jnp.zeros_like(sum_ref)

    sum_ref[...] += jnp.sum(grad * normed_ref[...].astype(F32), axis=0, keepdims=True)
    own = pl.ds(pl.multiple_of(step * tile, tile), tile)
    for j in range(count):
        out_ref[j, own, :] = grad[:, j * width : (j + 1) * width].astype(BF16)

    @pl.when(step == pl.num_programs(0) - 1)
    def _():
        line = lax.broadcasted_iota(jnp.int32, extra_ref.shape, 0)
        last = jnp.where(line == PAD_ROWS - 1, sum_ref[...], extra_ref[...]).astype(BF16)
        for j in range(count):
            out_ref[j, pl.ds(rows, PAD_ROWS), :] = last[:, j * width : (j + 1) * width]


def pack_rows(grad, normed, extra, count):
    rows, width = grad.shape
    tile = row_tiles(rows, 128)
    shape = (count, rows + PAD_ROWS, width // count)
    return pl.pallas_call(
        functools.partial(pack_kernel, count, tile),
        grid=(rows // tile,),
        in_specs=[
            pl.BlockSpec((tile, width), lambda t: (t, 0)),
            pl.BlockSpec((tile, width), lambda t: (t, 0)),
            pl.BlockSpec((PAD_ROWS, width), lambda t: (0, 0)),
        ],
        out_specs=pl.BlockSpec(shape, lambda t: (0, 0, 0)),
        out_shape=jax.ShapeDtypeStruct(shape, BF16),
        scratch_shapes=[pltpu.VMEM((1, width), F32)],
        compiler_params=PARAMS,
        cost_estimate=cost(4 * rows * width, 8 * rows * width),
        name="pack_rows",
    )(grad, normed, extra)


def block_product_kernel(left_ref, right_ref, out_ref):
    out_ref[0] = nn(left_ref[...], right_ref[...]).astype(BF16)


def block_product(left, right, count):
    rows, depth = left.shape
    width = right.shape[1] // count
    return pl.pallas_call(
        block_product_kernel,
        grid=(count,),
        in_specs=[
            pl.BlockSpec((rows, depth), lambda j: (0, 0)),
            pl.BlockSpec((depth, width), lambda j: (0, j)),
        ],
        out_specs=pl.BlockSpec((1, rows, width), lambda j: (j, 0, 0)),
        out_shape=jax.ShapeDtypeStruct((count, rows, width), BF16),
        compiler_params=PARAMS,
        cost_estimate=cost(2 * rows * depth * width * count, 2 * depth * width * count),
        name="block_product",
    )(left, right)


def line_gather(part):
    count = lax.axis_size("mp")
    right, left = [part], [part]
    for k in range(1, count):
        right.append(
            lax.ppermute(right[-1], "mp", [(j, j + 1) for j in range(k - 1, count - 1)])
        )
        left.append(lax.ppermute(left[-1], "mp", [(j, j - 1) for j in range(1, count - k + 1)]))
    return part, right[1:], left[1:]


def tie(value, *others):
    if not others:
        return value
    zero = sum(other[(0,) * other.ndim].astype(F32) * 0.0 for other in others)
    return value + zero.astype(value.dtype)


def block_at(blocks, index):
    count = blocks.shape[0]
    return lax.dynamic_index_in_dim(blocks, lax.rem(index + count, count), 0, keepdims=False)


def scatter_sum(blocks):
    count = lax.axis_size("mp")
    place = lax.axis_index("mp")
    right = left = None
    for k in range(1, count):
        to_right, to_left = block_at(blocks, place - k), block_at(blocks, place + k)
        if right is not None:
            to_right, to_left = to_right + right, to_left + left
        right = lax.ppermute(to_right, "mp", [(j, j + 1) for j in range(k)])
        left = lax.ppermute(to_left, "mp", [(j, j - 1) for j in range(count - k, count)])
    return block_at(blocks, place).astype(F32) + right.astype(F32) + left.astype(F32)


def scatter_sum_rows(partial_value, normed, row_values, *lines):
    rows, model_width = partial_value.shape
    count = lax.axis_size("mp")
    width = model_width // count
    places = rows // width
    extra = jnp.tile(row_values.reshape(places, width), (1, count))
    extra = jnp.concatenate([extra] + [line[None] for line in lines], axis=0)
    extra = jnp.pad(extra, ((0, PAD_ROWS - extra.shape[0]), (0, 0)))
    total = scatter_sum(pack_rows(partial_value, normed, extra, count))
    sums = [total[-1]] + [total[rows + places + j] for j in range(len(lines))]
    return total[:rows], total[rows : rows + places].reshape(rows), sums


def sum_groups(values, turn):
    count = lax.axis_size("dp")
    listed = [(j + turn) % count for j in range(count)]
    return [v.astype(F32) for v in lax.psum(tuple(values), "dp", axis_index_groups=[listed])]


def norm_backward(
    normed_grad, normed, row_values, lines, resid, inverse, gain_part, model_width, carried
):
    shard_grad, row_dot, sums = scatter_sum_rows(normed_grad, normed, row_values, *lines)
    normed_part = resid * inverse
    input_grad = carried + inverse * (
        shard_grad * gain_part - normed_part * (row_dot / model_width)[:, None]
    )
    return input_grad, sums


def row_product(*pairs):
    total = 0.0
    for left, right in pairs:
        total = total + jnp.sum(left.astype(F32) * right.astype(F32), axis=1)
    return total


def per_device(
    tokens,
    seq_lengths,
    gain_first,
    lin_query,
    lin_key,
    lin_value,
    lin_out,
    gain_second,
    win_query,
    win_key,
    win_value,
    win_out,
    gain_third,
    gate_weight,
    up_weight,
    down_weight,
    out_cotangent,
):
    row_count, width = tokens.shape
    count = lax.axis_size("mp")
    model_width = width * count
    rows = row_count // CHUNKS
    order = list(range(CHUNKS))
    offset = lax.axis_index("mp") * width
    places = jnp.arange(row_count, dtype=jnp.int32)
    validity = (places < seq_lengths[0, 0] + seq_lengths[0, 1]).astype(F32)
    valid = [validity[c * rows : (c + 1) * rows, None] for c in order]

    def cut(values):
        return [values[c * rows : (c + 1) * rows] for c in order]

    def join(values):
        return jnp.concatenate(values, axis=0) if len(values) > 1 else values[0]

    def part_of(gain):
        return lax.dynamic_slice_in_dim(gain, offset, width).astype(F32)

    blank = [None] * CHUNKS
    token_parts = cut(tokens)
    resid_zero = [t.astype(F32) for t in token_parts]
    cot_shard = [c.astype(F32) * v for c, v in zip(cut(out_cotangent), valid)]

    n1, r1, lq, lk, lv, lo, lo32, lden, b1, resid_one = [list(blank) for _ in range(10)]
    for c in order:
        n1[c], r1[c] = gather_norm(line_gather(token_parts[c]), gain_first)
        lq[c] = nn(n1[c], lin_query).astype(BF16)
        lk[c] = nn(n1[c], lin_key).astype(BF16)
        lv[c] = nn(n1[c], lin_value).astype(BF16)
        lo[c], lo32[c], lden[c] = linear_forward(
            c, seq_lengths, lq[c], lk[: c + 1], lv[: c + 1]
        )
        b1[c] = scatter_sum(block_product(lo[c], lin_out, count))
        resid_one[c] = resid_zero[c] + b1[c]
    cot_joined = lax.all_gather(
        join([c.astype(BF16) for c in cot_shard]), "mp", axis=1, tiled=True
    )
    cot_full = cut(cot_joined)
    n2, r2, wq, wk, wv, wo, b2, resid_two = [list(blank) for _ in range(8)]
    for c in order:
        n2[c], r2[c] = gather_norm(line_gather(resid_one[c].astype(BF16)), gain_second)
        wq[c] = nn(n2[c], win_query).astype(BF16)
        wk[c] = nn(n2[c], win_key).astype(BF16)
        wv[c] = nn(n2[c], win_value).astype(BF16)
        before = [wk[c - 1], wv[c - 1]] if c else []
        wo[c] = window_forward(c, seq_lengths, wq[c], wk[c], wv[c], before)
        b2[c] = scatter_sum(block_product(wo[c], win_out, count))
        resid_two[c] = resid_one[c] + b2[c]
    n3, r3, hid, dg, du, b3, resid_three, dn3, resid_two_grad = [list(blank) for _ in range(9)]
    gates, uppers = list(blank), list(blank)
    for c in order:
        n3[c], r3[c] = gather_norm(line_gather(resid_two[c].astype(BF16)), gain_third)
        gates[c] = nn(n3[c], gate_weight)
        uppers[c] = nn(n3[c], up_weight)
    def masked_squares(values):
        return sum(jnp.sum(v * jnp.sum(p * p, axis=1, keepdims=True)) for v, p in zip(valid, values))

    def stat_line(*values):
        block = jnp.pad(jnp.stack(values), (0, width - len(values)))
        return jnp.tile(block, count)

    stats = stat_line(masked_squares(resid_zero), masked_squares(b1), masked_squares(b2))
    sums_three, sums_two, sums_one = list(blank), list(blank), list(blank)
    for c in order:
        hid[c] = hidden_forward(gates[c], uppers[c], cot_joined)
    for c in reversed(order):
        hid_grad = nt(cot_full[c], down_weight)
        dg[c], du[c], row_values = hidden_backward(gates[c], uppers[c], hid_grad)
        dn3[c] = nt(dg[c], gate_weight) + nt(du[c], up_weight)
        resid_two_grad[c], sums_three[c] = norm_backward(
            dn3[c],
            n3[c],
            row_values[:, 0],
            (stats,),
            resid_two[c],
            r3[c],
            part_of(gain_third),
            model_width,
            cot_shard[c],
        )
    for c in order:
        b3[c] = scatter_sum(block_product(hid[c], down_weight, count))
        resid_three[c] = resid_two[c] + b3[c]
    ffn_normed, ffn_hid = join(n3), join(hid)
    ffn_grads = [
        tn(ffn_normed, join(dg)).astype(BF16),
        tn(ffn_normed, join(du)).astype(BF16),
        tn(ffn_hid, join(cot_full)).astype(BF16),
    ]
    ffn_sums = sum_groups(ffn_grads, 0)
    cot_two, wdq, wdk, wdv, dn2, resid_one_grad = [list(blank) for _ in range(6)]
    carry = []
    for c in reversed(order):
        shard = resid_two_grad[c] if c else tie(resid_two_grad[c], *ffn_grads)
        cot_two[c] = gather_join(line_gather(shard.astype(BF16)))
        mixed_grad = nt(cot_two[c], win_out).astype(BF16)
        before = [wk[c - 1], wv[c - 1]] if c else []
        (wdq[c], wdk[c], wdv[c]), carry = window_backward(
            c, seq_lengths, wq[c], wk[c], wv[c], before, mixed_grad, carry
        )
        dn2[c] = nt(wdq[c], win_query) + nt(wdk[c], win_key) + nt(wdv[c], win_value)
        resid_one_grad[c], sums_two[c] = norm_backward(
            dn2[c],
            n2[c],
            row_product((wdq[c], wq[c]), (wdk[c], wk[c]), (wdv[c], wv[c])),
            (),
            resid_one[c],
            r2[c],
            part_of(gain_second),
            model_width,
            resid_two_grad[c],
        )
    win_normed = join(n2)
    win_grads = [
        tn(win_normed, join(wdq)).astype(BF16),
        tn(win_normed, join(wdk)).astype(BF16),
        tn(win_normed, join(wdv)).astype(BF16),
        tn(join(wo), join(cot_two)).astype(BF16),
    ]
    win_sums = sum_groups(win_grads[:3] + [tie(win_grads[3], *ffn_sums)], 1)
    cot_one, ldq, ldk, ldv, dn1, tokens_grad = [list(blank) for _ in range(6)]
    pending = [[] for _ in order]
    for c in reversed(order):
        shard = resid_one_grad[c] if c else tie(resid_one_grad[c], *win_grads[:3])
        cot_one[c] = gather_join(line_gather(shard.astype(BF16)))
        mixed_grad = nt(cot_one[c], lin_out)
        carry = []
        if pending[c]:
            carry = [functools.reduce(jnp.add, [p[s] for p in pending[c]]) for s in (0, 1)]
        (ldq[c], ldk[c], ldv[c]), back = linear_backward(
            c,
            seq_lengths,
            lq[c],
            lk[: c + 1],
            lv[: c + 1],
            mixed_grad,
            lo32[c],
            lden[c],
            carry,
        )
        for earlier, pair in enumerate(back):
            pending[earlier].append(pair)
        dn1[c] = nt(ldq[c], lin_query) + nt(ldk[c], lin_key) + nt(ldv[c], lin_value)
        stats = stat_line(masked_squares(b3), masked_squares(resid_three))
        tokens_grad[c], sums_one[c] = norm_backward(
            dn1[c],
            n1[c],
            row_product((ldq[c], lq[c]), (ldk[c], lk[c]), (ldv[c], lv[c])),
            () if c else (stats,),
            resid_zero[c],
            r1[c],
            part_of(gain_first),
            model_width,
            resid_one_grad[c],
        )
    lin_normed = join(n1)
    lin_grads = [
        tn(lin_normed, join(ldq)).astype(BF16),
        tn(lin_normed, join(ldk)).astype(BF16),
        tn(lin_normed, join(ldv)).astype(BF16),
        tn(join(lo), join(cot_one)).astype(BF16),
    ]
    lin_sums = sum_groups(lin_grads[:3] + [tie(lin_grads[3], *win_sums)], 2)
    small = lax.psum(
        jnp.concatenate(
            [sum(part[0] for part in sums) for sums in (sums_one, sums_two, sums_three)]
            + [sums_three[0][1][:3], sums_one[0][1][:2], jnp.sum(validity)[None]]
        ),
        "dp",
    )
    gain_grads = [
        small[s * width : (s + 1) * width] / part_of(gain)
        for s, gain in enumerate((gain_first, gain_second, gain_third))
    ]
    rms_values = jnp.sqrt(small[3 * width : -1] / (small[-1] * model_width))
    return (
        join([v.astype(BF16) for v in resid_three]),
        join(tokens_grad),
        gain_grads[0],
        lin_sums[0],
        lin_sums[1],
        lin_sums[2],
        lin_sums[3],
        gain_grads[1],
        win_sums[0],
        win_sums[1],
        win_sums[2],
        win_sums[3],
        gain_grads[2],
        ffn_sums[0],
        ffn_sums[1],
        ffn_sums[2],
        rms_values,
    )


def solution(mesh):
    in_specs = (
        P("dp", "mp"),
        P("dp", None),
        P(),
        P(None, "mp"),
        P(None, "mp"),
        P(None, "mp"),
        P("mp", None),
        P(),
        P(None, "mp"),
        P(None, "mp"),
        P(None, "mp"),
        P("mp", None),
        P(),
        P(None, "mp"),
        P(None, "mp"),
        P("mp", None),
        P("dp", "mp"),
    )
    out_specs = (
        P("dp", "mp"),
        P("dp", "mp"),
        P("mp"),
        P(None, "mp"),
        P(None, "mp"),
        P(None, "mp"),
        P("mp", None),
        P("mp"),
        P(None, "mp"),
        P(None, "mp"),
        P(None, "mp"),
        P("mp", None),
        P("mp"),
        P(None, "mp"),
        P(None, "mp"),
        P("mp", None),
        P(),
    )
    return jax.shard_map(
        per_device, mesh=mesh, in_specs=in_specs, out_specs=out_specs, check_vma=False
    )
```

```python
import functools

import jax
import jax.numpy as jnp
from jax import lax
from jax.experimental import pallas as pl
from jax.experimental.pallas import tpu as pltpu
from jax.sharding import PartitionSpec as P

FEATURE_SIZE = 16
HEAD_DIM = 128
WINDOW = 64
EPSILON = 1e-05
NEGATIVE = -1e30
CHUNKS = 2
LIN_SCALE = FEATURE_SIZE ** (-0.5)
WIN_SCALE = HEAD_DIM ** (-0.5)
F32 = jnp.float32
BF16 = jnp.bfloat16
PAD_ROWS = 16
VMEM_LIMIT = 40 * 1024 * 1024


def nn(left, right):
    return lax.dot_general(left, right, (((1,), (0,)), ((), ())), preferred_element_type=F32)


def nt(left, right):
    return lax.dot_general(left, right, (((1,), (1,)), ((), ())), preferred_element_type=F32)


def tn(left, right):
    return lax.dot_general(left, right, (((0,), (0,)), ((), ())), preferred_element_type=F32)


def segment_start(lens_ref, place):
    first_end = lens_ref[0, 0]
    second_end = first_end + lens_ref[0, 1]
    return jnp.where(place < first_end, 0, jnp.where(place < second_end, first_end, second_end))


def causal_allowed(lens_ref, row_begin, key_begin, rows, keys, window):
    place = row_begin + lax.broadcasted_iota(jnp.int32, (rows, 1), 0)
    key_place = key_begin + lax.broadcasted_iota(jnp.int32, (rows, keys), 1)
    lowest = segment_start(lens_ref, place)
    if window:
        lowest = jnp.maximum(lowest, place - (window - 1))
    allowed = key_place >= lowest
    if key_begin + keys > row_begin:
        allowed = allowed & (key_place <= place)
    return allowed


def head_lanes(values, head):
    lane = lax.broadcasted_iota(jnp.int32, values.shape, 1) // FEATURE_SIZE
    return jnp.where(lane == head, values, jnp.zeros_like(values))


def linear_tile(lens_ref, query, key, row_begin, key_begin):
    logits = nt(query, key) * LIN_SCALE
    allowed = causal_allowed(lens_ref, row_begin, key_begin, query.shape[0], key.shape[0], 0)
    kernel = jnp.where(allowed, 1.0 + logits + 0.5 * logits * logits, 0.0)
    return logits, allowed, kernel


def linear_forward_kernel(chunk, rows, tile, lens_ref, q_ref, *refs):
    count = chunk + 1
    k_refs, v_refs = refs[:count], refs[count : 2 * count]
    low_ref, mixed_ref, total_ref = refs[2 * count :]
    head = pl.program_id(0)
    per = rows // tile
    for i in range(per):
        row_begin = chunk * rows + i * tile
        query = q_ref[pl.ds(i * tile, tile), :]
        total = jnp.zeros((tile, 1), F32)
        number = jnp.zeros((tile, HEAD_DIM), F32)
        for j in range(chunk * per + i + 1):
            span = pl.ds((j % per) * tile, tile)
            key = head_lanes(k_refs[j // per][span, :], head)
            _, _, kernel = linear_tile(lens_ref, query, key, row_begin, j * tile)
            total += jnp.sum(kernel, axis=1, keepdims=True)
            number += nn(kernel.astype(BF16), v_refs[j // per][span, :])
        mixed = number / total
        low_ref[pl.ds(i * tile, tile), :] = mixed.astype(BF16)
        mixed_ref[pl.ds(i * tile, tile), :] = mixed
        total_ref[0, pl.ds(i * tile, tile), :] = total


def linear_backward_kernel(chunk, rows, tile, carried, lens_ref, q_ref, *refs):
    count = chunk + 1
    k_refs, v_refs = refs[:count], refs[count : 2 * count]
    do_ref, mixed_ref, total_ref = refs[2 * count : 2 * count + 3]
    refs = refs[2 * count + 3 :]
    if carried:
        dk_in, dv_in = refs[:2]
        refs = refs[2:]
    dq_out, dk_out, dv_out = refs[:3]
    dk_prev, dv_prev = refs[3 : 3 + chunk], refs[3 + chunk : 3 + 2 * chunk]
    dq_acc, dk_acc, dv_acc = refs[3 + 2 * chunk :]
    head = pl.program_id(0)
    last = pl.num_programs(0) - 1
    per = rows // tile

    @pl.when(head == 0)
    def _():
        dq_acc[...] = jnp.zeros_like(dq_acc)
        dk_acc[...] = jnp.zeros_like(dk_acc)
        if carried:
            dk_acc[pl.ds(chunk * rows, rows), :] = dk_in[...]

    dv_acc[...] = jnp.zeros_like(dv_acc)
    if carried:
        dv_acc[pl.ds(chunk * rows, rows), :] = dv_in[...]
    for i in range(per):
        row_begin = chunk * rows + i * tile
        own = pl.ds(i * tile, tile)
        query = head_lanes(q_ref[own, :], head)
        grad = do_ref[own, :]
        inverse = 1.0 / total_ref[0, own, :]
        number_grad = (grad * inverse).astype(BF16)
        total_grad = -jnp.sum(grad * mixed_ref[own, :], axis=1, keepdims=True) * inverse
        dq = jnp.zeros((tile, q_ref.shape[1]), F32)
        for j in range(chunk * per + i + 1):
            span = pl.ds((j % per) * tile, tile)
            key = head_lanes(k_refs[j // per][span, :], head)
            logits, allowed, kernel = linear_tile(lens_ref, query, key, row_begin, j * tile)
            kernel_grad = nt(number_grad, v_refs[j // per][span, :]) + total_grad
            scores_grad = jnp.where(allowed, kernel_grad * (1.0 + logits), 0.0).astype(BF16)
            dq += nn(scores_grad, key)
            keys = pl.ds(j * tile, tile)
            dk_acc[keys, :] += tn(scores_grad, query) * LIN_SCALE
            dv_acc[keys, :] += tn(kernel.astype(BF16), number_grad)
        dq_acc[own, :] += dq * LIN_SCALE
    dv_out[...] = dv_acc[pl.ds(chunk * rows, rows), :].astype(BF16)
    for c in range(chunk):
        dv_prev[c][...] = dv_acc[pl.ds(c * rows, rows), :]

    @pl.when(head == last)
    def _():
        dq_out[...] = dq_acc[...].astype(BF16)
        dk_out[...] = dk_acc[pl.ds(chunk * rows, rows), :].astype(BF16)
        for c in range(chunk):
            dk_prev[c][...] = dk_acc[pl.ds(c * rows, rows), :]


def window_tile(lens_ref, query, key, row_begin, key_begin):
    logits = nt(query, key) * WIN_SCALE
    allowed = causal_allowed(lens_ref, row_begin, key_begin, query.shape[0], key.shape[0], WINDOW)
    logits = jnp.where(allowed, logits, NEGATIVE)
    exponent = jnp.exp(logits - jnp.max(logits, axis=1, keepdims=True))
    return exponent / jnp.sum(exponent, axis=1, keepdims=True)


def window_keys(current_ref, prev_ref, i, tile):
    if i > 0:
        return current_ref[pl.ds(i * tile - WINDOW, tile + WINDOW), :], i * tile - WINDOW
    if prev_ref is not None:
        return jnp.concatenate([prev_ref[...], current_ref[pl.ds(0, tile), :]], axis=0), -WINDOW
    return current_ref[pl.ds(0, tile), :], 0


def window_forward_kernel(chunk, rows, tile, lens_ref, q_ref, k_ref, v_ref, *refs):
    k_prev, v_prev = refs[:2] if chunk else (None, None)
    out_ref = refs[-1]
    for i in range(rows // tile):
        own = pl.ds(i * tile, tile)
        key, key_begin = window_keys(k_ref, k_prev, i, tile)
        value, _ = window_keys(v_ref, v_prev, i, tile)
        base = chunk * rows
        weights = window_tile(lens_ref, q_ref[own, :], key, base + i * tile, base + key_begin)
        out_ref[own, :] = nn(weights.astype(BF16), value).astype(BF16)


def window_backward_kernel(chunk, rows, tile, carried, lens_ref, q_ref, k_ref, v_ref, *refs):
    k_prev, v_prev = refs[:2] if chunk else (None, None)
    refs = refs[2:] if chunk else refs
    do_ref, refs = refs[0], refs[1:]
    if carried:
        dk_in, dv_in = refs[:2]
        refs = refs[2:]
    dq_out, dk_out, dv_out = refs[:3]
    dk_back, dv_back = refs[3:5] if chunk else (None, None)
    dk_acc, dv_acc = refs[-2:]
    dk_acc[...] = jnp.zeros_like(dk_acc)
    dv_acc[...] = jnp.zeros_like(dv_acc)
    if carried:
        dk_acc[pl.ds(rows, WINDOW), :] = dk_in[...]
        dv_acc[pl.ds(rows, WINDOW), :] = dv_in[...]
    for i in range(rows // tile):
        own = pl.ds(i * tile, tile)
        key, key_begin = window_keys(k_ref, k_prev, i, tile)
        value, _ = window_keys(v_ref, v_prev, i, tile)
        base = chunk * rows
        query = q_ref[own, :]
        grad = do_ref[own, :]
        weights = window_tile(lens_ref, query, key, base + i * tile, base + key_begin)
        weight_grad = nt(grad, value)
        delta = jnp.sum(weights * weight_grad, axis=1, keepdims=True)
        scores_grad = (weights * (weight_grad - delta)).astype(BF16)
        dq_out[own, :] = (nn(scores_grad, key) * WIN_SCALE).astype(BF16)
        keys = pl.ds(WINDOW + key_begin, key.shape[0])
        dk_acc[keys, :] += tn(scores_grad, query) * WIN_SCALE
        dv_acc[keys, :] += tn(weights.astype(BF16), grad)
    dk_out[...] = dk_acc[pl.ds(WINDOW, rows), :].astype(BF16)
    dv_out[...] = dv_acc[pl.ds(WINDOW, rows), :].astype(BF16)
    if chunk:
        dk_back[...] = dk_acc[pl.ds(0, WINDOW), :]
        dv_back[...] = dv_acc[pl.ds(0, WINDOW), :]


SMEM_SPEC = pl.BlockSpec(memory_space=pltpu.SMEM)
PARAMS = pltpu.CompilerParams(
    dimension_semantics=("arbitrary",), vmem_limit_bytes=VMEM_LIMIT
)


def cost(flops, moved):
    return pl.CostEstimate(flops=flops, bytes_accessed=moved, transcendentals=0)


def narrow_spec(rows, width):
    return pl.BlockSpec((rows, width), lambda h: (0, 0))


def head_spec(rows):
    return pl.BlockSpec((rows, HEAD_DIM), lambda h: (0, h))


def total_spec(rows):
    return pl.BlockSpec((1, rows, 1), lambda h: (h, 0, 0))


def linear_forward(chunk, lengths, query, keys, values):
    rows, width = query.shape
    heads = width // FEATURE_SIZE
    tile = min(256, rows)
    count = chunk + 1
    wide = heads * HEAD_DIM
    return pl.pallas_call(
        functools.partial(linear_forward_kernel, chunk, rows, tile),
        grid=(heads,),
        in_specs=[SMEM_SPEC, narrow_spec(rows, width)]
        + [narrow_spec(rows, width)] * count
        + [head_spec(rows)] * count,
        out_specs=[head_spec(rows), head_spec(rows), total_spec(rows)],
        out_shape=[
            jax.ShapeDtypeStruct((rows, wide), BF16),
            jax.ShapeDtypeStruct((rows, wide), F32),
            jax.ShapeDtypeStruct((heads, rows, 1), F32),
        ],
        compiler_params=PARAMS,
        cost_estimate=cost(4 * heads * rows * rows * count * HEAD_DIM, 8 * rows * wide),
        name="linear_forward",
    )(lengths, query, *keys, *values)


def linear_backward(chunk, lengths, query, keys, values, grad, mixed, total, carry):
    rows, width = query.shape
    heads = width // FEATURE_SIZE
    tile = min(256, rows)
    count = chunk + 1
    wide = heads * HEAD_DIM
    carry = list(carry)
    outs = pl.pallas_call(
        functools.partial(linear_backward_kernel, chunk, rows, tile, bool(carry)),
        grid=(heads,),
        in_specs=[SMEM_SPEC, narrow_spec(rows, width)]
        + [narrow_spec(rows, width)] * count
        + [head_spec(rows)] * count
        + [head_spec(rows), head_spec(rows), total_spec(rows)]
        + ([narrow_spec(rows, width), head_spec(rows)] if carry else []),
        out_specs=[narrow_spec(rows, width), narrow_spec(rows, width), head_spec(rows)]
        + [narrow_spec(rows, width)] * chunk
        + [head_spec(rows)] * chunk,
        out_shape=[
            jax.ShapeDtypeStruct((rows, width), BF16),
            jax.ShapeDtypeStruct((rows, width), BF16),
            jax.ShapeDtypeStruct((rows, wide), BF16),
        ]
        + [jax.ShapeDtypeStruct((rows, width), F32)] * chunk
        + [jax.ShapeDtypeStruct((rows, wide), F32)] * chunk,
        scratch_shapes=[
            pltpu.VMEM((rows, width), F32),
            pltpu.VMEM((count * rows, width), F32),
            pltpu.VMEM((count * rows, HEAD_DIM), F32),
        ],
        compiler_params=PARAMS,
        cost_estimate=cost(10 * heads * rows * rows * count * HEAD_DIM, 16 * rows * wide),
        name="linear_backward",
    )(lengths, query, *keys, *values, grad, mixed, total, *carry)
    return outs[:3], list(zip(outs[3 : 3 + chunk], outs[3 + chunk :]))


def prev_spec(rows):
    return pl.BlockSpec((WINDOW, HEAD_DIM), lambda h: (rows // WINDOW - 1, h))


def edge_spec():
    return pl.BlockSpec((WINDOW, HEAD_DIM), lambda h: (0, h))


def window_forward(chunk, lengths, query, key, value, before):
    rows, wide = query.shape
    heads = wide // HEAD_DIM
    tile = min(128, rows)
    return pl.pallas_call(
        functools.partial(window_forward_kernel, chunk, rows, tile),
        grid=(heads,),
        in_specs=[SMEM_SPEC] + [head_spec(rows)] * 3 + [prev_spec(rows)] * len(before),
        out_specs=head_spec(rows),
        out_shape=jax.ShapeDtypeStruct((rows, wide), BF16),
        compiler_params=PARAMS,
        cost_estimate=cost(4 * rows * 4 * HEAD_DIM * wide, 8 * rows * wide),
        name="window_forward",
    )(lengths, query, key, value, *before)


def window_backward(chunk, lengths, query, key, value, before, grad, carry):
    rows, wide = query.shape
    heads = wide // HEAD_DIM
    tile = min(128, rows)
    carry = list(carry)
    edges = 2 if chunk else 0
    outs = pl.pallas_call(
        functools.partial(window_backward_kernel, chunk, rows, tile, bool(carry)),
        grid=(heads,),
        in_specs=[SMEM_SPEC]
        + [head_spec(rows)] * 3
        + [prev_spec(rows)] * len(before)
        + [head_spec(rows)]
        + [edge_spec()] * len(carry),
        out_specs=[head_spec(rows)] * 3 + [edge_spec()] * edges,
        out_shape=[jax.ShapeDtypeStruct((rows, wide), BF16)] * 3
        + [jax.ShapeDtypeStruct((WINDOW, wide), F32)] * edges,
        scratch_shapes=[pltpu.VMEM((WINDOW + rows, HEAD_DIM), F32)] * 2,
        compiler_params=PARAMS,
        cost_estimate=cost(10 * rows * 4 * HEAD_DIM * wide, 16 * rows * wide),
        name="window_backward",
    )(lengths, query, key, value, *before, grad, *carry)
    return outs[:3], outs[3:]


def gather_norm_kernel(count, width, place_ref, own_ref, *refs):
    right, left = refs[: count - 1], refs[count - 1 : 2 * count - 2]
    gain_ref, normed_ref, inverse_ref, held = refs[2 * count - 2 :]
    place = place_ref[0]
    squares = jnp.zeros((own_ref.shape[0], 1), F32)
    for k in range(count):
        if k == 0:
            piece = own_ref[...].astype(F32)
        else:
            piece = jnp.where(place >= k, right[k - 1][...], left[count - k - 1][...]).astype(F32)
        held[k] = piece
        squares += jnp.sum(piece * piece, axis=1, keepdims=True)
    inverse = lax.rsqrt(squares * (1.0 / (count * width)) + EPSILON)
    inverse_ref[...] = inverse
    for k in range(count):
        block = lax.rem(place - k + count, count)
        columns = pl.ds(pl.multiple_of(block * width, width), width)
        gain = gain_ref[:, columns].astype(F32)
        normed_ref[:, columns] = (held[k] * inverse * gain).astype(BF16)


def gather_norm(pieces, gain_vector):
    own, right, left = pieces
    rows, width = own.shape
    count = len(right) + 1
    tile = min(128, rows)
    place = lax.axis_index("mp").astype(jnp.int32).reshape(1)
    piece_spec = pl.BlockSpec((tile, width), lambda t: (t, 0))
    return pl.pallas_call(
        functools.partial(gather_norm_kernel, count, width),
        grid=(rows // tile,),
        in_specs=[SMEM_SPEC]
        + [piece_spec] * (2 * count - 1)
        + [pl.BlockSpec((1, count * width), lambda t: (0, 0))],
        out_specs=[
            pl.BlockSpec((tile, count * width), lambda t: (t, 0)),
            pl.BlockSpec((tile, 1), lambda t: (t, 0)),
        ],
        out_shape=[
            jax.ShapeDtypeStruct((rows, count * width), BF16),
            jax.ShapeDtypeStruct((rows, 1), F32),
        ],
        scratch_shapes=[pltpu.VMEM((count, tile, width), F32)],
        compiler_params=PARAMS,
        cost_estimate=cost(8 * rows * width * count, 6 * rows * width * count),
        name="gather_norm",
    )(place, own, *right, *left, gain_vector.reshape(1, -1))


def gather_join_kernel(count, width, place_ref, own_ref, *refs):
    right, left = refs[: count - 1], refs[count - 1 : 2 * count - 2]
    out_ref = refs[-1]
    place = place_ref[0]
    for k in range(count):
        if k == 0:
            piece = own_ref[...]
        else:
            piece = jnp.where(place >= k, right[k - 1][...], left[count - k - 1][...])
        block = lax.rem(place - k + count, count)
        out_ref[:, pl.ds(pl.multiple_of(block * width, width), width)] = piece


def gather_join(pieces):
    own, right, left = pieces
    rows, width = own.shape
    count = len(right) + 1
    tile = min(128, rows)
    place = lax.axis_index("mp").astype(jnp.int32).reshape(1)
    piece_spec = pl.BlockSpec((tile, width), lambda t: (t, 0))
    return pl.pallas_call(
        functools.partial(gather_join_kernel, count, width),
        grid=(rows // tile,),
        in_specs=[SMEM_SPEC] + [piece_spec] * (2 * count - 1),
        out_specs=pl.BlockSpec((tile, count * width), lambda t: (t, 0)),
        out_shape=jax.ShapeDtypeStruct((rows, count * width), BF16),
        compiler_params=PARAMS,
        cost_estimate=cost(rows * width * count, 6 * rows * width * count),
        name="gather_join",
    )(place, own, *right, *left)


def hidden_kernel(gate_ref, upper_ref, after_ref, hidden_ref):
    gate = gate_ref[...]
    hidden_ref[...] = (gate * jax.nn.sigmoid(gate) * upper_ref[...]).astype(BF16)


def hidden_backward_kernel(gate_ref, upper_ref, grad_ref, dg_ref, du_ref, row_ref):
    gate, upper, grad = gate_ref[...], upper_ref[...], grad_ref[...]
    sigma = jax.nn.sigmoid(gate)
    gate_grad = (grad * upper * sigma * (1.0 + gate * (1.0 - sigma))).astype(BF16)
    upper_grad = (grad * gate * sigma).astype(BF16)
    dg_ref[...] = gate_grad
    du_ref[...] = upper_grad
    row_ref[...] = jnp.sum(
        gate_grad.astype(F32) * gate + upper_grad.astype(F32) * upper, axis=1, keepdims=True
    )


def row_tiles(rows, most):
    return max(t for t in range(16, most + 1, 16) if rows % t == 0)


def hidden_forward(gate, upper, after):
    rows, width = gate.shape
    tile = row_tiles(rows, 128)
    spec = pl.BlockSpec((tile, width), lambda t: (t, 0))
    return pl.pallas_call(
        hidden_kernel,
        grid=(rows // tile,),
        in_specs=[spec, spec, pl.BlockSpec(memory_space=pl.ANY)],
        out_specs=spec,
        out_shape=jax.ShapeDtypeStruct((rows, width), BF16),
        compiler_params=PARAMS,
        cost_estimate=cost(8 * rows * width, 10 * rows * width),
        name="hidden_forward",
    )(gate, upper, after)


def hidden_backward(gate, upper, grad):
    rows, width = gate.shape
    tile = row_tiles(rows, 128)
    spec = pl.BlockSpec((tile, width), lambda t: (t, 0))
    return pl.pallas_call(
        hidden_backward_kernel,
        grid=(rows // tile,),
        in_specs=[spec] * 3,
        out_specs=[spec, spec, pl.BlockSpec((tile, 1), lambda t: (t, 0))],
        out_shape=[jax.ShapeDtypeStruct((rows, width), BF16)] * 2
        + [jax.ShapeDtypeStruct((rows, 1), F32)],
        compiler_params=PARAMS,
        cost_estimate=cost(20 * rows * width, 16 * rows * width),
        name="hidden_backward",
    )(gate, upper, grad)


def pack_kernel(count, tile, grad_ref, normed_ref, extra_ref, out_ref, sum_ref):
    step = pl.program_id(0)
    rows = out_ref.shape[1] - PAD_ROWS
    width = out_ref.shape[2]
    grad = grad_ref[...]

    @pl.when(step == 0)
    def _():
        sum_ref[...] = jnp.zeros_like(sum_ref)

    sum_ref[...] += jnp.sum(grad * normed_ref[...].astype(F32), axis=0, keepdims=True)
    own = pl.ds(pl.multiple_of(step * tile, tile), tile)
    for j in range(count):
        out_ref[j, own, :] = grad[:, j * width : (j + 1) * width].astype(BF16)

    @pl.when(step == pl.num_programs(0) - 1)
    def _():
        line = lax.broadcasted_iota(jnp.int32, extra_ref.shape, 0)
        last = jnp.where(line == PAD_ROWS - 1, sum_ref[...], extra_ref[...]).astype(BF16)
        for j in range(count):
            out_ref[j, pl.ds(rows, PAD_ROWS), :] = last[:, j * width : (j + 1) * width]


def pack_rows(grad, normed, extra, count):
    rows, width = grad.shape
    tile = row_tiles(rows, 128)
    shape = (count, rows + PAD_ROWS, width // count)
    return pl.pallas_call(
        functools.partial(pack_kernel, count, tile),
        grid=(rows // tile,),
        in_specs=[
            pl.BlockSpec((tile, width), lambda t: (t, 0)),
            pl.BlockSpec((tile, width), lambda t: (t, 0)),
            pl.BlockSpec((PAD_ROWS, width), lambda t: (0, 0)),
        ],
        out_specs=pl.BlockSpec(shape, lambda t: (0, 0, 0)),
        out_shape=jax.ShapeDtypeStruct(shape, BF16),
        scratch_shapes=[pltpu.VMEM((1, width), F32)],
        compiler_params=PARAMS,
        cost_estimate=cost(4 * rows * width, 8 * rows * width),
        name="pack_rows",
    )(grad, normed, extra)


def block_product_kernel(left_ref, right_ref, out_ref):
    out_ref[0] = nn(left_ref[...], right_ref[...]).astype(BF16)


def block_product(left, right, count):
    rows, depth = left.shape
    width = right.shape[1] // count
    return pl.pallas_call(
        block_product_kernel,
        grid=(count,),
        in_specs=[
            pl.BlockSpec((rows, depth), lambda j: (0, 0)),
            pl.BlockSpec((depth, width), lambda j: (0, j)),
        ],
        out_specs=pl.BlockSpec((1, rows, width), lambda j: (j, 0, 0)),
        out_shape=jax.ShapeDtypeStruct((count, rows, width), BF16),
        compiler_params=PARAMS,
        cost_estimate=cost(2 * rows * depth * width * count, 2 * depth * width * count),
        name="block_product",
    )(left, right)


def residual_kernel(place_ref, resid_ref, own_ref, right_ref, left_ref, *outs):
    next_ref, low_ref, branch_ref, square_ref = outs
    branch = own_ref[0].astype(F32) + right_ref[...].astype(F32) + left_ref[...].astype(F32)
    total = resid_ref[...] + branch
    next_ref[...] = total
    low_ref[...] = total.astype(BF16)
    branch_ref[...] = jnp.sum(branch * branch, axis=1, keepdims=True)
    square_ref[...] = jnp.sum(total * total, axis=1, keepdims=True)


def residual_add(place, resid, pieces):
    blocks, right, left = pieces
    rows, width = resid.shape
    tile = row_tiles(rows, 256)
    spec = pl.BlockSpec((tile, width), lambda t, p: (t, 0))
    column = pl.BlockSpec((tile, 1), lambda t, p: (t, 0))
    return pl.pallas_call(
        residual_kernel,
        grid_spec=pltpu.PrefetchScalarGridSpec(
            num_scalar_prefetch=1,
            grid=(rows // tile,),
            in_specs=[
                spec,
                pl.BlockSpec((1, tile, width), lambda t, p: (p[0], t, 0)),
                spec,
                spec,
            ],
            out_specs=[spec, spec, column, column],
        ),
        out_shape=[
            jax.ShapeDtypeStruct((rows, width), F32),
            jax.ShapeDtypeStruct((rows, width), BF16),
            jax.ShapeDtypeStruct((rows, 1), F32),
            jax.ShapeDtypeStruct((rows, 1), F32),
        ],
        compiler_params=PARAMS,
        cost_estimate=cost(8 * rows * width, 16 * rows * width),
        name="residual_add",
    )(place, resid, blocks, right, left)


def gradient_kernel(rows, model_width, place_ref, *refs):
    own_ref, right_ref, left_ref, carried_ref, resid_ref, inverse_ref, gain_ref = refs[:7]
    next_ref, low_ref = refs[7:]
    width = gain_ref.shape[1]
    tile = row_tiles(rows, 128)
    extra = pl.ds(rows, PAD_ROWS)
    dots = own_ref[0, extra, :].astype(F32)
    dots = dots + right_ref[extra, :].astype(F32) + left_ref[extra, :].astype(F32)
    square = lax.broadcasted_iota(jnp.int32, (tile, tile), 0) == lax.broadcasted_iota(
        jnp.int32, (tile, tile), 1
    )
    for step in range(rows // tile):
        span = pl.ds(step * tile, tile)
        line, begin = divmod(step * tile, width)
        row = dots[line : line + 1, begin : begin + tile]
        dot = jnp.sum(jnp.where(square, row, 0.0), axis=1, keepdims=True)
        shard = own_ref[0, span, :].astype(F32)
        shard = shard + right_ref[span, :].astype(F32) + left_ref[span, :].astype(F32)
        inverse = inverse_ref[span, :]
        normed = resid_ref[span, :] * inverse
        grad = carried_ref[span, :] + inverse * (
            shard * gain_ref[...] - normed * (dot * (1.0 / model_width))
        )
        next_ref[span, :] = grad
        low_ref[span, :] = grad.astype(BF16)


def gradient_step(place, pieces, carried, resid, inverse, gain_part, model_width):
    blocks, right, left = pieces
    rows, width = resid.shape
    whole = lambda shape: pl.BlockSpec(shape, lambda t, p: (0,) * len(shape))
    return pl.pallas_call(
        functools.partial(gradient_kernel, rows, model_width),
        grid_spec=pltpu.PrefetchScalarGridSpec(
            num_scalar_prefetch=1,
            grid=(1,),
            in_specs=[
                pl.BlockSpec((1, rows + PAD_ROWS, width), lambda t, p: (p[0], 0, 0)),
                whole(right.shape),
                whole(left.shape),
                whole(carried.shape),
                whole(resid.shape),
                whole(inverse.shape),
                whole((1, width)),
            ],
            out_specs=[whole(resid.shape), whole(resid.shape)],
        ),
        out_shape=[
            jax.ShapeDtypeStruct((rows, width), F32),
            jax.ShapeDtypeStruct((rows, width), BF16),
        ],
        compiler_params=PARAMS,
        cost_estimate=cost(10 * rows * width, 20 * rows * width),
        name="gradient_step",
    )(place, blocks, right, left, carried, resid, inverse, gain_part.reshape(1, width))


def split_kernel(widths, own_ref, *refs):
    count = len(widths)
    kept_ref, away_ref = refs[2 * count :]
    begin = 0
    for j, width in enumerate(widths):
        kept_ref[:, begin : begin + width] = refs[j][...]
        away_ref[:, begin : begin + width] = refs[count + j][...]
        begin += width


def split_rows(own, arrays):
    rows = arrays[0].shape[0] // 2
    widths = [a.shape[1] for a in arrays]
    tile = row_tiles(rows, 256)
    steps = rows // tile
    kept = [pl.BlockSpec((tile, w), lambda t, o: (o[0] * steps + t, 0)) for w in widths]
    away = [pl.BlockSpec((tile, w), lambda t, o: ((1 - o[0]) * steps + t, 0)) for w in widths]
    spec = pl.BlockSpec((tile, sum(widths)), lambda t, o: (t, 0))
    return pl.pallas_call(
        functools.partial(split_kernel, widths),
        grid_spec=pltpu.PrefetchScalarGridSpec(
            num_scalar_prefetch=1,
            grid=(steps,),
            in_specs=kept + away,
            out_specs=[spec, spec],
        ),
        out_shape=[jax.ShapeDtypeStruct((rows, sum(widths)), BF16)] * 2,
        compiler_params=PARAMS,
        cost_estimate=cost(rows * sum(widths), 8 * rows * sum(widths)),
        name="split_rows",
    )(own.reshape(1), *arrays, *arrays)


def finish_kernel(widths, steps, own_ref, *refs):
    sources, outs = refs[:4], refs[4:]
    step = pl.program_id(0)
    for kind in range(2):
        for part in range(2):
            half = own_ref[0] if kind == 0 else 1 - own_ref[0]
            begin = (half * 2 + part) * steps

            @pl.when((step >= begin) & (step < begin + steps))
            def _(source=sources[2 * kind + part]):
                first = 0
                for out, width in zip(outs, widths):
                    out[...] = source[:, first : first + width].astype(F32)
                    first += width


def finish_rows(own, held, arrived, widths):
    rows = held[0].shape[0]
    tile = row_tiles(rows, 128)
    steps = rows // tile

    def place(kind, part):
        def index(t, o):
            half = o[0] if kind == 0 else 1 - o[0]
            return (jnp.clip(t - (half * 2 + part) * steps, 0, steps - 1), 0)

        return index

    specs = [
        pl.BlockSpec((tile, sum(widths)), place(kind, part))
        for kind in range(2)
        for part in range(2)
    ]
    return pl.pallas_call(
        functools.partial(finish_kernel, widths, steps),
        grid_spec=pltpu.PrefetchScalarGridSpec(
            num_scalar_prefetch=1,
            grid=(4 * steps,),
            in_specs=specs,
            out_specs=[pl.BlockSpec((tile, w), lambda t, o: (t, 0)) for w in widths],
        ),
        out_shape=[jax.ShapeDtypeStruct((4 * rows, w), F32) for w in widths],
        compiler_params=PARAMS,
        cost_estimate=cost(rows * sum(widths), 24 * rows * sum(widths)),
        name="finish_rows",
    )(own.reshape(1), *held, *arrived)


def line_gather(part):
    count = lax.axis_size("mp")
    right, left = [part], [part]
    for k in range(1, count):
        right.append(
            lax.ppermute(right[-1], "mp", [(j, j + 1) for j in range(k - 1, count - 1)])
        )
        left.append(lax.ppermute(left[-1], "mp", [(j, j - 1) for j in range(1, count - k + 1)]))
    return part, right[1:], left[1:]


def tie(value, *others):
    if not others:
        return value
    zero = sum(other[(0,) * other.ndim].astype(F32) * 0.0 for other in others)
    return value + zero.astype(value.dtype)


def block_at(blocks, index):
    count = blocks.shape[0]
    return lax.dynamic_index_in_dim(blocks, lax.rem(index + count, count), 0, keepdims=False)


def scatter_sum(blocks):
    count = lax.axis_size("mp")
    place = lax.axis_index("mp")
    right = left = None
    for k in range(1, count):
        to_right, to_left = block_at(blocks, place - k), block_at(blocks, place + k)
        if right is not None:
            to_right, to_left = to_right + right, to_left + left
        right = lax.ppermute(to_right, "mp", [(j, j + 1) for j in range(k)])
        left = lax.ppermute(to_left, "mp", [(j, j - 1) for j in range(count - k, count)])
    return blocks, right, left


def scatter_sum_rows(partial_value, normed, row_values, *lines):
    rows, model_width = partial_value.shape
    count = lax.axis_size("mp")
    width = model_width // count
    places = rows // width
    extra = jnp.tile(row_values.reshape(places, width), (1, count))
    extra = jnp.concatenate([extra] + [line[None] for line in lines], axis=0)
    extra = jnp.pad(extra, ((0, PAD_ROWS - extra.shape[0]), (0, 0)))
    pieces = scatter_sum(pack_rows(partial_value, normed, extra, count))
    tails = [block_at(pieces[0], lax.axis_index("mp"))] + list(pieces[1:])
    tail = sum(part[rows:].astype(F32) for part in tails)
    sums = [tail[-1]] + [tail[places + j] for j in range(len(lines))]
    return pieces, sums


def sum_groups(values, turn):
    count = lax.axis_size("dp")
    listed = [(j + turn) % count for j in range(count)]
    return lax.psum(tuple(values), "dp", axis_index_groups=[listed])


class GroupSum:
    def __init__(self, arrays):
        self.arrays = [array.astype(BF16) for array in arrays]
        count = lax.axis_size("dp")
        self.bits = count.bit_length() - 1
        place = lax.axis_index("dp")
        self.own = [lax.rem(place // 2**bit, 2) for bit in range(self.bits)]
        self.orders = [list(range(1, self.bits)), list(range(1, self.bits))[::-1]]
        self.plan = [self.first]
        self.plan += [lambda *t, k=k: self.reduce(k, *t) for k in range(self.bits - 1)]
        self.plan += [lambda *t, k=k: self.spread(k, *t) for k in reversed(range(self.bits - 1))]
        self.plan += [self.last]

    def swap(self, values, bit):
        count = lax.axis_size("dp")
        return lax.ppermute(values, "dp", [(j, j ^ (1 << bit)) for j in range(count)])

    def half(self, values, which):
        rows = values.shape[0] // 2
        return lax.dynamic_slice_in_dim(values, which * rows, rows, 0)

    def first(self, *after):
        kept, away = split_rows(self.own[0], self.arrays)
        total = kept + self.swap(tie(away, *after), 0)
        rows = total.shape[0] // 2
        self.parts = [total[:rows], total[rows:]]

    def reduce(self, k, *after):
        for p in range(2):
            bit = self.orders[p][k]
            own = self.own[bit]
            arrived = self.swap(tie(self.half(self.parts[p], 1 - own), *after), bit)
            self.parts[p] = self.half(self.parts[p], own) + arrived

    def both(self, values, arrived, own):
        low = jnp.where(own == 0, values, arrived)
        high = jnp.where(own == 0, arrived, values)
        return jnp.concatenate([low, high], axis=0)

    def spread(self, k, *after):
        for p in range(2):
            bit = self.orders[p][k]
            arrived = self.swap(tie(self.parts[p], *after), bit)
            self.parts[p] = self.both(self.parts[p], arrived, self.own[bit])

    def last(self, *after):
        arrived = [self.swap(tie(part, *after), 0) for part in self.parts]
        widths = [a.shape[1] for a in self.arrays]
        self.parts = finish_rows(self.own[0], self.parts, arrived, widths)

    def step(self, *after):
        self.plan.pop(0)(*after)
        return tuple(self.parts)

    def result(self):
        while self.plan:
            self.step()
        return self.parts


def norm_backward(
    normed_grad, normed, row_values, lines, resid, inverse, gain_part, model_width, carried
):
    place = lax.axis_index("mp").astype(jnp.int32).reshape(1)
    pieces, sums = scatter_sum_rows(normed_grad, normed, row_values, *lines)
    grads = gradient_step(place, pieces, carried, resid, inverse, gain_part, model_width)
    return grads, sums


def row_product(*pairs):
    total = 0.0
    for left, right in pairs:
        total = total + jnp.sum(left.astype(F32) * right.astype(F32), axis=1)
    return total


def per_device(
    tokens,
    seq_lengths,
    gain_first,
    lin_query,
    lin_key,
    lin_value,
    lin_out,
    gain_second,
    win_query,
    win_key,
    win_value,
    win_out,
    gain_third,
    gate_weight,
    up_weight,
    down_weight,
    out_cotangent,
):
    row_count, width = tokens.shape
    count = lax.axis_size("mp")
    model_width = width * count
    rows = row_count // CHUNKS
    order = list(range(CHUNKS))
    offset = lax.axis_index("mp") * width
    places = jnp.arange(row_count, dtype=jnp.int32)
    validity = (places < seq_lengths[0, 0] + seq_lengths[0, 1]).astype(F32)
    valid = [validity[c * rows : (c + 1) * rows, None] for c in order]

    def cut(values):
        return [values[c * rows : (c + 1) * rows] for c in order]

    def join(values):
        return jnp.concatenate(values, axis=0) if len(values) > 1 else values[0]

    def part_of(gain):
        return lax.dynamic_slice_in_dim(gain, offset, width).astype(F32)

    blank = [None] * CHUNKS
    low_one, low_two, low_three = list(blank), list(blank), list(blank)
    low_two_grad, low_one_grad = list(blank), list(blank)
    place = lax.axis_index("mp").astype(jnp.int32).reshape(1)
    token_parts = cut(tokens)
    resid_zero = [t.astype(F32) for t in token_parts]
    cot_shard = [c.astype(F32) * v for c, v in zip(cut(out_cotangent), valid)]

    cot_low = join([c.astype(BF16) for c in cot_shard])
    cot_joined = lax.all_gather(cot_low, "mp", axis=1, tiled=True)
    cot_full = cut(cot_joined)
    n1, r1, lq, lk, lv, lo, lo32, lden, b1, resid_one = [list(blank) for _ in range(10)]
    for c in order:
        part = tie(token_parts[c], r1[c - 1]) if c else token_parts[c]
        n1[c], r1[c] = gather_norm(line_gather(part), gain_first)
        lq[c] = nn(n1[c], lin_query).astype(BF16)
        lk[c] = nn(n1[c], lin_key).astype(BF16)
        lv[c] = nn(n1[c], lin_value).astype(BF16)
        lo[c], lo32[c], lden[c] = linear_forward(
            c,
            tie(seq_lengths, cot_joined) if c else seq_lengths,
            lq[c],
            lk[: c + 1],
            lv[: c + 1],
        )
        pieces = scatter_sum(block_product(lo[c], lin_out, count))
        resid_one[c], low_one[c], b1[c], _ = residual_add(place, resid_zero[c], pieces)
    n2, r2, wq, wk, wv, wo, b2, resid_two = [list(blank) for _ in range(8)]
    for c in order:
        n2[c], r2[c] = gather_norm(line_gather(low_one[c]), gain_second)
        wq[c] = nn(n2[c], win_query).astype(BF16)
        wk[c] = nn(n2[c], win_key).astype(BF16)
        wv[c] = nn(n2[c], win_value).astype(BF16)
        before = [wk[c - 1], wv[c - 1]] if c else []
        wo[c] = window_forward(c, seq_lengths, wq[c], wk[c], wv[c], before)
        pieces = scatter_sum(block_product(wo[c], win_out, count))
        resid_two[c], low_two[c], b2[c], _ = residual_add(place, resid_one[c], pieces)
    n3, r3, hid, dg, du, b3, resid_three, dn3, resid_two_grad = [list(blank) for _ in range(9)]
    gates, uppers = list(blank), list(blank)
    for c in order:
        n3[c], r3[c] = gather_norm(line_gather(low_two[c]), gain_third)
        gates[c] = nn(n3[c], gate_weight)
        uppers[c] = nn(n3[c], up_weight)
    def masked(values):
        return sum(jnp.sum(v * p) for v, p in zip(valid, values))

    def stat_line(*values):
        block = jnp.pad(jnp.stack(values), (0, width - len(values)))
        return jnp.tile(block, count)

    stats = stat_line(
        masked([jnp.sum(x * x, axis=1, keepdims=True) for x in resid_zero]), masked(b1), masked(b2)
    )
    sums_three, sums_two, sums_one = list(blank), list(blank), list(blank)
    for c in order:
        hid[c] = hidden_forward(gates[c], uppers[c], cot_joined if c else seq_lengths)
    for c in reversed(order):
        hid_grad = nt(cot_full[c], down_weight)
        dg[c], du[c], row_values = hidden_backward(gates[c], uppers[c], hid_grad)
        dn3[c] = nt(dg[c], gate_weight) + nt(du[c], up_weight)
        (resid_two_grad[c], low_two_grad[c]), sums_three[c] = norm_backward(
            dn3[c],
            n3[c],
            row_values[:, 0],
            (stats,),
            resid_two[c],
            r3[c],
            part_of(gain_third),
            model_width,
            cot_shard[c],
        )
    for c in order:
        pieces = scatter_sum(block_product(hid[c], down_weight, count))
        _, low_three[c], b3[c], resid_three[c] = residual_add(place, resid_two[c], pieces)
    ffn_normed, ffn_hid = join(n3), join(hid)
    down_grad = tn(ffn_hid, cot_joined).astype(BF16)
    down_sums = sum_groups([down_grad], 3)
    ffn_grads = [
        tn(ffn_normed, join(dg)).astype(BF16),
        tn(ffn_normed, join(du)).astype(BF16),
    ]
    ffn_sums = sum_groups(ffn_grads, 0)
    cot_two, wdq, wdk, wdv, dn2, resid_one_grad = [list(blank) for _ in range(6)]
    carry = []
    for c in reversed(order):
        shard = tie(low_two_grad[c], *(ffn_grads if c == 0 else [down_grad]))
        cot_two[c] = gather_join(line_gather(shard))
        mixed_grad = nt(cot_two[c], win_out).astype(BF16)
        before = [wk[c - 1], wv[c - 1]] if c else []
        (wdq[c], wdk[c], wdv[c]), carry = window_backward(
            c, seq_lengths, wq[c], wk[c], wv[c], before, mixed_grad, carry
        )
        dn2[c] = nt(wdq[c], win_query) + nt(wdk[c], win_key) + nt(wdv[c], win_value)
        (resid_one_grad[c], low_one_grad[c]), sums_two[c] = norm_backward(
            dn2[c],
            n2[c],
            row_product((wdq[c], wq[c]), (wdk[c], wk[c]), (wdv[c], wv[c])),
            (),
            resid_one[c],
            r2[c],
            part_of(gain_second),
            model_width,
            resid_two_grad[c],
        )
    win_normed = join(n2)
    win_grads = [
        tn(win_normed, join(wdq)).astype(BF16),
        tn(win_normed, join(wdk)).astype(BF16),
        tn(win_normed, join(wdv)).astype(BF16),
        tn(join(wo), join(cot_two)).astype(BF16),
    ]
    win_sums = sum_groups(win_grads, 1)
    cot_one, ldq, ldk, ldv, dn1, tokens_grad = [list(blank) for _ in range(6)]
    pending = [[] for _ in order]
    for c in reversed(order):
        shard = low_one_grad[c] if c else tie(low_one_grad[c], *win_grads)
        cot_one[c] = gather_join(line_gather(shard))
        mixed_grad = nt(cot_one[c], lin_out)
        carry = []
        if pending[c]:
            carry = [functools.reduce(jnp.add, [p[s] for p in pending[c]]) for s in (0, 1)]
        (ldq[c], ldk[c], ldv[c]), back = linear_backward(
            c,
            seq_lengths,
            lq[c],
            lk[: c + 1],
            lv[: c + 1],
            mixed_grad,
            lo32[c],
            lden[c],
            carry,
        )
        for earlier, pair in enumerate(back):
            pending[earlier].append(pair)
        dn1[c] = nt(ldq[c], lin_query) + nt(ldk[c], lin_key) + nt(ldv[c], lin_value)
        stats = stat_line(masked(b3), masked(resid_three))
        (tokens_grad[c], _), sums_one[c] = norm_backward(
            dn1[c],
            n1[c],
            row_product((ldq[c], lq[c]), (ldk[c], lk[c]), (ldv[c], lv[c])),
            () if c else (stats,),
            resid_zero[c],
            r1[c],
            part_of(gain_first),
            model_width,
            resid_one_grad[c],
        )
    lin_normed = join(n1)
    lin_grads = [
        tn(lin_normed, join(ldq)).astype(BF16),
        tn(lin_normed, join(ldk)).astype(BF16),
        tn(lin_normed, join(ldv)).astype(BF16),
        tn(join(lo), join(cot_one)).astype(BF16),
    ]
    lin_sums = sum_groups(lin_grads, 2)
    small = lax.psum(
        jnp.concatenate(
            [sum(part[0] for part in sums) for sums in (sums_one, sums_two, sums_three)]
            + [sums_three[0][1][:3], sums_one[0][1][:2], jnp.sum(validity)[None]]
        ),
        "dp",
    )
    gain_grads = [
        small[s * width : (s + 1) * width] / part_of(gain)
        for s, gain in enumerate((gain_first, gain_second, gain_third))
    ]
    rms_values = jnp.sqrt(small[3 * width : -1] / (small[-1] * model_width))
    down_sums = [tie(v.astype(F32), wdq[0]) for v in down_sums]
    ffn_sums = [tie(v.astype(F32), ldq[0]) for v in ffn_sums]
    win_sums = [tie(v.astype(F32), tokens_grad[0]) for v in win_sums]
    lin_sums = [v.astype(F32) for v in lin_sums]
    return (
        join(low_three),
        join(tokens_grad),
        gain_grads[0],
        lin_sums[0],
        lin_sums[1],
        lin_sums[2],
        lin_sums[3],
        gain_grads[1],
        win_sums[0],
        win_sums[1],
        win_sums[2],
        win_sums[3],
        gain_grads[2],
        ffn_sums[0],
        ffn_sums[1],
        down_sums[0],
        rms_values,
    )


def solution(mesh):
    in_specs = (
        P("dp", "mp"),
        P("dp", None),
        P(),
        P(None, "mp"),
        P(None, "mp"),
        P(None, "mp"),
        P("mp", None),
        P(),
        P(None, "mp"),
        P(None, "mp"),
        P(None, "mp"),
        P("mp", None),
        P(),
        P(None, "mp"),
        P(None, "mp"),
        P("mp", None),
        P("dp", "mp"),
    )
    out_specs = (
        P("dp", "mp"),
        P("dp", "mp"),
        P("mp"),
        P(None, "mp"),
        P(None, "mp"),
        P(None, "mp"),
        P("mp", None),
        P("mp"),
        P(None, "mp"),
        P(None, "mp"),
        P(None, "mp"),
        P("mp", None),
        P("mp"),
        P(None, "mp"),
        P(None, "mp"),
        P("mp", None),
        P(),
    )
    return jax.shard_map(
        per_device, mesh=mesh, in_specs=in_specs, out_specs=out_specs, check_vma=False
    )
```

```python
import functools

import jax
import jax.numpy as jnp
from jax import lax
from jax.experimental import pallas as pl
from jax.experimental.pallas import tpu as pltpu
from jax.sharding import PartitionSpec as P

FEATURE_SIZE = 16
HEAD_DIM = 128
WINDOW = 64
EPSILON = 1e-05
NEGATIVE = -1e30
CHUNKS = 2
LIN_SCALE = FEATURE_SIZE ** (-0.5)
WIN_SCALE = HEAD_DIM ** (-0.5)
F32 = jnp.float32
BF16 = jnp.bfloat16
PAD_ROWS = 16
VMEM_LIMIT = 40 * 1024 * 1024


def nn(left, right):
    return lax.dot_general(left, right, (((1,), (0,)), ((), ())), preferred_element_type=F32)


def nt(left, right):
    return lax.dot_general(left, right, (((1,), (1,)), ((), ())), preferred_element_type=F32)


def tn(left, right):
    return lax.dot_general(left, right, (((0,), (0,)), ((), ())), preferred_element_type=F32)


def segment_start(lens_ref, place):
    first_end = lens_ref[0, 0]
    second_end = first_end + lens_ref[0, 1]
    return jnp.where(place < first_end, 0, jnp.where(place < second_end, first_end, second_end))


def causal_allowed(lens_ref, row_begin, key_begin, rows, keys, window):
    place = row_begin + lax.broadcasted_iota(jnp.int32, (rows, 1), 0)
    key_place = key_begin + lax.broadcasted_iota(jnp.int32, (rows, keys), 1)
    lowest = segment_start(lens_ref, place)
    if window:
        lowest = jnp.maximum(lowest, place - (window - 1))
    allowed = key_place >= lowest
    if key_begin + keys > row_begin:
        allowed = allowed & (key_place <= place)
    return allowed


def head_lanes(values, head):
    lane = lax.broadcasted_iota(jnp.int32, values.shape, 1) // FEATURE_SIZE
    return jnp.where(lane == head, values, jnp.zeros_like(values))


def linear_tile(lens_ref, query, key, row_begin, key_begin):
    logits = nt(query, key) * LIN_SCALE
    allowed = causal_allowed(lens_ref, row_begin, key_begin, query.shape[0], key.shape[0], 0)
    kernel = jnp.where(allowed, 1.0 + logits + 0.5 * logits * logits, 0.0)
    return logits, allowed, kernel


def linear_forward_kernel(chunk, rows, tile, lens_ref, q_ref, *refs):
    count = chunk + 1
    k_refs, v_refs = refs[:count], refs[count : 2 * count]
    low_ref, mixed_ref, total_ref = refs[2 * count :]
    head = pl.program_id(0)
    per = rows // tile
    for i in range(per):
        row_begin = chunk * rows + i * tile
        query = q_ref[pl.ds(i * tile, tile), :]
        total = jnp.zeros((tile, 1), F32)
        number = jnp.zeros((tile, HEAD_DIM), F32)
        for j in range(chunk * per + i + 1):
            span = pl.ds((j % per) * tile, tile)
            key = head_lanes(k_refs[j // per][span, :], head)
            _, _, kernel = linear_tile(lens_ref, query, key, row_begin, j * tile)
            total += jnp.sum(kernel, axis=1, keepdims=True)
            number += nn(kernel.astype(BF16), v_refs[j // per][span, :])
        mixed = number / total
        low_ref[pl.ds(i * tile, tile), :] = mixed.astype(BF16)
        mixed_ref[pl.ds(i * tile, tile), :] = mixed
        total_ref[0, pl.ds(i * tile, tile), :] = total


def linear_backward_kernel(chunk, rows, tile, carried, lens_ref, q_ref, *refs):
    count = chunk + 1
    k_refs, v_refs = refs[:count], refs[count : 2 * count]
    do_ref, mixed_ref, total_ref = refs[2 * count : 2 * count + 3]
    refs = refs[2 * count + 3 :]
    if carried:
        dk_in, dv_in = refs[:2]
        refs = refs[2:]
    dq_out, dk_out, dv_out = refs[:3]
    dk_prev, dv_prev = refs[3 : 3 + chunk], refs[3 + chunk : 3 + 2 * chunk]
    dq_acc, dk_acc, dv_acc = refs[3 + 2 * chunk :]
    head = pl.program_id(0)
    last = pl.num_programs(0) - 1
    per = rows // tile

    @pl.when(head == 0)
    def _():
        dq_acc[...] = jnp.zeros_like(dq_acc)
        dk_acc[...] = jnp.zeros_like(dk_acc)
        if carried:
            dk_acc[pl.ds(chunk * rows, rows), :] = dk_in[...]

    dv_acc[...] = jnp.zeros_like(dv_acc)
    if carried:
        dv_acc[pl.ds(chunk * rows, rows), :] = dv_in[...]
    for i in range(per):
        row_begin = chunk * rows + i * tile
        own = pl.ds(i * tile, tile)
        query = head_lanes(q_ref[own, :], head)
        grad = do_ref[own, :]
        inverse = 1.0 / total_ref[0, own, :]
        number_grad = (grad * inverse).astype(BF16)
        total_grad = -jnp.sum(grad * mixed_ref[own, :], axis=1, keepdims=True) * inverse
        dq = jnp.zeros((tile, q_ref.shape[1]), F32)
        for j in range(chunk * per + i + 1):
            span = pl.ds((j % per) * tile, tile)
            key = head_lanes(k_refs[j // per][span, :], head)
            logits, allowed, kernel = linear_tile(lens_ref, query, key, row_begin, j * tile)
            kernel_grad = nt(number_grad, v_refs[j // per][span, :]) + total_grad
            scores_grad = jnp.where(allowed, kernel_grad * (1.0 + logits), 0.0).astype(BF16)
            dq += nn(scores_grad, key)
            keys = pl.ds(j * tile, tile)
            dk_acc[keys, :] += tn(scores_grad, query) * LIN_SCALE
            dv_acc[keys, :] += tn(kernel.astype(BF16), number_grad)
        dq_acc[own, :] += dq * LIN_SCALE
    dv_out[...] = dv_acc[pl.ds(chunk * rows, rows), :].astype(BF16)
    for c in range(chunk):
        dv_prev[c][...] = dv_acc[pl.ds(c * rows, rows), :]

    @pl.when(head == last)
    def _():
        dq_out[...] = dq_acc[...].astype(BF16)
        dk_out[...] = dk_acc[pl.ds(chunk * rows, rows), :].astype(BF16)
        for c in range(chunk):
            dk_prev[c][...] = dk_acc[pl.ds(c * rows, rows), :]


def window_tile(lens_ref, query, key, row_begin, key_begin):
    logits = nt(query, key) * WIN_SCALE
    allowed = causal_allowed(lens_ref, row_begin, key_begin, query.shape[0], key.shape[0], WINDOW)
    logits = jnp.where(allowed, logits, NEGATIVE)
    exponent = jnp.exp(logits - jnp.max(logits, axis=1, keepdims=True))
    return exponent / jnp.sum(exponent, axis=1, keepdims=True)


def window_keys(current_ref, prev_ref, i, tile):
    if i > 0:
        return current_ref[pl.ds(i * tile - WINDOW, tile + WINDOW), :], i * tile - WINDOW
    if prev_ref is not None:
        return jnp.concatenate([prev_ref[...], current_ref[pl.ds(0, tile), :]], axis=0), -WINDOW
    return current_ref[pl.ds(0, tile), :], 0


def window_forward_kernel(chunk, rows, tile, lens_ref, q_ref, k_ref, v_ref, *refs):
    k_prev, v_prev = refs[:2] if chunk else (None, None)
    out_ref = refs[-1]
    for i in range(rows // tile):
        own = pl.ds(i * tile, tile)
        key, key_begin = window_keys(k_ref, k_prev, i, tile)
        value, _ = window_keys(v_ref, v_prev, i, tile)
        base = chunk * rows
        weights = window_tile(lens_ref, q_ref[own, :], key, base + i * tile, base + key_begin)
        out_ref[own, :] = nn(weights.astype(BF16), value).astype(BF16)


def window_backward_kernel(chunk, rows, tile, carried, lens_ref, q_ref, k_ref, v_ref, *refs):
    k_prev, v_prev = refs[:2] if chunk else (None, None)
    refs = refs[2:] if chunk else refs
    do_ref, refs = refs[0], refs[1:]
    if carried:
        dk_in, dv_in = refs[:2]
        refs = refs[2:]
    dq_out, dk_out, dv_out = refs[:3]
    dk_back, dv_back = refs[3:5] if chunk else (None, None)
    dk_acc, dv_acc = refs[-2:]
    dk_acc[...] = jnp.zeros_like(dk_acc)
    dv_acc[...] = jnp.zeros_like(dv_acc)
    if carried:
        dk_acc[pl.ds(rows, WINDOW), :] = dk_in[...]
        dv_acc[pl.ds(rows, WINDOW), :] = dv_in[...]
    for i in range(rows // tile):
        own = pl.ds(i * tile, tile)
        key, key_begin = window_keys(k_ref, k_prev, i, tile)
        value, _ = window_keys(v_ref, v_prev, i, tile)
        base = chunk * rows
        query = q_ref[own, :]
        grad = do_ref[own, :]
        weights = window_tile(lens_ref, query, key, base + i * tile, base + key_begin)
        weight_grad = nt(grad, value)
        delta = jnp.sum(weights * weight_grad, axis=1, keepdims=True)
        scores_grad = (weights * (weight_grad - delta)).astype(BF16)
        dq_out[own, :] = (nn(scores_grad, key) * WIN_SCALE).astype(BF16)
        keys = pl.ds(WINDOW + key_begin, key.shape[0])
        dk_acc[keys, :] += tn(scores_grad, query) * WIN_SCALE
        dv_acc[keys, :] += tn(weights.astype(BF16), grad)
    dk_out[...] = dk_acc[pl.ds(WINDOW, rows), :].astype(BF16)
    dv_out[...] = dv_acc[pl.ds(WINDOW, rows), :].astype(BF16)
    if chunk:
        dk_back[...] = dk_acc[pl.ds(0, WINDOW), :]
        dv_back[...] = dv_acc[pl.ds(0, WINDOW), :]


SMEM_SPEC = pl.BlockSpec(memory_space=pltpu.SMEM)
PARAMS = pltpu.CompilerParams(
    dimension_semantics=("arbitrary",), vmem_limit_bytes=VMEM_LIMIT
)


def cost(flops, moved):
    return pl.CostEstimate(flops=flops, bytes_accessed=moved, transcendentals=0)


def narrow_spec(rows, width):
    return pl.BlockSpec((rows, width), lambda h: (0, 0))


def head_spec(rows):
    return pl.BlockSpec((rows, HEAD_DIM), lambda h: (0, h))


def total_spec(rows):
    return pl.BlockSpec((1, rows, 1), lambda h: (h, 0, 0))


def linear_forward(chunk, lengths, query, keys, values):
    rows, width = query.shape
    heads = width // FEATURE_SIZE
    tile = min(256, rows)
    count = chunk + 1
    wide = heads * HEAD_DIM
    return pl.pallas_call(
        functools.partial(linear_forward_kernel, chunk, rows, tile),
        grid=(heads,),
        in_specs=[SMEM_SPEC, narrow_spec(rows, width)]
        + [narrow_spec(rows, width)] * count
        + [head_spec(rows)] * count,
        out_specs=[head_spec(rows), head_spec(rows), total_spec(rows)],
        out_shape=[
            jax.ShapeDtypeStruct((rows, wide), BF16),
            jax.ShapeDtypeStruct((rows, wide), F32),
            jax.ShapeDtypeStruct((heads, rows, 1), F32),
        ],
        compiler_params=PARAMS,
        cost_estimate=cost(4 * heads * rows * rows * count * HEAD_DIM, 8 * rows * wide),
        name="linear_forward",
    )(lengths, query, *keys, *values)


def linear_backward(chunk, lengths, query, keys, values, grad, mixed, total, carry):
    rows, width = query.shape
    heads = width // FEATURE_SIZE
    tile = min(256, rows)
    count = chunk + 1
    wide = heads * HEAD_DIM
    carry = list(carry)
    outs = pl.pallas_call(
        functools.partial(linear_backward_kernel, chunk, rows, tile, bool(carry)),
        grid=(heads,),
        in_specs=[SMEM_SPEC, narrow_spec(rows, width)]
        + [narrow_spec(rows, width)] * count
        + [head_spec(rows)] * count
        + [head_spec(rows), head_spec(rows), total_spec(rows)]
        + ([narrow_spec(rows, width), head_spec(rows)] if carry else []),
        out_specs=[narrow_spec(rows, width), narrow_spec(rows, width), head_spec(rows)]
        + [narrow_spec(rows, width)] * chunk
        + [head_spec(rows)] * chunk,
        out_shape=[
            jax.ShapeDtypeStruct((rows, width), BF16),
            jax.ShapeDtypeStruct((rows, width), BF16),
            jax.ShapeDtypeStruct((rows, wide), BF16),
        ]
        + [jax.ShapeDtypeStruct((rows, width), F32)] * chunk
        + [jax.ShapeDtypeStruct((rows, wide), F32)] * chunk,
        scratch_shapes=[
            pltpu.VMEM((rows, width), F32),
            pltpu.VMEM((count * rows, width), F32),
            pltpu.VMEM((count * rows, HEAD_DIM), F32),
        ],
        compiler_params=PARAMS,
        cost_estimate=cost(10 * heads * rows * rows * count * HEAD_DIM, 16 * rows * wide),
        name="linear_backward",
    )(lengths, query, *keys, *values, grad, mixed, total, *carry)
    return outs[:3], list(zip(outs[3 : 3 + chunk], outs[3 + chunk :]))


def prev_spec(rows):
    return pl.BlockSpec((WINDOW, HEAD_DIM), lambda h: (rows // WINDOW - 1, h))


def edge_spec():
    return pl.BlockSpec((WINDOW, HEAD_DIM), lambda h: (0, h))


def window_forward(chunk, lengths, query, key, value, before):
    rows, wide = query.shape
    heads = wide // HEAD_DIM
    tile = min(256, rows)
    return pl.pallas_call(
        functools.partial(window_forward_kernel, chunk, rows, tile),
        grid=(heads,),
        in_specs=[SMEM_SPEC] + [head_spec(rows)] * 3 + [prev_spec(rows)] * len(before),
        out_specs=head_spec(rows),
        out_shape=jax.ShapeDtypeStruct((rows, wide), BF16),
        compiler_params=PARAMS,
        cost_estimate=cost(4 * rows * 4 * HEAD_DIM * wide, 8 * rows * wide),
        name="window_forward",
    )(lengths, query, key, value, *before)


def window_backward(chunk, lengths, query, key, value, before, grad, carry):
    rows, wide = query.shape
    heads = wide // HEAD_DIM
    tile = min(256, rows)
    carry = list(carry)
    edges = 2 if chunk else 0
    outs = pl.pallas_call(
        functools.partial(window_backward_kernel, chunk, rows, tile, bool(carry)),
        grid=(heads,),
        in_specs=[SMEM_SPEC]
        + [head_spec(rows)] * 3
        + [prev_spec(rows)] * len(before)
        + [head_spec(rows)]
        + [edge_spec()] * len(carry),
        out_specs=[head_spec(rows)] * 3 + [edge_spec()] * edges,
        out_shape=[jax.ShapeDtypeStruct((rows, wide), BF16)] * 3
        + [jax.ShapeDtypeStruct((WINDOW, wide), F32)] * edges,
        scratch_shapes=[pltpu.VMEM((WINDOW + rows, HEAD_DIM), F32)] * 2,
        compiler_params=PARAMS,
        cost_estimate=cost(10 * rows * 4 * HEAD_DIM * wide, 16 * rows * wide),
        name="window_backward",
    )(lengths, query, key, value, *before, grad, *carry)
    return outs[:3], outs[3:]


def gather_norm_kernel(count, width, place_ref, own_ref, *refs):
    right, left = refs[: count - 1], refs[count - 1 : 2 * count - 2]
    gain_ref, normed_ref, inverse_ref, held = refs[2 * count - 2 :]
    place = place_ref[0]
    squares = jnp.zeros((own_ref.shape[0], 1), F32)
    for k in range(count):
        if k == 0:
            piece = own_ref[...].astype(F32)
        else:
            piece = jnp.where(place >= k, right[k - 1][...], left[count - k - 1][...]).astype(F32)
        held[k] = piece
        squares += jnp.sum(piece * piece, axis=1, keepdims=True)
    inverse = lax.rsqrt(squares * (1.0 / (count * width)) + EPSILON)
    inverse_ref[...] = inverse
    for k in range(count):
        block = lax.rem(place - k + count, count)
        columns = pl.ds(pl.multiple_of(block * width, width), width)
        gain = gain_ref[:, columns].astype(F32)
        normed_ref[:, columns] = (held[k] * inverse * gain).astype(BF16)


def gather_norm(pieces, gain_vector):
    own, right, left = pieces
    rows, width = own.shape
    count = len(right) + 1
    tile = min(128, rows)
    place = lax.axis_index("mp").astype(jnp.int32).reshape(1)
    piece_spec = pl.BlockSpec((tile, width), lambda t: (t, 0))
    return pl.pallas_call(
        functools.partial(gather_norm_kernel, count, width),
        grid=(rows // tile,),
        in_specs=[SMEM_SPEC]
        + [piece_spec] * (2 * count - 1)
        + [pl.BlockSpec((1, count * width), lambda t: (0, 0))],
        out_specs=[
            pl.BlockSpec((tile, count * width), lambda t: (t, 0)),
            pl.BlockSpec((tile, 1), lambda t: (t, 0)),
        ],
        out_shape=[
            jax.ShapeDtypeStruct((rows, count * width), BF16),
            jax.ShapeDtypeStruct((rows, 1), F32),
        ],
        scratch_shapes=[pltpu.VMEM((count, tile, width), F32)],
        compiler_params=PARAMS,
        cost_estimate=cost(8 * rows * width * count, 6 * rows * width * count),
        name="gather_norm",
    )(place, own, *right, *left, gain_vector.reshape(1, -1))


def gather_join_kernel(count, width, place_ref, own_ref, *refs):
    right, left = refs[: count - 1], refs[count - 1 : 2 * count - 2]
    out_ref = refs[-1]
    place = place_ref[0]
    for k in range(count):
        if k == 0:
            piece = own_ref[...]
        else:
            piece = jnp.where(place >= k, right[k - 1][...], left[count - k - 1][...])
        block = lax.rem(place - k + count, count)
        out_ref[:, pl.ds(pl.multiple_of(block * width, width), width)] = piece


def gather_join(pieces):
    own, right, left = pieces
    rows, width = own.shape
    count = len(right) + 1
    tile = min(128, rows)
    place = lax.axis_index("mp").astype(jnp.int32).reshape(1)
    piece_spec = pl.BlockSpec((tile, width), lambda t: (t, 0))
    return pl.pallas_call(
        functools.partial(gather_join_kernel, count, width),
        grid=(rows // tile,),
        in_specs=[SMEM_SPEC] + [piece_spec] * (2 * count - 1),
        out_specs=pl.BlockSpec((tile, count * width), lambda t: (t, 0)),
        out_shape=jax.ShapeDtypeStruct((rows, count * width), BF16),
        compiler_params=PARAMS,
        cost_estimate=cost(rows * width * count, 6 * rows * width * count),
        name="gather_join",
    )(place, own, *right, *left)


def hidden_kernel(gate_ref, upper_ref, after_ref, hidden_ref):
    gate = gate_ref[...]
    hidden_ref[...] = (gate * jax.nn.sigmoid(gate) * upper_ref[...]).astype(BF16)


def hidden_backward_kernel(gate_ref, upper_ref, grad_ref, dg_ref, du_ref, row_ref):
    gate, upper, grad = gate_ref[...], upper_ref[...], grad_ref[...]
    sigma = jax.nn.sigmoid(gate)
    gate_grad = (grad * upper * sigma * (1.0 + gate * (1.0 - sigma))).astype(BF16)
    upper_grad = (grad * gate * sigma).astype(BF16)
    dg_ref[...] = gate_grad
    du_ref[...] = upper_grad
    row_ref[...] = jnp.sum(
        gate_grad.astype(F32) * gate + upper_grad.astype(F32) * upper, axis=1, keepdims=True
    )


def row_tiles(rows, most):
    return max(t for t in range(16, most + 1, 16) if rows % t == 0)


def hidden_forward(gate, upper, after):
    rows, width = gate.shape
    tile = row_tiles(rows, 128)
    spec = pl.BlockSpec((tile, width), lambda t: (t, 0))
    return pl.pallas_call(
        hidden_kernel,
        grid=(rows // tile,),
        in_specs=[spec, spec, pl.BlockSpec(memory_space=pl.ANY)],
        out_specs=spec,
        out_shape=jax.ShapeDtypeStruct((rows, width), BF16),
        compiler_params=PARAMS,
        cost_estimate=cost(8 * rows * width, 10 * rows * width),
        name="hidden_forward",
    )(gate, upper, after)


def hidden_backward(gate, upper, grad):
    rows, width = gate.shape
    tile = row_tiles(rows, 128)
    spec = pl.BlockSpec((tile, width), lambda t: (t, 0))
    return pl.pallas_call(
        hidden_backward_kernel,
        grid=(rows // tile,),
        in_specs=[spec] * 3,
        out_specs=[spec, spec, pl.BlockSpec((tile, 1), lambda t: (t, 0))],
        out_shape=[jax.ShapeDtypeStruct((rows, width), BF16)] * 2
        + [jax.ShapeDtypeStruct((rows, 1), F32)],
        compiler_params=PARAMS,
        cost_estimate=cost(20 * rows * width, 16 * rows * width),
        name="hidden_backward",
    )(gate, upper, grad)


def pack_kernel(count, tile, grad_ref, normed_ref, extra_ref, out_ref, sum_ref):
    step = pl.program_id(0)
    rows = out_ref.shape[1] - PAD_ROWS
    width = out_ref.shape[2]
    grad = grad_ref[...]

    @pl.when(step == 0)
    def _():
        sum_ref[...] = jnp.zeros_like(sum_ref)

    sum_ref[...] += jnp.sum(grad * normed_ref[...].astype(F32), axis=0, keepdims=True)
    own = pl.ds(pl.multiple_of(step * tile, tile), tile)
    for j in range(count):
        out_ref[j, own, :] = grad[:, j * width : (j + 1) * width].astype(BF16)

    @pl.when(step == pl.num_programs(0) - 1)
    def _():
        line = lax.broadcasted_iota(jnp.int32, extra_ref.shape, 0)
        last = jnp.where(line == PAD_ROWS - 1, sum_ref[...], extra_ref[...]).astype(BF16)
        for j in range(count):
            out_ref[j, pl.ds(rows, PAD_ROWS), :] = last[:, j * width : (j + 1) * width]


def pack_rows(grad, normed, extra, count):
    rows, width = grad.shape
    tile = row_tiles(rows, 128)
    shape = (count, rows + PAD_ROWS, width // count)
    return pl.pallas_call(
        functools.partial(pack_kernel, count, tile),
        grid=(rows // tile,),
        in_specs=[
            pl.BlockSpec((tile, width), lambda t: (t, 0)),
            pl.BlockSpec((tile, width), lambda t: (t, 0)),
            pl.BlockSpec((PAD_ROWS, width), lambda t: (0, 0)),
        ],
        out_specs=pl.BlockSpec(shape, lambda t: (0, 0, 0)),
        out_shape=jax.ShapeDtypeStruct(shape, BF16),
        scratch_shapes=[pltpu.VMEM((1, width), F32)],
        compiler_params=PARAMS,
        cost_estimate=cost(4 * rows * width, 8 * rows * width),
        name="pack_rows",
    )(grad, normed, extra)


def block_product_kernel(left_ref, right_ref, out_ref):
    out_ref[0] = nn(left_ref[...], right_ref[...]).astype(BF16)


def block_product(left, right, count):
    rows, depth = left.shape
    width = right.shape[1] // count
    return pl.pallas_call(
        block_product_kernel,
        grid=(count,),
        in_specs=[
            pl.BlockSpec((rows, depth), lambda j: (0, 0)),
            pl.BlockSpec((depth, width), lambda j: (0, j)),
        ],
        out_specs=pl.BlockSpec((1, rows, width), lambda j: (j, 0, 0)),
        out_shape=jax.ShapeDtypeStruct((count, rows, width), BF16),
        compiler_params=PARAMS,
        cost_estimate=cost(2 * rows * depth * width * count, 2 * depth * width * count),
        name="block_product",
    )(left, right)


def residual_kernel(place_ref, resid_ref, own_ref, right_ref, left_ref, *outs):
    next_ref, low_ref, branch_ref, square_ref = outs
    branch = own_ref[0].astype(F32) + right_ref[...].astype(F32) + left_ref[...].astype(F32)
    total = resid_ref[...] + branch
    next_ref[...] = total
    low_ref[...] = total.astype(BF16)
    branch_ref[...] = jnp.sum(branch * branch, axis=1, keepdims=True)
    square_ref[...] = jnp.sum(total * total, axis=1, keepdims=True)


def residual_add(place, resid, pieces):
    blocks, right, left = pieces
    rows, width = resid.shape
    tile = row_tiles(rows, 256)
    spec = pl.BlockSpec((tile, width), lambda t, p: (t, 0))
    column = pl.BlockSpec((tile, 1), lambda t, p: (t, 0))
    return pl.pallas_call(
        residual_kernel,
        grid_spec=pltpu.PrefetchScalarGridSpec(
            num_scalar_prefetch=1,
            grid=(rows // tile,),
            in_specs=[
                spec,
                pl.BlockSpec((1, tile, width), lambda t, p: (p[0], t, 0)),
                spec,
                spec,
            ],
            out_specs=[spec, spec, column, column],
        ),
        out_shape=[
            jax.ShapeDtypeStruct((rows, width), F32),
            jax.ShapeDtypeStruct((rows, width), BF16),
            jax.ShapeDtypeStruct((rows, 1), F32),
            jax.ShapeDtypeStruct((rows, 1), F32),
        ],
        compiler_params=PARAMS,
        cost_estimate=cost(8 * rows * width, 16 * rows * width),
        name="residual_add",
    )(place, resid, blocks, right, left)


def gradient_kernel(rows, model_width, place_ref, *refs):
    own_ref, right_ref, left_ref, carried_ref, resid_ref, inverse_ref, gain_ref = refs[:7]
    next_ref, low_ref = refs[7:]
    width = gain_ref.shape[1]
    tile = row_tiles(rows, 128)
    extra = pl.ds(rows, PAD_ROWS)
    dots = own_ref[0, extra, :].astype(F32)
    dots = dots + right_ref[extra, :].astype(F32) + left_ref[extra, :].astype(F32)
    square = lax.broadcasted_iota(jnp.int32, (tile, tile), 0) == lax.broadcasted_iota(
        jnp.int32, (tile, tile), 1
    )
    for step in range(rows // tile):
        span = pl.ds(step * tile, tile)
        line, begin = divmod(step * tile, width)
        row = dots[line : line + 1, begin : begin + tile]
        dot = jnp.sum(jnp.where(square, row, 0.0), axis=1, keepdims=True)
        shard = own_ref[0, span, :].astype(F32)
        shard = shard + right_ref[span, :].astype(F32) + left_ref[span, :].astype(F32)
        inverse = inverse_ref[span, :]
        normed = resid_ref[span, :] * inverse
        grad = carried_ref[span, :] + inverse * (
            shard * gain_ref[...] - normed * (dot * (1.0 / model_width))
        )
        next_ref[span, :] = grad
        low_ref[span, :] = grad.astype(BF16)


def gradient_step(place, pieces, carried, resid, inverse, gain_part, model_width):
    blocks, right, left = pieces
    rows, width = resid.shape
    whole = lambda shape: pl.BlockSpec(shape, lambda t, p: (0,) * len(shape))
    return pl.pallas_call(
        functools.partial(gradient_kernel, rows, model_width),
        grid_spec=pltpu.PrefetchScalarGridSpec(
            num_scalar_prefetch=1,
            grid=(1,),
            in_specs=[
                pl.BlockSpec((1, rows + PAD_ROWS, width), lambda t, p: (p[0], 0, 0)),
                whole(right.shape),
                whole(left.shape),
                whole(carried.shape),
                whole(resid.shape),
                whole(inverse.shape),
                whole((1, width)),
            ],
            out_specs=[whole(resid.shape), whole(resid.shape)],
        ),
        out_shape=[
            jax.ShapeDtypeStruct((rows, width), F32),
            jax.ShapeDtypeStruct((rows, width), BF16),
        ],
        compiler_params=PARAMS,
        cost_estimate=cost(10 * rows * width, 20 * rows * width),
        name="gradient_step",
    )(place, blocks, right, left, carried, resid, inverse, gain_part.reshape(1, width))


def split_kernel(widths, own_ref, *refs):
    count = len(widths)
    kept_ref, away_ref = refs[2 * count :]
    begin = 0
    for j, width in enumerate(widths):
        kept_ref[:, begin : begin + width] = refs[j][...]
        away_ref[:, begin : begin + width] = refs[count + j][...]
        begin += width


def split_rows(own, arrays):
    rows = arrays[0].shape[0] // 2
    widths = [a.shape[1] for a in arrays]
    tile = row_tiles(rows, 256)
    steps = rows // tile
    kept = [pl.BlockSpec((tile, w), lambda t, o: (o[0] * steps + t, 0)) for w in widths]
    away = [pl.BlockSpec((tile, w), lambda t, o: ((1 - o[0]) * steps + t, 0)) for w in widths]
    spec = pl.BlockSpec((tile, sum(widths)), lambda t, o: (t, 0))
    return pl.pallas_call(
        functools.partial(split_kernel, widths),
        grid_spec=pltpu.PrefetchScalarGridSpec(
            num_scalar_prefetch=1,
            grid=(steps,),
            in_specs=kept + away,
            out_specs=[spec, spec],
        ),
        out_shape=[jax.ShapeDtypeStruct((rows, sum(widths)), BF16)] * 2,
        compiler_params=PARAMS,
        cost_estimate=cost(rows * sum(widths), 8 * rows * sum(widths)),
        name="split_rows",
    )(own.reshape(1), *arrays, *arrays)


def finish_kernel(widths, steps, own_ref, *refs):
    sources, outs = refs[:4], refs[4:]
    step = pl.program_id(0)
    for kind in range(2):
        for part in range(2):
            half = own_ref[0] if kind == 0 else 1 - own_ref[0]
            begin = (half * 2 + part) * steps

            @pl.when((step >= begin) & (step < begin + steps))
            def _(source=sources[2 * kind + part]):
                first = 0
                for out, width in zip(outs, widths):
                    out[...] = source[:, first : first + width].astype(F32)
                    first += width


def finish_rows(own, held, arrived, widths):
    rows = held[0].shape[0]
    tile = row_tiles(rows, 128)
    steps = rows // tile

    def place(kind, part):
        def index(t, o):
            half = o[0] if kind == 0 else 1 - o[0]
            return (jnp.clip(t - (half * 2 + part) * steps, 0, steps - 1), 0)

        return index

    specs = [
        pl.BlockSpec((tile, sum(widths)), place(kind, part))
        for kind in range(2)
        for part in range(2)
    ]
    return pl.pallas_call(
        functools.partial(finish_kernel, widths, steps),
        grid_spec=pltpu.PrefetchScalarGridSpec(
            num_scalar_prefetch=1,
            grid=(4 * steps,),
            in_specs=specs,
            out_specs=[pl.BlockSpec((tile, w), lambda t, o: (t, 0)) for w in widths],
        ),
        out_shape=[jax.ShapeDtypeStruct((4 * rows, w), F32) for w in widths],
        compiler_params=PARAMS,
        cost_estimate=cost(rows * sum(widths), 24 * rows * sum(widths)),
        name="finish_rows",
    )(own.reshape(1), *held, *arrived)


def line_gather(part):
    count = lax.axis_size("mp")
    right, left = [part], [part]
    for k in range(1, count):
        right.append(
            lax.ppermute(right[-1], "mp", [(j, j + 1) for j in range(k - 1, count - 1)])
        )
        left.append(lax.ppermute(left[-1], "mp", [(j, j - 1) for j in range(1, count - k + 1)]))
    return part, right[1:], left[1:]


def tie(value, *others):
    if not others:
        return value
    zero = sum(other[(0,) * other.ndim].astype(F32) * 0.0 for other in others)
    return value + zero.astype(value.dtype)


def block_at(blocks, index):
    count = blocks.shape[0]
    return lax.dynamic_index_in_dim(blocks, lax.rem(index + count, count), 0, keepdims=False)


def scatter_sum(blocks):
    count = lax.axis_size("mp")
    place = lax.axis_index("mp")
    right = left = None
    for k in range(1, count):
        to_right, to_left = block_at(blocks, place - k), block_at(blocks, place + k)
        if right is not None:
            to_right, to_left = to_right + right, to_left + left
        right = lax.ppermute(to_right, "mp", [(j, j + 1) for j in range(k)])
        left = lax.ppermute(to_left, "mp", [(j, j - 1) for j in range(count - k, count)])
    return blocks, right, left


def scatter_sum_rows(partial_value, normed, row_values, *lines):
    rows, model_width = partial_value.shape
    count = lax.axis_size("mp")
    width = model_width // count
    places = rows // width
    extra = jnp.tile(row_values.reshape(places, width), (1, count))
    extra = jnp.concatenate([extra] + [line[None] for line in lines], axis=0)
    extra = jnp.pad(extra, ((0, PAD_ROWS - extra.shape[0]), (0, 0)))
    pieces = scatter_sum(pack_rows(partial_value, normed, extra, count))
    tails = [block_at(pieces[0], lax.axis_index("mp"))] + list(pieces[1:])
    tail = sum(part[rows:].astype(F32) for part in tails)
    sums = [tail[-1]] + [tail[places + j] for j in range(len(lines))]
    return pieces, sums


def sum_groups(values, turn):
    count = lax.axis_size("dp")
    listed = [(j + turn) % count for j in range(count)]
    return lax.psum(tuple(values), "dp", axis_index_groups=[listed])


class GroupSum:
    def __init__(self, arrays):
        self.arrays = [array.astype(BF16) for array in arrays]
        count = lax.axis_size("dp")
        self.bits = count.bit_length() - 1
        place = lax.axis_index("dp")
        self.own = [lax.rem(place // 2**bit, 2) for bit in range(self.bits)]
        self.orders = [list(range(1, self.bits)), list(range(1, self.bits))[::-1]]
        self.plan = [self.first]
        self.plan += [lambda *t, k=k: self.reduce(k, *t) for k in range(self.bits - 1)]
        self.plan += [lambda *t, k=k: self.spread(k, *t) for k in reversed(range(self.bits - 1))]
        self.plan += [self.last]

    def swap(self, values, bit):
        count = lax.axis_size("dp")
        return lax.ppermute(values, "dp", [(j, j ^ (1 << bit)) for j in range(count)])

    def half(self, values, which):
        rows = values.shape[0] // 2
        return lax.dynamic_slice_in_dim(values, which * rows, rows, 0)

    def first(self, *after):
        kept, away = split_rows(self.own[0], self.arrays)
        total = kept + self.swap(tie(away, *after), 0)
        rows = total.shape[0] // 2
        self.parts = [total[:rows], total[rows:]]

    def reduce(self, k, *after):
        for p in range(2):
            bit = self.orders[p][k]
            own = self.own[bit]
            arrived = self.swap(tie(self.half(self.parts[p], 1 - own), *after), bit)
            self.parts[p] = self.half(self.parts[p], own) + arrived

    def both(self, values, arrived, own):
        low = jnp.where(own == 0, values, arrived)
        high = jnp.where(own == 0, arrived, values)
        return jnp.concatenate([low, high], axis=0)

    def spread(self, k, *after):
        for p in range(2):
            bit = self.orders[p][k]
            arrived = self.swap(tie(self.parts[p], *after), bit)
            self.parts[p] = self.both(self.parts[p], arrived, self.own[bit])

    def last(self, *after):
        arrived = [self.swap(tie(part, *after), 0) for part in self.parts]
        widths = [a.shape[1] for a in self.arrays]
        self.parts = finish_rows(self.own[0], self.parts, arrived, widths)

    def step(self, *after):
        self.plan.pop(0)(*after)
        return tuple(self.parts)

    def result(self):
        while self.plan:
            self.step()
        return self.parts


def norm_backward(
    normed_grad, normed, row_values, lines, resid, inverse, gain_part, model_width, carried
):
    place = lax.axis_index("mp").astype(jnp.int32).reshape(1)
    pieces, sums = scatter_sum_rows(normed_grad, normed, row_values, *lines)
    grads = gradient_step(place, pieces, carried, resid, inverse, gain_part, model_width)
    return grads, sums


def row_product(*pairs):
    total = 0.0
    for left, right in pairs:
        total = total + jnp.sum(left.astype(F32) * right.astype(F32), axis=1)
    return total


def per_device(
    tokens,
    seq_lengths,
    gain_first,
    lin_query,
    lin_key,
    lin_value,
    lin_out,
    gain_second,
    win_query,
    win_key,
    win_value,
    win_out,
    gain_third,
    gate_weight,
    up_weight,
    down_weight,
    out_cotangent,
):
    row_count, width = tokens.shape
    count = lax.axis_size("mp")
    model_width = width * count
    rows = row_count // CHUNKS
    order = list(range(CHUNKS))
    offset = lax.axis_index("mp") * width
    places = jnp.arange(row_count, dtype=jnp.int32)
    validity = (places < seq_lengths[0, 0] + seq_lengths[0, 1]).astype(F32)
    valid = [validity[c * rows : (c + 1) * rows, None] for c in order]

    def cut(values):
        return [values[c * rows : (c + 1) * rows] for c in order]

    def join(values):
        return jnp.concatenate(values, axis=0) if len(values) > 1 else values[0]

    def part_of(gain):
        return lax.dynamic_slice_in_dim(gain, offset, width).astype(F32)

    blank = [None] * CHUNKS
    low_one, low_two, low_three = list(blank), list(blank), list(blank)
    low_two_grad, low_one_grad = list(blank), list(blank)
    place = lax.axis_index("mp").astype(jnp.int32).reshape(1)
    token_parts = cut(tokens)
    resid_zero = [t.astype(F32) for t in token_parts]
    cot_shard = [c.astype(F32) * v for c, v in zip(cut(out_cotangent), valid)]

    cot_low = join([c.astype(BF16) for c in cot_shard])
    cot_joined = lax.all_gather(cot_low, "mp", axis=1, tiled=True)
    cot_full = cut(cot_joined)
    n1, r1, lq, lk, lv, lo, lo32, lden, b1, resid_one = [list(blank) for _ in range(10)]
    for c in order:
        part = tie(token_parts[c], r1[c - 1]) if c else token_parts[c]
        n1[c], r1[c] = gather_norm(line_gather(part), gain_first)
        lq[c] = nn(n1[c], lin_query).astype(BF16)
        lk[c] = nn(n1[c], lin_key).astype(BF16)
        lv[c] = nn(n1[c], lin_value).astype(BF16)
        lo[c], lo32[c], lden[c] = linear_forward(
            c,
            seq_lengths,
            lq[c],
            lk[: c + 1],
            lv[: c + 1],
        )
        pieces = scatter_sum(block_product(lo[c], lin_out, count))
        resid_one[c], low_one[c], b1[c], _ = residual_add(place, resid_zero[c], pieces)
    n2, r2, wq, wk, wv, wo, b2, resid_two = [list(blank) for _ in range(8)]
    for c in order:
        n2[c], r2[c] = gather_norm(line_gather(low_one[c]), gain_second)
        wq[c] = nn(n2[c], win_query).astype(BF16)
        wk[c] = nn(n2[c], win_key).astype(BF16)
        wv[c] = nn(n2[c], win_value).astype(BF16)
        before = [wk[c - 1], wv[c - 1]] if c else []
        spans = seq_lengths if c else tie(seq_lengths, cot_joined)
        wo[c] = window_forward(c, spans, wq[c], wk[c], wv[c], before)
        pieces = scatter_sum(block_product(wo[c], win_out, count))
        resid_two[c], low_two[c], b2[c], _ = residual_add(place, resid_one[c], pieces)
    n3, r3, hid, dg, du, b3, resid_three, dn3, resid_two_grad = [list(blank) for _ in range(9)]
    gates, uppers = list(blank), list(blank)
    for c in order:
        n3[c], r3[c] = gather_norm(line_gather(low_two[c]), gain_third)
        gates[c] = nn(n3[c], gate_weight)
        uppers[c] = nn(n3[c], up_weight)
    def masked(values):
        return sum(jnp.sum(v * p) for v, p in zip(valid, values))

    def stat_line(*values):
        block = jnp.pad(jnp.stack(values), (0, width - len(values)))
        return jnp.tile(block, count)

    stats = stat_line(
        masked([jnp.sum(x * x, axis=1, keepdims=True) for x in resid_zero]), masked(b1), masked(b2)
    )
    sums_three, sums_two, sums_one = list(blank), list(blank), list(blank)
    for c in order:
        hid[c] = hidden_forward(gates[c], uppers[c], cot_joined if c else seq_lengths)
    for c in reversed(order):
        hid_grad = nt(cot_full[c], down_weight)
        dg[c], du[c], row_values = hidden_backward(gates[c], uppers[c], hid_grad)
        dn3[c] = nt(dg[c], gate_weight) + nt(du[c], up_weight)
        (resid_two_grad[c], low_two_grad[c]), sums_three[c] = norm_backward(
            dn3[c],
            n3[c],
            row_values[:, 0],
            (stats,),
            resid_two[c],
            r3[c],
            part_of(gain_third),
            model_width,
            cot_shard[c],
        )
    for c in order:
        partial_sum = nn(hid[c], down_weight).astype(BF16)
        branch = lax.psum_scatter(partial_sum, "mp", scatter_dimension=1, tiled=True)
        branch = branch.astype(F32)
        total = resid_two[c] + branch
        low_three[c] = total.astype(BF16)
        b3[c] = jnp.sum(branch * branch, axis=1, keepdims=True)
        resid_three[c] = jnp.sum(total * total, axis=1, keepdims=True)
    ffn_normed, ffn_hid = join(n3), join(hid)
    down_grad = tn(ffn_hid, cot_joined).astype(BF16)
    down_sums = sum_groups([down_grad], 3)
    ffn_grads = [
        tn(ffn_normed, join(dg)).astype(BF16),
        tn(ffn_normed, join(du)).astype(BF16),
    ]
    ffn_sums = sum_groups(ffn_grads, 0)
    cot_two, wdq, wdk, wdv, dn2, resid_one_grad = [list(blank) for _ in range(6)]
    carry = []
    for c in reversed(order):
        shard = tie(low_two_grad[c], *(ffn_grads if c == 0 else [down_grad]))
        cot_two[c] = gather_join(line_gather(shard))
        mixed_grad = nt(cot_two[c], win_out).astype(BF16)
        before = [wk[c - 1], wv[c - 1]] if c else []
        (wdq[c], wdk[c], wdv[c]), carry = window_backward(
            c, seq_lengths, wq[c], wk[c], wv[c], before, mixed_grad, carry
        )
        dn2[c] = nt(wdq[c], win_query) + nt(wdk[c], win_key) + nt(wdv[c], win_value)
        (resid_one_grad[c], low_one_grad[c]), sums_two[c] = norm_backward(
            dn2[c],
            n2[c],
            row_product((wdq[c], wq[c]), (wdk[c], wk[c]), (wdv[c], wv[c])),
            (),
            resid_one[c],
            r2[c],
            part_of(gain_second),
            model_width,
            resid_two_grad[c],
        )
    win_normed = join(n2)
    win_grads = [
        tn(win_normed, join(wdq)).astype(BF16),
        tn(win_normed, join(wdk)).astype(BF16),
        tn(win_normed, join(wdv)).astype(BF16),
        tn(join(wo), join(cot_two)).astype(BF16),
    ]
    win_sums = sum_groups(win_grads, 1)
    cot_one, ldq, ldk, ldv, dn1, tokens_grad = [list(blank) for _ in range(6)]
    pending = [[] for _ in order]
    for c in reversed(order):
        shard = low_one_grad[c] if c else tie(low_one_grad[c], *win_grads)
        cot_one[c] = gather_join(line_gather(shard))
        mixed_grad = nt(cot_one[c], lin_out)
        carry = []
        if pending[c]:
            carry = [functools.reduce(jnp.add, [p[s] for p in pending[c]]) for s in (0, 1)]
        (ldq[c], ldk[c], ldv[c]), back = linear_backward(
            c,
            seq_lengths,
            lq[c],
            lk[: c + 1],
            lv[: c + 1],
            mixed_grad,
            lo32[c],
            lden[c],
            carry,
        )
        for earlier, pair in enumerate(back):
            pending[earlier].append(pair)
        dn1[c] = nt(ldq[c], lin_query) + nt(ldk[c], lin_key) + nt(ldv[c], lin_value)
        stats = stat_line(masked(b3), masked(resid_three))
        (tokens_grad[c], _), sums_one[c] = norm_backward(
            dn1[c],
            n1[c],
            row_product((ldq[c], lq[c]), (ldk[c], lk[c]), (ldv[c], lv[c])),
            () if c else (stats,),
            resid_zero[c],
            r1[c],
            part_of(gain_first),
            model_width,
            resid_one_grad[c],
        )
    lin_normed = join(n1)
    lin_grads = [
        tn(lin_normed, join(ldq)).astype(BF16),
        tn(lin_normed, join(ldk)).astype(BF16),
        tn(lin_normed, join(ldv)).astype(BF16),
        tn(join(lo), join(cot_one)).astype(BF16),
    ]
    lin_sums = sum_groups(lin_grads, 2)
    small = lax.psum(
        jnp.concatenate(
            [sum(part[0] for part in sums) for sums in (sums_one, sums_two, sums_three)]
            + [sums_three[0][1][:3], sums_one[0][1][:2], jnp.sum(validity)[None]]
        ),
        "dp",
    )
    gain_grads = [
        small[s * width : (s + 1) * width] / part_of(gain)
        for s, gain in enumerate((gain_first, gain_second, gain_third))
    ]
    rms_values = jnp.sqrt(small[3 * width : -1] / (small[-1] * model_width))
    down_sums = [tie(v.astype(F32), wdq[0]) for v in down_sums]
    ffn_sums = [tie(v.astype(F32), ldq[0]) for v in ffn_sums]
    win_sums = [tie(v.astype(F32), tokens_grad[0]) for v in win_sums]
    lin_sums = [v.astype(F32) for v in lin_sums]
    return (
        join(low_three),
        join(tokens_grad),
        gain_grads[0],
        lin_sums[0],
        lin_sums[1],
        lin_sums[2],
        lin_sums[3],
        gain_grads[1],
        win_sums[0],
        win_sums[1],
        win_sums[2],
        win_sums[3],
        gain_grads[2],
        ffn_sums[0],
        ffn_sums[1],
        down_sums[0],
        rms_values,
    )


def solution(mesh):
    in_specs = (
        P("dp", "mp"),
        P("dp", None),
        P(),
        P(None, "mp"),
        P(None, "mp"),
        P(None, "mp"),
        P("mp", None),
        P(),
        P(None, "mp"),
        P(None, "mp"),
        P(None, "mp"),
        P("mp", None),
        P(),
        P(None, "mp"),
        P(None, "mp"),
        P("mp", None),
        P("dp", "mp"),
    )
    out_specs = (
        P("dp", "mp"),
        P("dp", "mp"),
        P("mp"),
        P(None, "mp"),
        P(None, "mp"),
        P(None, "mp"),
        P("mp", None),
        P("mp"),
        P(None, "mp"),
        P(None, "mp"),
        P(None, "mp"),
        P("mp", None),
        P("mp"),
        P(None, "mp"),
        P(None, "mp"),
        P("mp", None),
        P(),
    )
    return jax.shard_map(
        per_device, mesh=mesh, in_specs=in_specs, out_specs=out_specs, check_vma=False
    )
```

```python
import functools

import jax
import jax.numpy as jnp
from jax import lax
from jax.experimental import pallas as pl
from jax.experimental.pallas import tpu as pltpu
from jax.sharding import PartitionSpec as P

FEATURE_SIZE = 16
HEAD_DIM = 128
WINDOW = 64
EPSILON = 1e-05
NEGATIVE = -1e30
CHUNKS = 2
LIN_SCALE = FEATURE_SIZE ** (-0.5)
WIN_SCALE = HEAD_DIM ** (-0.5)
F32 = jnp.float32
BF16 = jnp.bfloat16
PAD_ROWS = 16
VMEM_LIMIT = 40 * 1024 * 1024


def nn(left, right):
    return lax.dot_general(left, right, (((1,), (0,)), ((), ())), preferred_element_type=F32)


def nt(left, right):
    return lax.dot_general(left, right, (((1,), (1,)), ((), ())), preferred_element_type=F32)


def tn(left, right):
    return lax.dot_general(left, right, (((0,), (0,)), ((), ())), preferred_element_type=F32)


def segment_start(lens_ref, place):
    first_end = lens_ref[0, 0]
    second_end = first_end + lens_ref[0, 1]
    return jnp.where(place < first_end, 0, jnp.where(place < second_end, first_end, second_end))


def causal_allowed(lens_ref, row_begin, key_begin, rows, keys, window):
    place = row_begin + lax.broadcasted_iota(jnp.int32, (rows, 1), 0)
    key_place = key_begin + lax.broadcasted_iota(jnp.int32, (rows, keys), 1)
    lowest = segment_start(lens_ref, place)
    if window:
        lowest = jnp.maximum(lowest, place - (window - 1))
    allowed = key_place >= lowest
    if key_begin + keys > row_begin:
        allowed = allowed & (key_place <= place)
    return allowed


def head_lanes(values, head):
    lane = lax.broadcasted_iota(jnp.int32, values.shape, 1) // FEATURE_SIZE
    return jnp.where(lane == head, values, jnp.zeros_like(values))


def linear_tile(lens_ref, query, key, row_begin, key_begin):
    logits = nt(query, key) * LIN_SCALE
    allowed = causal_allowed(lens_ref, row_begin, key_begin, query.shape[0], key.shape[0], 0)
    kernel = jnp.where(allowed, 1.0 + logits + 0.5 * logits * logits, 0.0)
    return logits, allowed, kernel


def linear_forward_kernel(chunk, rows, tile, lens_ref, q_ref, *refs):
    count = chunk + 1
    k_refs, v_refs = refs[:count], refs[count : 2 * count]
    low_ref, mixed_ref, total_ref = refs[2 * count :]
    head = pl.program_id(0)
    per = rows // tile
    for i in range(per):
        row_begin = chunk * rows + i * tile
        query = q_ref[pl.ds(i * tile, tile), :]
        total = jnp.zeros((tile, 1), F32)
        number = jnp.zeros((tile, HEAD_DIM), F32)
        for j in range(chunk * per + i + 1):
            span = pl.ds((j % per) * tile, tile)
            key = head_lanes(k_refs[j // per][span, :], head)
            _, _, kernel = linear_tile(lens_ref, query, key, row_begin, j * tile)
            total += jnp.sum(kernel, axis=1, keepdims=True)
            number += nn(kernel.astype(BF16), v_refs[j // per][span, :])
        mixed = number / total
        low_ref[pl.ds(i * tile, tile), :] = mixed.astype(BF16)
        mixed_ref[pl.ds(i * tile, tile), :] = mixed
        total_ref[0, pl.ds(i * tile, tile), :] = total


def linear_backward_kernel(chunk, rows, tile, carried, lens_ref, q_ref, *refs):
    count = chunk + 1
    k_refs, v_refs = refs[:count], refs[count : 2 * count]
    do_ref, mixed_ref, total_ref = refs[2 * count : 2 * count + 3]
    refs = refs[2 * count + 3 :]
    if carried:
        dk_in, dv_in = refs[:2]
        refs = refs[2:]
    dq_out, dk_out, dv_out = refs[:3]
    dk_prev, dv_prev = refs[3 : 3 + chunk], refs[3 + chunk : 3 + 2 * chunk]
    dq_acc, dk_acc, dv_acc = refs[3 + 2 * chunk :]
    head = pl.program_id(0)
    last = pl.num_programs(0) - 1
    per = rows // tile

    @pl.when(head == 0)
    def _():
        dq_acc[...] = jnp.zeros_like(dq_acc)
        dk_acc[...] = jnp.zeros_like(dk_acc)
        if carried:
            dk_acc[pl.ds(chunk * rows, rows), :] = dk_in[...]

    dv_acc[...] = jnp.zeros_like(dv_acc)
    if carried:
        dv_acc[pl.ds(chunk * rows, rows), :] = dv_in[...]
    for i in range(per):
        row_begin = chunk * rows + i * tile
        own = pl.ds(i * tile, tile)
        query = head_lanes(q_ref[own, :], head)
        grad = do_ref[own, :]
        inverse = 1.0 / total_ref[0, own, :]
        number_grad = (grad * inverse).astype(BF16)
        total_grad = -jnp.sum(grad * mixed_ref[own, :], axis=1, keepdims=True) * inverse
        dq = jnp.zeros((tile, q_ref.shape[1]), F32)
        for j in range(chunk * per + i + 1):
            span = pl.ds((j % per) * tile, tile)
            key = head_lanes(k_refs[j // per][span, :], head)
            logits, allowed, kernel = linear_tile(lens_ref, query, key, row_begin, j * tile)
            kernel_grad = nt(number_grad, v_refs[j // per][span, :]) + total_grad
            scores_grad = jnp.where(allowed, kernel_grad * (1.0 + logits), 0.0).astype(BF16)
            dq += nn(scores_grad, key)
            keys = pl.ds(j * tile, tile)
            dk_acc[keys, :] += tn(scores_grad, query) * LIN_SCALE
            dv_acc[keys, :] += tn(kernel.astype(BF16), number_grad)
        dq_acc[own, :] += dq * LIN_SCALE
    dv_out[...] = dv_acc[pl.ds(chunk * rows, rows), :].astype(BF16)
    for c in range(chunk):
        dv_prev[c][...] = dv_acc[pl.ds(c * rows, rows), :]

    @pl.when(head == last)
    def _():
        dq_out[...] = dq_acc[...].astype(BF16)
        dk_out[...] = dk_acc[pl.ds(chunk * rows, rows), :].astype(BF16)
        for c in range(chunk):
            dk_prev[c][...] = dk_acc[pl.ds(c * rows, rows), :]


def window_tile(lens_ref, query, key, row_begin, key_begin):
    logits = nt(query, key) * WIN_SCALE
    allowed = causal_allowed(lens_ref, row_begin, key_begin, query.shape[0], key.shape[0], WINDOW)
    logits = jnp.where(allowed, logits, NEGATIVE)
    exponent = jnp.exp(logits - jnp.max(logits, axis=1, keepdims=True))
    return exponent / jnp.sum(exponent, axis=1, keepdims=True)


def window_keys(current_ref, prev_ref, i, tile):
    if i > 0:
        return current_ref[pl.ds(i * tile - WINDOW, tile + WINDOW), :], i * tile - WINDOW
    if prev_ref is not None:
        return jnp.concatenate([prev_ref[...], current_ref[pl.ds(0, tile), :]], axis=0), -WINDOW
    return current_ref[pl.ds(0, tile), :], 0


def window_forward_kernel(chunk, rows, tile, lens_ref, q_ref, k_ref, v_ref, *refs):
    k_prev, v_prev = refs[:2] if chunk else (None, None)
    out_ref = refs[-1]
    for i in range(rows // tile):
        own = pl.ds(i * tile, tile)
        key, key_begin = window_keys(k_ref, k_prev, i, tile)
        value, _ = window_keys(v_ref, v_prev, i, tile)
        base = chunk * rows
        weights = window_tile(lens_ref, q_ref[own, :], key, base + i * tile, base + key_begin)
        out_ref[own, :] = nn(weights.astype(BF16), value).astype(BF16)


def window_backward_kernel(chunk, rows, tile, carried, lens_ref, q_ref, k_ref, v_ref, *refs):
    k_prev, v_prev = refs[:2] if chunk else (None, None)
    refs = refs[2:] if chunk else refs
    do_ref, refs = refs[0], refs[1:]
    if carried:
        dk_in, dv_in = refs[:2]
        refs = refs[2:]
    dq_out, dk_out, dv_out = refs[:3]
    dk_back, dv_back = refs[3:5] if chunk else (None, None)
    dk_acc, dv_acc = refs[-2:]
    dk_acc[...] = jnp.zeros_like(dk_acc)
    dv_acc[...] = jnp.zeros_like(dv_acc)
    if carried:
        dk_acc[pl.ds(rows, WINDOW), :] = dk_in[...]
        dv_acc[pl.ds(rows, WINDOW), :] = dv_in[...]
    for i in range(rows // tile):
        own = pl.ds(i * tile, tile)
        key, key_begin = window_keys(k_ref, k_prev, i, tile)
        value, _ = window_keys(v_ref, v_prev, i, tile)
        base = chunk * rows
        query = q_ref[own, :]
        grad = do_ref[own, :]
        weights = window_tile(lens_ref, query, key, base + i * tile, base + key_begin)
        weight_grad = nt(grad, value)
        delta = jnp.sum(weights * weight_grad, axis=1, keepdims=True)
        scores_grad = (weights * (weight_grad - delta)).astype(BF16)
        dq_out[own, :] = (nn(scores_grad, key) * WIN_SCALE).astype(BF16)
        keys = pl.ds(WINDOW + key_begin, key.shape[0])
        dk_acc[keys, :] += tn(scores_grad, query) * WIN_SCALE
        dv_acc[keys, :] += tn(weights.astype(BF16), grad)
    dk_out[...] = dk_acc[pl.ds(WINDOW, rows), :].astype(BF16)
    dv_out[...] = dv_acc[pl.ds(WINDOW, rows), :].astype(BF16)
    if chunk:
        dk_back[...] = dk_acc[pl.ds(0, WINDOW), :]
        dv_back[...] = dv_acc[pl.ds(0, WINDOW), :]


SMEM_SPEC = pl.BlockSpec(memory_space=pltpu.SMEM)
PARAMS = pltpu.CompilerParams(
    dimension_semantics=("arbitrary",), vmem_limit_bytes=VMEM_LIMIT
)


def cost(flops, moved):
    return pl.CostEstimate(flops=flops, bytes_accessed=moved, transcendentals=0)


def narrow_spec(rows, width):
    return pl.BlockSpec((rows, width), lambda h: (0, 0))


def head_spec(rows):
    return pl.BlockSpec((rows, HEAD_DIM), lambda h: (0, h))


def total_spec(rows):
    return pl.BlockSpec((1, rows, 1), lambda h: (h, 0, 0))


def linear_forward(chunk, lengths, query, keys, values):
    rows, width = query.shape
    heads = width // FEATURE_SIZE
    tile = min(256, rows)
    count = chunk + 1
    wide = heads * HEAD_DIM
    return pl.pallas_call(
        functools.partial(linear_forward_kernel, chunk, rows, tile),
        grid=(heads,),
        in_specs=[SMEM_SPEC, narrow_spec(rows, width)]
        + [narrow_spec(rows, width)] * count
        + [head_spec(rows)] * count,
        out_specs=[head_spec(rows), head_spec(rows), total_spec(rows)],
        out_shape=[
            jax.ShapeDtypeStruct((rows, wide), BF16),
            jax.ShapeDtypeStruct((rows, wide), F32),
            jax.ShapeDtypeStruct((heads, rows, 1), F32),
        ],
        compiler_params=PARAMS,
        cost_estimate=cost(4 * heads * rows * rows * count * HEAD_DIM, 8 * rows * wide),
        name="linear_forward",
    )(lengths, query, *keys, *values)


def linear_backward(chunk, lengths, query, keys, values, grad, mixed, total, carry):
    rows, width = query.shape
    heads = width // FEATURE_SIZE
    tile = min(512, rows)
    count = chunk + 1
    wide = heads * HEAD_DIM
    carry = list(carry)
    outs = pl.pallas_call(
        functools.partial(linear_backward_kernel, chunk, rows, tile, bool(carry)),
        grid=(heads,),
        in_specs=[SMEM_SPEC, narrow_spec(rows, width)]
        + [narrow_spec(rows, width)] * count
        + [head_spec(rows)] * count
        + [head_spec(rows), head_spec(rows), total_spec(rows)]
        + ([narrow_spec(rows, width), head_spec(rows)] if carry else []),
        out_specs=[narrow_spec(rows, width), narrow_spec(rows, width), head_spec(rows)]
        + [narrow_spec(rows, width)] * chunk
        + [head_spec(rows)] * chunk,
        out_shape=[
            jax.ShapeDtypeStruct((rows, width), BF16),
            jax.ShapeDtypeStruct((rows, width), BF16),
            jax.ShapeDtypeStruct((rows, wide), BF16),
        ]
        + [jax.ShapeDtypeStruct((rows, width), F32)] * chunk
        + [jax.ShapeDtypeStruct((rows, wide), F32)] * chunk,
        scratch_shapes=[
            pltpu.VMEM((rows, width), F32),
            pltpu.VMEM((count * rows, width), F32),
            pltpu.VMEM((count * rows, HEAD_DIM), F32),
        ],
        compiler_params=PARAMS,
        cost_estimate=cost(10 * heads * rows * rows * count * HEAD_DIM, 16 * rows * wide),
        name="linear_backward",
    )(lengths, query, *keys, *values, grad, mixed, total, *carry)
    return outs[:3], list(zip(outs[3 : 3 + chunk], outs[3 + chunk :]))


def prev_spec(rows):
    return pl.BlockSpec((WINDOW, HEAD_DIM), lambda h: (rows // WINDOW - 1, h))


def edge_spec():
    return pl.BlockSpec((WINDOW, HEAD_DIM), lambda h: (0, h))


def window_forward(chunk, lengths, query, key, value, before):
    rows, wide = query.shape
    heads = wide // HEAD_DIM
    tile = min(256, rows)
    return pl.pallas_call(
        functools.partial(window_forward_kernel, chunk, rows, tile),
        grid=(heads,),
        in_specs=[SMEM_SPEC] + [head_spec(rows)] * 3 + [prev_spec(rows)] * len(before),
        out_specs=head_spec(rows),
        out_shape=jax.ShapeDtypeStruct((rows, wide), BF16),
        compiler_params=PARAMS,
        cost_estimate=cost(4 * rows * 4 * HEAD_DIM * wide, 8 * rows * wide),
        name="window_forward",
    )(lengths, query, key, value, *before)


def window_backward(chunk, lengths, query, key, value, before, grad, carry):
    rows, wide = query.shape
    heads = wide // HEAD_DIM
    tile = min(256, rows)
    carry = list(carry)
    edges = 2 if chunk else 0
    outs = pl.pallas_call(
        functools.partial(window_backward_kernel, chunk, rows, tile, bool(carry)),
        grid=(heads,),
        in_specs=[SMEM_SPEC]
        + [head_spec(rows)] * 3
        + [prev_spec(rows)] * len(before)
        + [head_spec(rows)]
        + [edge_spec()] * len(carry),
        out_specs=[head_spec(rows)] * 3 + [edge_spec()] * edges,
        out_shape=[jax.ShapeDtypeStruct((rows, wide), BF16)] * 3
        + [jax.ShapeDtypeStruct((WINDOW, wide), F32)] * edges,
        scratch_shapes=[pltpu.VMEM((WINDOW + rows, HEAD_DIM), F32)] * 2,
        compiler_params=PARAMS,
        cost_estimate=cost(10 * rows * 4 * HEAD_DIM * wide, 16 * rows * wide),
        name="window_backward",
    )(lengths, query, key, value, *before, grad, *carry)
    return outs[:3], outs[3:]


def gather_norm_kernel(count, width, place_ref, own_ref, *refs):
    right, left = refs[: count - 1], refs[count - 1 : 2 * count - 2]
    gain_ref, normed_ref, inverse_ref, held = refs[2 * count - 2 :]
    place = place_ref[0]
    squares = jnp.zeros((own_ref.shape[0], 1), F32)
    for k in range(count):
        if k == 0:
            piece = own_ref[...].astype(F32)
        else:
            piece = jnp.where(place >= k, right[k - 1][...], left[count - k - 1][...]).astype(F32)
        held[k] = piece
        squares += jnp.sum(piece * piece, axis=1, keepdims=True)
    inverse = lax.rsqrt(squares * (1.0 / (count * width)) + EPSILON)
    inverse_ref[...] = inverse
    for k in range(count):
        block = lax.rem(place - k + count, count)
        columns = pl.ds(pl.multiple_of(block * width, width), width)
        gain = gain_ref[:, columns].astype(F32)
        normed_ref[:, columns] = (held[k] * inverse * gain).astype(BF16)


def gather_norm(pieces, gain_vector):
    own, right, left = pieces
    rows, width = own.shape
    count = len(right) + 1
    tile = min(256, rows)
    place = lax.axis_index("mp").astype(jnp.int32).reshape(1)
    piece_spec = pl.BlockSpec((tile, width), lambda t: (t, 0))
    return pl.pallas_call(
        functools.partial(gather_norm_kernel, count, width),
        grid=(rows // tile,),
        in_specs=[SMEM_SPEC]
        + [piece_spec] * (2 * count - 1)
        + [pl.BlockSpec((1, count * width), lambda t: (0, 0))],
        out_specs=[
            pl.BlockSpec((tile, count * width), lambda t: (t, 0)),
            pl.BlockSpec((tile, 1), lambda t: (t, 0)),
        ],
        out_shape=[
            jax.ShapeDtypeStruct((rows, count * width), BF16),
            jax.ShapeDtypeStruct((rows, 1), F32),
        ],
        scratch_shapes=[pltpu.VMEM((count, tile, width), F32)],
        compiler_params=PARAMS,
        cost_estimate=cost(8 * rows * width * count, 6 * rows * width * count),
        name="gather_norm",
    )(place, own, *right, *left, gain_vector.reshape(1, -1))


def gather_join_kernel(count, width, place_ref, own_ref, *refs):
    right, left = refs[: count - 1], refs[count - 1 : 2 * count - 2]
    out_ref = refs[-1]
    place = place_ref[0]
    for k in range(count):
        if k == 0:
            piece = own_ref[...]
        else:
            piece = jnp.where(place >= k, right[k - 1][...], left[count - k - 1][...])
        block = lax.rem(place - k + count, count)
        out_ref[:, pl.ds(pl.multiple_of(block * width, width), width)] = piece


def gather_join(pieces):
    own, right, left = pieces
    rows, width = own.shape
    count = len(right) + 1
    tile = min(256, rows)
    place = lax.axis_index("mp").astype(jnp.int32).reshape(1)
    piece_spec = pl.BlockSpec((tile, width), lambda t: (t, 0))
    return pl.pallas_call(
        functools.partial(gather_join_kernel, count, width),
        grid=(rows // tile,),
        in_specs=[SMEM_SPEC] + [piece_spec] * (2 * count - 1),
        out_specs=pl.BlockSpec((tile, count * width), lambda t: (t, 0)),
        out_shape=jax.ShapeDtypeStruct((rows, count * width), BF16),
        compiler_params=PARAMS,
        cost_estimate=cost(rows * width * count, 6 * rows * width * count),
        name="gather_join",
    )(place, own, *right, *left)


def hidden_kernel(gate_ref, upper_ref, after_ref, hidden_ref):
    gate = gate_ref[...]
    hidden_ref[...] = (gate * jax.nn.sigmoid(gate) * upper_ref[...]).astype(BF16)


def hidden_backward_kernel(gate_ref, upper_ref, grad_ref, dg_ref, du_ref, row_ref):
    gate, upper, grad = gate_ref[...], upper_ref[...], grad_ref[...]
    sigma = jax.nn.sigmoid(gate)
    gate_grad = (grad * upper * sigma * (1.0 + gate * (1.0 - sigma))).astype(BF16)
    upper_grad = (grad * gate * sigma).astype(BF16)
    dg_ref[...] = gate_grad
    du_ref[...] = upper_grad
    row_ref[...] = jnp.sum(
        gate_grad.astype(F32) * gate + upper_grad.astype(F32) * upper, axis=1, keepdims=True
    )


def row_tiles(rows, most):
    return max(t for t in range(16, most + 1, 16) if rows % t == 0)


def hidden_forward(gate, upper, after):
    rows, width = gate.shape
    tile = row_tiles(rows, 128)
    spec = pl.BlockSpec((tile, width), lambda t: (t, 0))
    return pl.pallas_call(
        hidden_kernel,
        grid=(rows // tile,),
        in_specs=[spec, spec, pl.BlockSpec(memory_space=pl.ANY)],
        out_specs=spec,
        out_shape=jax.ShapeDtypeStruct((rows, width), BF16),
        compiler_params=PARAMS,
        cost_estimate=cost(8 * rows * width, 10 * rows * width),
        name="hidden_forward",
    )(gate, upper, after)


def hidden_backward(gate, upper, grad):
    rows, width = gate.shape
    tile = row_tiles(rows, 128)
    spec = pl.BlockSpec((tile, width), lambda t: (t, 0))
    return pl.pallas_call(
        hidden_backward_kernel,
        grid=(rows // tile,),
        in_specs=[spec] * 3,
        out_specs=[spec, spec, pl.BlockSpec((tile, 1), lambda t: (t, 0))],
        out_shape=[jax.ShapeDtypeStruct((rows, width), BF16)] * 2
        + [jax.ShapeDtypeStruct((rows, 1), F32)],
        compiler_params=PARAMS,
        cost_estimate=cost(20 * rows * width, 16 * rows * width),
        name="hidden_backward",
    )(gate, upper, grad)


def pack_kernel(count, tile, grad_ref, normed_ref, extra_ref, out_ref, sum_ref):
    step = pl.program_id(0)
    rows = out_ref.shape[1] - PAD_ROWS
    width = out_ref.shape[2]
    grad = grad_ref[...]

    @pl.when(step == 0)
    def _():
        sum_ref[...] = jnp.zeros_like(sum_ref)

    sum_ref[...] += jnp.sum(grad * normed_ref[...].astype(F32), axis=0, keepdims=True)
    own = pl.ds(pl.multiple_of(step * tile, tile), tile)
    for j in range(count):
        out_ref[j, own, :] = grad[:, j * width : (j + 1) * width].astype(BF16)

    @pl.when(step == pl.num_programs(0) - 1)
    def _():
        line = lax.broadcasted_iota(jnp.int32, extra_ref.shape, 0)
        last = jnp.where(line == PAD_ROWS - 1, sum_ref[...], extra_ref[...]).astype(BF16)
        for j in range(count):
            out_ref[j, pl.ds(rows, PAD_ROWS), :] = last[:, j * width : (j + 1) * width]


def pack_rows(grad, normed, extra, count):
    rows, width = grad.shape
    tile = row_tiles(rows, 128)
    shape = (count, rows + PAD_ROWS, width // count)
    return pl.pallas_call(
        functools.partial(pack_kernel, count, tile),
        grid=(rows // tile,),
        in_specs=[
            pl.BlockSpec((tile, width), lambda t: (t, 0)),
            pl.BlockSpec((tile, width), lambda t: (t, 0)),
            pl.BlockSpec((PAD_ROWS, width), lambda t: (0, 0)),
        ],
        out_specs=pl.BlockSpec(shape, lambda t: (0, 0, 0)),
        out_shape=jax.ShapeDtypeStruct(shape, BF16),
        scratch_shapes=[pltpu.VMEM((1, width), F32)],
        compiler_params=PARAMS,
        cost_estimate=cost(4 * rows * width, 8 * rows * width),
        name="pack_rows",
    )(grad, normed, extra)


def block_product_kernel(left_ref, right_ref, out_ref):
    out_ref[0] = nn(left_ref[...], right_ref[...]).astype(BF16)


def block_product(left, right, count):
    rows, depth = left.shape
    width = right.shape[1] // count
    return pl.pallas_call(
        block_product_kernel,
        grid=(count,),
        in_specs=[
            pl.BlockSpec((rows, depth), lambda j: (0, 0)),
            pl.BlockSpec((depth, width), lambda j: (0, j)),
        ],
        out_specs=pl.BlockSpec((1, rows, width), lambda j: (j, 0, 0)),
        out_shape=jax.ShapeDtypeStruct((count, rows, width), BF16),
        compiler_params=PARAMS,
        cost_estimate=cost(2 * rows * depth * width * count, 2 * depth * width * count),
        name="block_product",
    )(left, right)


def residual_kernel(place_ref, resid_ref, own_ref, right_ref, left_ref, *outs):
    next_ref, low_ref, branch_ref, square_ref = outs
    branch = own_ref[0].astype(F32) + right_ref[...].astype(F32) + left_ref[...].astype(F32)
    total = resid_ref[...] + branch
    next_ref[...] = total
    low_ref[...] = total.astype(BF16)
    branch_ref[...] = jnp.sum(branch * branch, axis=1, keepdims=True)
    square_ref[...] = jnp.sum(total * total, axis=1, keepdims=True)


def residual_add(place, resid, pieces):
    blocks, right, left = pieces
    rows, width = resid.shape
    tile = row_tiles(rows, 256)
    spec = pl.BlockSpec((tile, width), lambda t, p: (t, 0))
    column = pl.BlockSpec((tile, 1), lambda t, p: (t, 0))
    return pl.pallas_call(
        residual_kernel,
        grid_spec=pltpu.PrefetchScalarGridSpec(
            num_scalar_prefetch=1,
            grid=(rows // tile,),
            in_specs=[
                spec,
                pl.BlockSpec((1, tile, width), lambda t, p: (p[0], t, 0)),
                spec,
                spec,
            ],
            out_specs=[spec, spec, column, column],
        ),
        out_shape=[
            jax.ShapeDtypeStruct((rows, width), F32),
            jax.ShapeDtypeStruct((rows, width), BF16),
            jax.ShapeDtypeStruct((rows, 1), F32),
            jax.ShapeDtypeStruct((rows, 1), F32),
        ],
        compiler_params=PARAMS,
        cost_estimate=cost(8 * rows * width, 16 * rows * width),
        name="residual_add",
    )(place, resid, blocks, right, left)


def gradient_kernel(rows, model_width, place_ref, *refs):
    own_ref, right_ref, left_ref, carried_ref, resid_ref, inverse_ref, gain_ref = refs[:7]
    next_ref, low_ref = refs[7:]
    width = gain_ref.shape[1]
    tile = row_tiles(rows, 128)
    extra = pl.ds(rows, PAD_ROWS)
    dots = own_ref[0, extra, :].astype(F32)
    dots = dots + right_ref[extra, :].astype(F32) + left_ref[extra, :].astype(F32)
    square = lax.broadcasted_iota(jnp.int32, (tile, tile), 0) == lax.broadcasted_iota(
        jnp.int32, (tile, tile), 1
    )
    for step in range(rows // tile):
        span = pl.ds(step * tile, tile)
        line, begin = divmod(step * tile, width)
        row = dots[line : line + 1, begin : begin + tile]
        dot = jnp.sum(jnp.where(square, row, 0.0), axis=1, keepdims=True)
        shard = own_ref[0, span, :].astype(F32)
        shard = shard + right_ref[span, :].astype(F32) + left_ref[span, :].astype(F32)
        inverse = inverse_ref[span, :]
        normed = resid_ref[span, :] * inverse
        grad = carried_ref[span, :] + inverse * (
            shard * gain_ref[...] - normed * (dot * (1.0 / model_width))
        )
        next_ref[span, :] = grad
        low_ref[span, :] = grad.astype(BF16)


def gradient_step(place, pieces, carried, resid, inverse, gain_part, model_width):
    blocks, right, left = pieces
    rows, width = resid.shape
    whole = lambda shape: pl.BlockSpec(shape, lambda t, p: (0,) * len(shape))
    return pl.pallas_call(
        functools.partial(gradient_kernel, rows, model_width),
        grid_spec=pltpu.PrefetchScalarGridSpec(
            num_scalar_prefetch=1,
            grid=(1,),
            in_specs=[
                pl.BlockSpec((1, rows + PAD_ROWS, width), lambda t, p: (p[0], 0, 0)),
                whole(right.shape),
                whole(left.shape),
                whole(carried.shape),
                whole(resid.shape),
                whole(inverse.shape),
                whole((1, width)),
            ],
            out_specs=[whole(resid.shape), whole(resid.shape)],
        ),
        out_shape=[
            jax.ShapeDtypeStruct((rows, width), F32),
            jax.ShapeDtypeStruct((rows, width), BF16),
        ],
        compiler_params=PARAMS,
        cost_estimate=cost(10 * rows * width, 20 * rows * width),
        name="gradient_step",
    )(place, blocks, right, left, carried, resid, inverse, gain_part.reshape(1, width))


def split_kernel(widths, own_ref, *refs):
    count = len(widths)
    kept_ref, away_ref = refs[2 * count :]
    begin = 0
    for j, width in enumerate(widths):
        kept_ref[:, begin : begin + width] = refs[j][...]
        away_ref[:, begin : begin + width] = refs[count + j][...]
        begin += width


def split_rows(own, arrays):
    rows = arrays[0].shape[0] // 2
    widths = [a.shape[1] for a in arrays]
    tile = row_tiles(rows, 256)
    steps = rows // tile
    kept = [pl.BlockSpec((tile, w), lambda t, o: (o[0] * steps + t, 0)) for w in widths]
    away = [pl.BlockSpec((tile, w), lambda t, o: ((1 - o[0]) * steps + t, 0)) for w in widths]
    spec = pl.BlockSpec((tile, sum(widths)), lambda t, o: (t, 0))
    return pl.pallas_call(
        functools.partial(split_kernel, widths),
        grid_spec=pltpu.PrefetchScalarGridSpec(
            num_scalar_prefetch=1,
            grid=(steps,),
            in_specs=kept + away,
            out_specs=[spec, spec],
        ),
        out_shape=[jax.ShapeDtypeStruct((rows, sum(widths)), BF16)] * 2,
        compiler_params=PARAMS,
        cost_estimate=cost(rows * sum(widths), 8 * rows * sum(widths)),
        name="split_rows",
    )(own.reshape(1), *arrays, *arrays)


def finish_kernel(widths, steps, own_ref, *refs):
    sources, outs = refs[:4], refs[4:]
    step = pl.program_id(0)
    for kind in range(2):
        for part in range(2):
            half = own_ref[0] if kind == 0 else 1 - own_ref[0]
            begin = (half * 2 + part) * steps

            @pl.when((step >= begin) & (step < begin + steps))
            def _(source=sources[2 * kind + part]):
                first = 0
                for out, width in zip(outs, widths):
                    out[...] = source[:, first : first + width].astype(F32)
                    first += width


def finish_rows(own, held, arrived, widths):
    rows = held[0].shape[0]
    tile = row_tiles(rows, 128)
    steps = rows // tile

    def place(kind, part):
        def index(t, o):
            half = o[0] if kind == 0 else 1 - o[0]
            return (jnp.clip(t - (half * 2 + part) * steps, 0, steps - 1), 0)

        return index

    specs = [
        pl.BlockSpec((tile, sum(widths)), place(kind, part))
        for kind in range(2)
        for part in range(2)
    ]
    return pl.pallas_call(
        functools.partial(finish_kernel, widths, steps),
        grid_spec=pltpu.PrefetchScalarGridSpec(
            num_scalar_prefetch=1,
            grid=(4 * steps,),
            in_specs=specs,
            out_specs=[pl.BlockSpec((tile, w), lambda t, o: (t, 0)) for w in widths],
        ),
        out_shape=[jax.ShapeDtypeStruct((4 * rows, w), F32) for w in widths],
        compiler_params=PARAMS,
        cost_estimate=cost(rows * sum(widths), 24 * rows * sum(widths)),
        name="finish_rows",
    )(own.reshape(1), *held, *arrived)


def line_gather(part):
    count = lax.axis_size("mp")
    right, left = [part], [part]
    for k in range(1, count):
        right.append(
            lax.ppermute(right[-1], "mp", [(j, j + 1) for j in range(k - 1, count - 1)])
        )
        left.append(lax.ppermute(left[-1], "mp", [(j, j - 1) for j in range(1, count - k + 1)]))
    return part, right[1:], left[1:]


def tie(value, *others):
    if not others:
        return value
    zero = sum(other[(0,) * other.ndim].astype(F32) * 0.0 for other in others)
    return value + zero.astype(value.dtype)


def block_at(blocks, index):
    count = blocks.shape[0]
    return lax.dynamic_index_in_dim(blocks, lax.rem(index + count, count), 0, keepdims=False)


def scatter_sum(blocks):
    count = lax.axis_size("mp")
    place = lax.axis_index("mp")
    right = left = None
    for k in range(1, count):
        to_right, to_left = block_at(blocks, place - k), block_at(blocks, place + k)
        if right is not None:
            to_right, to_left = to_right + right, to_left + left
        right = lax.ppermute(to_right, "mp", [(j, j + 1) for j in range(k)])
        left = lax.ppermute(to_left, "mp", [(j, j - 1) for j in range(count - k, count)])
    return blocks, right, left


def scatter_sum_rows(partial_value, normed, row_values, *lines):
    rows, model_width = partial_value.shape
    count = lax.axis_size("mp")
    width = model_width // count
    places = rows // width
    extra = jnp.tile(row_values.reshape(places, width), (1, count))
    extra = jnp.concatenate([extra] + [line[None] for line in lines], axis=0)
    extra = jnp.pad(extra, ((0, PAD_ROWS - extra.shape[0]), (0, 0)))
    pieces = scatter_sum(pack_rows(partial_value, normed, extra, count))
    tails = [block_at(pieces[0], lax.axis_index("mp"))] + list(pieces[1:])
    tail = sum(part[rows:].astype(F32) for part in tails)
    sums = [tail[-1]] + [tail[places + j] for j in range(len(lines))]
    return pieces, sums


def sum_groups(values, turn):
    count = lax.axis_size("dp")
    listed = [(j + turn) % count for j in range(count)]
    return lax.psum(tuple(values), "dp", axis_index_groups=[listed])


class GroupSum:
    def __init__(self, arrays):
        self.arrays = [array.astype(BF16) for array in arrays]
        count = lax.axis_size("dp")
        self.bits = count.bit_length() - 1
        place = lax.axis_index("dp")
        self.own = [lax.rem(place // 2**bit, 2) for bit in range(self.bits)]
        self.orders = [list(range(1, self.bits)), list(range(1, self.bits))[::-1]]
        self.plan = [self.first]
        self.plan += [lambda *t, k=k: self.reduce(k, *t) for k in range(self.bits - 1)]
        self.plan += [lambda *t, k=k: self.spread(k, *t) for k in reversed(range(self.bits - 1))]
        self.plan += [self.last]

    def swap(self, values, bit):
        count = lax.axis_size("dp")
        return lax.ppermute(values, "dp", [(j, j ^ (1 << bit)) for j in range(count)])

    def half(self, values, which):
        rows = values.shape[0] // 2
        return lax.dynamic_slice_in_dim(values, which * rows, rows, 0)

    def first(self, *after):
        kept, away = split_rows(self.own[0], self.arrays)
        total = kept + self.swap(tie(away, *after), 0)
        rows = total.shape[0] // 2
        self.parts = [total[:rows], total[rows:]]

    def reduce(self, k, *after):
        for p in range(2):
            bit = self.orders[p][k]
            own = self.own[bit]
            arrived = self.swap(tie(self.half(self.parts[p], 1 - own), *after), bit)
            self.parts[p] = self.half(self.parts[p], own) + arrived

    def both(self, values, arrived, own):
        low = jnp.where(own == 0, values, arrived)
        high = jnp.where(own == 0, arrived, values)
        return jnp.concatenate([low, high], axis=0)

    def spread(self, k, *after):
        for p in range(2):
            bit = self.orders[p][k]
            arrived = self.swap(tie(self.parts[p], *after), bit)
            self.parts[p] = self.both(self.parts[p], arrived, self.own[bit])

    def last(self, *after):
        arrived = [self.swap(tie(part, *after), 0) for part in self.parts]
        widths = [a.shape[1] for a in self.arrays]
        self.parts = finish_rows(self.own[0], self.parts, arrived, widths)

    def step(self, *after):
        self.plan.pop(0)(*after)
        return tuple(self.parts)

    def result(self):
        while self.plan:
            self.step()
        return self.parts


def norm_backward(
    normed_grad, normed, row_values, lines, resid, inverse, gain_part, model_width, carried
):
    place = lax.axis_index("mp").astype(jnp.int32).reshape(1)
    pieces, sums = scatter_sum_rows(normed_grad, normed, row_values, *lines)
    grads = gradient_step(place, pieces, carried, resid, inverse, gain_part, model_width)
    return grads, sums


def row_product(*pairs):
    total = 0.0
    for left, right in pairs:
        total = total + jnp.sum(left.astype(F32) * right.astype(F32), axis=1)
    return total


def per_device(
    tokens,
    seq_lengths,
    gain_first,
    lin_query,
    lin_key,
    lin_value,
    lin_out,
    gain_second,
    win_query,
    win_key,
    win_value,
    win_out,
    gain_third,
    gate_weight,
    up_weight,
    down_weight,
    out_cotangent,
):
    row_count, width = tokens.shape
    count = lax.axis_size("mp")
    model_width = width * count
    rows = row_count // CHUNKS
    order = list(range(CHUNKS))
    offset = lax.axis_index("mp") * width
    places = jnp.arange(row_count, dtype=jnp.int32)
    validity = (places < seq_lengths[0, 0] + seq_lengths[0, 1]).astype(F32)
    valid = [validity[c * rows : (c + 1) * rows, None] for c in order]

    def cut(values):
        return [values[c * rows : (c + 1) * rows] for c in order]

    def join(values):
        return jnp.concatenate(values, axis=0) if len(values) > 1 else values[0]

    def part_of(gain):
        return lax.dynamic_slice_in_dim(gain, offset, width).astype(F32)

    blank = [None] * CHUNKS
    low_one, low_two, low_three = list(blank), list(blank), list(blank)
    low_two_grad, low_one_grad = list(blank), list(blank)
    place = lax.axis_index("mp").astype(jnp.int32).reshape(1)
    token_parts = cut(tokens)
    resid_zero = [t.astype(F32) for t in token_parts]
    cot_shard = [c.astype(F32) * v for c, v in zip(cut(out_cotangent), valid)]

    cot_low = join([c.astype(BF16) for c in cot_shard])
    cot_joined = lax.all_gather(cot_low, "mp", axis=1, tiled=True)
    cot_full = cut(cot_joined)
    n1, r1, lq, lk, lv, lo, lo32, lden, b1, resid_one = [list(blank) for _ in range(10)]
    for c in order:
        part = tie(token_parts[c], r1[c - 1]) if c else token_parts[c]
        n1[c], r1[c] = gather_norm(line_gather(part), gain_first)
        lq[c] = nn(n1[c], lin_query).astype(BF16)
        lk[c] = nn(n1[c], lin_key).astype(BF16)
        lv[c] = nn(n1[c], lin_value).astype(BF16)
        lo[c], lo32[c], lden[c] = linear_forward(
            c,
            seq_lengths,
            lq[c],
            lk[: c + 1],
            lv[: c + 1],
        )
        pieces = scatter_sum(block_product(lo[c], lin_out, count))
        resid_one[c], low_one[c], b1[c], _ = residual_add(place, resid_zero[c], pieces)
    n2, r2, wq, wk, wv, wo, b2, resid_two = [list(blank) for _ in range(8)]
    for c in order:
        n2[c], r2[c] = gather_norm(line_gather(low_one[c]), gain_second)
        wq[c] = nn(n2[c], win_query).astype(BF16)
        wk[c] = nn(n2[c], win_key).astype(BF16)
        wv[c] = nn(n2[c], win_value).astype(BF16)
        before = [wk[c - 1], wv[c - 1]] if c else []
        spans = seq_lengths if c else tie(seq_lengths, cot_joined)
        wo[c] = window_forward(c, spans, wq[c], wk[c], wv[c], before)
        pieces = scatter_sum(block_product(wo[c], win_out, count))
        resid_two[c], low_two[c], b2[c], _ = residual_add(place, resid_one[c], pieces)
    n3, r3, hid, dg, du, b3, resid_three, dn3, resid_two_grad = [list(blank) for _ in range(9)]
    gates, uppers = list(blank), list(blank)
    for c in order:
        n3[c], r3[c] = gather_norm(line_gather(low_two[c]), gain_third)
        gates[c] = nn(n3[c], gate_weight)
        uppers[c] = nn(n3[c], up_weight)
    def masked(values):
        return sum(jnp.sum(v * p) for v, p in zip(valid, values))

    def stat_line(*values):
        block = jnp.pad(jnp.stack(values), (0, width - len(values)))
        return jnp.tile(block, count)

    stats = stat_line(
        masked([jnp.sum(x * x, axis=1, keepdims=True) for x in resid_zero]), masked(b1), masked(b2)
    )
    sums_three, sums_two, sums_one = list(blank), list(blank), list(blank)
    for c in order:
        hid[c] = hidden_forward(gates[c], uppers[c], cot_joined if c else seq_lengths)
    for c in reversed(order):
        hid_grad = nt(cot_full[c], down_weight)
        dg[c], du[c], row_values = hidden_backward(gates[c], uppers[c], hid_grad)
        dn3[c] = nt(dg[c], gate_weight) + nt(du[c], up_weight)
        (resid_two_grad[c], low_two_grad[c]), sums_three[c] = norm_backward(
            dn3[c],
            n3[c],
            row_values[:, 0],
            (stats,),
            resid_two[c],
            r3[c],
            part_of(gain_third),
            model_width,
            cot_shard[c],
        )
    for c in order:
        partial_sum = nn(hid[c], down_weight).astype(BF16)
        branch = lax.psum_scatter(partial_sum, "mp", scatter_dimension=1, tiled=True)
        branch = branch.astype(F32)
        total = resid_two[c] + branch
        low_three[c] = total.astype(BF16)
        b3[c] = jnp.sum(branch * branch, axis=1, keepdims=True)
        resid_three[c] = jnp.sum(total * total, axis=1, keepdims=True)
    ffn_normed, ffn_hid = join(n3), join(hid)
    down_grad = tn(ffn_hid, cot_joined).astype(BF16)
    down_sums = sum_groups([down_grad], 3)
    ffn_grads = [
        tn(ffn_normed, join(dg)).astype(BF16),
        tn(ffn_normed, join(du)).astype(BF16),
    ]
    ffn_sums = sum_groups(ffn_grads, 0)
    cot_two, wdq, wdk, wdv, dn2, resid_one_grad = [list(blank) for _ in range(6)]
    carry = []
    for c in reversed(order):
        shard = tie(low_two_grad[c], *(ffn_grads if c == 0 else [down_grad]))
        cot_two[c] = gather_join(line_gather(shard))
        mixed_grad = nt(cot_two[c], win_out).astype(BF16)
        before = [wk[c - 1], wv[c - 1]] if c else []
        (wdq[c], wdk[c], wdv[c]), carry = window_backward(
            c, seq_lengths, wq[c], wk[c], wv[c], before, mixed_grad, carry
        )
        dn2[c] = nt(wdq[c], win_query) + nt(wdk[c], win_key) + nt(wdv[c], win_value)
        (resid_one_grad[c], low_one_grad[c]), sums_two[c] = norm_backward(
            dn2[c],
            n2[c],
            row_product((wdq[c], wq[c]), (wdk[c], wk[c]), (wdv[c], wv[c])),
            (),
            resid_one[c],
            r2[c],
            part_of(gain_second),
            model_width,
            resid_two_grad[c],
        )
    win_normed = join(n2)
    win_grads = [
        tn(win_normed, join(wdq)).astype(BF16),
        tn(win_normed, join(wdk)).astype(BF16),
        tn(win_normed, join(wdv)).astype(BF16),
        tn(join(wo), join(cot_two)).astype(BF16),
    ]
    win_sums = sum_groups(win_grads, 1)
    cot_one, ldq, ldk, ldv, dn1, tokens_grad = [list(blank) for _ in range(6)]
    pending = [[] for _ in order]
    for c in reversed(order):
        shard = low_one_grad[c] if c else tie(low_one_grad[c], *win_grads)
        cot_one[c] = gather_join(line_gather(shard))
        mixed_grad = nt(cot_one[c], lin_out)
        carry = []
        if pending[c]:
            carry = [functools.reduce(jnp.add, [p[s] for p in pending[c]]) for s in (0, 1)]
        (ldq[c], ldk[c], ldv[c]), back = linear_backward(
            c,
            seq_lengths,
            lq[c],
            lk[: c + 1],
            lv[: c + 1],
            mixed_grad,
            lo32[c],
            lden[c],
            carry,
        )
        for earlier, pair in enumerate(back):
            pending[earlier].append(pair)
        dn1[c] = nt(ldq[c], lin_query) + nt(ldk[c], lin_key) + nt(ldv[c], lin_value)
        stats = stat_line(masked(b3), masked(resid_three))
        (tokens_grad[c], _), sums_one[c] = norm_backward(
            dn1[c],
            n1[c],
            row_product((ldq[c], lq[c]), (ldk[c], lk[c]), (ldv[c], lv[c])),
            () if c else (stats,),
            resid_zero[c],
            r1[c],
            part_of(gain_first),
            model_width,
            resid_one_grad[c],
        )
    lin_normed = join(n1)
    lin_grads = [
        tn(lin_normed, join(ldq)).astype(BF16),
        tn(lin_normed, join(ldk)).astype(BF16),
        tn(lin_normed, join(ldv)).astype(BF16),
        tn(join(lo), join(cot_one)).astype(BF16),
    ]
    lin_sums = sum_groups(lin_grads, 2)
    small = lax.psum(
        jnp.concatenate(
            [sum(part[0] for part in sums) for sums in (sums_one, sums_two, sums_three)]
            + [sums_three[0][1][:3], sums_one[0][1][:2], jnp.sum(validity)[None]]
        ),
        "dp",
    )
    gain_grads = [
        small[s * width : (s + 1) * width] / part_of(gain)
        for s, gain in enumerate((gain_first, gain_second, gain_third))
    ]
    rms_values = jnp.sqrt(small[3 * width : -1] / (small[-1] * model_width))
    down_sums = [tie(v.astype(F32), wdq[0]) for v in down_sums]
    ffn_sums = [tie(v.astype(F32), ldq[0]) for v in ffn_sums]
    win_sums = [tie(v.astype(F32), tokens_grad[0]) for v in win_sums]
    lin_sums = [v.astype(F32) for v in lin_sums]
    return (
        join(low_three),
        join(tokens_grad),
        gain_grads[0],
        lin_sums[0],
        lin_sums[1],
        lin_sums[2],
        lin_sums[3],
        gain_grads[1],
        win_sums[0],
        win_sums[1],
        win_sums[2],
        win_sums[3],
        gain_grads[2],
        ffn_sums[0],
        ffn_sums[1],
        down_sums[0],
        rms_values,
    )


def solution(mesh):
    in_specs = (
        P("dp", "mp"),
        P("dp", None),
        P(),
        P(None, "mp"),
        P(None, "mp"),
        P(None, "mp"),
        P("mp", None),
        P(),
        P(None, "mp"),
        P(None, "mp"),
        P(None, "mp"),
        P("mp", None),
        P(),
        P(None, "mp"),
        P(None, "mp"),
        P("mp", None),
        P("dp", "mp"),
    )
    out_specs = (
        P("dp", "mp"),
        P("dp", "mp"),
        P("mp"),
        P(None, "mp"),
        P(None, "mp"),
        P(None, "mp"),
        P("mp", None),
        P("mp"),
        P(None, "mp"),
        P(None, "mp"),
        P(None, "mp"),
        P("mp", None),
        P("mp"),
        P(None, "mp"),
        P(None, "mp"),
        P("mp", None),
        P(),
    )
    return jax.shard_map(
        per_device, mesh=mesh, in_specs=in_specs, out_specs=out_specs, check_vma=False
    )
```

```python
import functools

import jax
import jax.numpy as jnp
from jax import lax
from jax.experimental import pallas as pl
from jax.experimental.pallas import tpu as pltpu
from jax.sharding import PartitionSpec as P

FEATURE_SIZE = 16
HEAD_DIM = 128
WINDOW = 64
EPSILON = 1e-05
NEGATIVE = -1e30
CHUNKS = 2
LIN_SCALE = FEATURE_SIZE ** (-0.5)
WIN_SCALE = HEAD_DIM ** (-0.5)
F32 = jnp.float32
BF16 = jnp.bfloat16
PAD_ROWS = 16
VMEM_LIMIT = 40 * 1024 * 1024


def nn(left, right):
    return lax.dot_general(left, right, (((1,), (0,)), ((), ())), preferred_element_type=F32)


def nt(left, right):
    return lax.dot_general(left, right, (((1,), (1,)), ((), ())), preferred_element_type=F32)


def tn(left, right):
    return lax.dot_general(left, right, (((0,), (0,)), ((), ())), preferred_element_type=F32)


def segment_start(lens_ref, place):
    first_end = lens_ref[0, 0]
    second_end = first_end + lens_ref[0, 1]
    return jnp.where(place < first_end, 0, jnp.where(place < second_end, first_end, second_end))


def causal_allowed(lens_ref, row_begin, key_begin, rows, keys, window):
    place = row_begin + lax.broadcasted_iota(jnp.int32, (rows, 1), 0)
    key_place = key_begin + lax.broadcasted_iota(jnp.int32, (rows, keys), 1)
    lowest = segment_start(lens_ref, place)
    if window:
        lowest = jnp.maximum(lowest, place - (window - 1))
    allowed = key_place >= lowest
    if key_begin + keys > row_begin:
        allowed = allowed & (key_place <= place)
    return allowed


def head_lanes(values, head):
    lane = lax.broadcasted_iota(jnp.int32, values.shape, 1) // FEATURE_SIZE
    return jnp.where(lane == head, values, jnp.zeros_like(values))


def linear_tile(lens_ref, query, key, row_begin, key_begin):
    logits = nt(query, key) * LIN_SCALE
    allowed = causal_allowed(lens_ref, row_begin, key_begin, query.shape[0], key.shape[0], 0)
    kernel = jnp.where(allowed, 1.0 + logits + 0.5 * logits * logits, 0.0)
    return logits, allowed, kernel


def linear_forward_kernel(chunk, rows, tile, lens_ref, q_ref, *refs):
    count = chunk + 1
    k_refs, v_refs = refs[:count], refs[count : 2 * count]
    low_ref, mixed_ref, total_ref = refs[2 * count :]
    head = pl.program_id(0)
    per = rows // tile
    for i in range(per):
        row_begin = chunk * rows + i * tile
        query = q_ref[pl.ds(i * tile, tile), :]
        total = jnp.zeros((tile, 1), F32)
        number = jnp.zeros((tile, HEAD_DIM), F32)
        for j in range(chunk * per + i + 1):
            span = pl.ds((j % per) * tile, tile)
            key = head_lanes(k_refs[j // per][span, :], head)
            _, _, kernel = linear_tile(lens_ref, query, key, row_begin, j * tile)
            total += jnp.sum(kernel, axis=1, keepdims=True)
            number += nn(kernel.astype(BF16), v_refs[j // per][span, :])
        mixed = number / total
        low_ref[pl.ds(i * tile, tile), :] = mixed.astype(BF16)
        mixed_ref[pl.ds(i * tile, tile), :] = mixed
        total_ref[0, pl.ds(i * tile, tile), :] = total


def linear_backward_kernel(chunk, rows, tile, carried, lens_ref, q_ref, *refs):
    count = chunk + 1
    k_refs, v_refs = refs[:count], refs[count : 2 * count]
    do_ref, mixed_ref, total_ref = refs[2 * count : 2 * count + 3]
    refs = refs[2 * count + 3 :]
    if carried:
        dk_in, dv_in = refs[:2]
        refs = refs[2:]
    dq_out, dk_out, dv_out = refs[:3]
    dk_prev, dv_prev = refs[3 : 3 + chunk], refs[3 + chunk : 3 + 2 * chunk]
    dq_acc, dk_acc, dv_acc = refs[3 + 2 * chunk :]
    head = pl.program_id(0)
    last = pl.num_programs(0) - 1
    per = rows // tile

    @pl.when(head == 0)
    def _():
        dq_acc[...] = jnp.zeros_like(dq_acc)
        dk_acc[...] = jnp.zeros_like(dk_acc)
        if carried:
            dk_acc[pl.ds(chunk * rows, rows), :] = dk_in[...]

    dv_acc[...] = jnp.zeros_like(dv_acc)
    if carried:
        dv_acc[pl.ds(chunk * rows, rows), :] = dv_in[...]
    for i in range(per):
        row_begin = chunk * rows + i * tile
        own = pl.ds(i * tile, tile)
        query = head_lanes(q_ref[own, :], head)
        grad = do_ref[own, :]
        inverse = 1.0 / total_ref[0, own, :]
        number_grad = (grad * inverse).astype(BF16)
        total_grad = -jnp.sum(grad * mixed_ref[own, :], axis=1, keepdims=True) * inverse
        dq = jnp.zeros((tile, q_ref.shape[1]), F32)
        for j in range(chunk * per + i + 1):
            span = pl.ds((j % per) * tile, tile)
            key = head_lanes(k_refs[j // per][span, :], head)
            logits, allowed, kernel = linear_tile(lens_ref, query, key, row_begin, j * tile)
            kernel_grad = nt(number_grad, v_refs[j // per][span, :]) + total_grad
            scores_grad = jnp.where(allowed, kernel_grad * (1.0 + logits), 0.0).astype(BF16)
            dq += nn(scores_grad, key)
            keys = pl.ds(j * tile, tile)
            dk_acc[keys, :] += tn(scores_grad, query) * LIN_SCALE
            dv_acc[keys, :] += tn(kernel.astype(BF16), number_grad)
        dq_acc[own, :] += dq * LIN_SCALE
    dv_out[...] = dv_acc[pl.ds(chunk * rows, rows), :].astype(BF16)
    for c in range(chunk):
        dv_prev[c][...] = dv_acc[pl.ds(c * rows, rows), :]

    @pl.when(head == last)
    def _():
        dq_out[...] = dq_acc[...].astype(BF16)
        dk_out[...] = dk_acc[pl.ds(chunk * rows, rows), :].astype(BF16)
        for c in range(chunk):
            dk_prev[c][...] = dk_acc[pl.ds(c * rows, rows), :]


def window_tile(lens_ref, query, key, row_begin, key_begin):
    logits = nt(query, key) * WIN_SCALE
    allowed = causal_allowed(lens_ref, row_begin, key_begin, query.shape[0], key.shape[0], WINDOW)
    logits = jnp.where(allowed, logits, NEGATIVE)
    exponent = jnp.exp(logits - jnp.max(logits, axis=1, keepdims=True))
    return exponent / jnp.sum(exponent, axis=1, keepdims=True)


def window_keys(current_ref, prev_ref, i, tile):
    if i > 0:
        return current_ref[pl.ds(i * tile - WINDOW, tile + WINDOW), :], i * tile - WINDOW
    if prev_ref is not None:
        return jnp.concatenate([prev_ref[...], current_ref[pl.ds(0, tile), :]], axis=0), -WINDOW
    return current_ref[pl.ds(0, tile), :], 0


def window_forward_kernel(chunk, rows, tile, lens_ref, q_ref, k_ref, v_ref, *refs):
    k_prev, v_prev = refs[:2] if chunk else (None, None)
    out_ref = refs[-1]
    for i in range(rows // tile):
        own = pl.ds(i * tile, tile)
        key, key_begin = window_keys(k_ref, k_prev, i, tile)
        value, _ = window_keys(v_ref, v_prev, i, tile)
        base = chunk * rows
        weights = window_tile(lens_ref, q_ref[own, :], key, base + i * tile, base + key_begin)
        out_ref[own, :] = nn(weights.astype(BF16), value).astype(BF16)


def window_backward_kernel(chunk, rows, tile, carried, lens_ref, q_ref, k_ref, v_ref, *refs):
    k_prev, v_prev = refs[:2] if chunk else (None, None)
    refs = refs[2:] if chunk else refs
    do_ref, refs = refs[0], refs[1:]
    if carried:
        dk_in, dv_in = refs[:2]
        refs = refs[2:]
    dq_out, dk_out, dv_out = refs[:3]
    dk_back, dv_back = refs[3:5] if chunk else (None, None)
    dk_acc, dv_acc = refs[-2:]
    dk_acc[...] = jnp.zeros_like(dk_acc)
    dv_acc[...] = jnp.zeros_like(dv_acc)
    if carried:
        dk_acc[pl.ds(rows, WINDOW), :] = dk_in[...]
        dv_acc[pl.ds(rows, WINDOW), :] = dv_in[...]
    for i in range(rows // tile):
        own = pl.ds(i * tile, tile)
        key, key_begin = window_keys(k_ref, k_prev, i, tile)
        value, _ = window_keys(v_ref, v_prev, i, tile)
        base = chunk * rows
        query = q_ref[own, :]
        grad = do_ref[own, :]
        weights = window_tile(lens_ref, query, key, base + i * tile, base + key_begin)
        weight_grad = nt(grad, value)
        delta = jnp.sum(weights * weight_grad, axis=1, keepdims=True)
        scores_grad = (weights * (weight_grad - delta)).astype(BF16)
        dq_out[own, :] = (nn(scores_grad, key) * WIN_SCALE).astype(BF16)
        keys = pl.ds(WINDOW + key_begin, key.shape[0])
        dk_acc[keys, :] += tn(scores_grad, query) * WIN_SCALE
        dv_acc[keys, :] += tn(weights.astype(BF16), grad)
    dk_out[...] = dk_acc[pl.ds(WINDOW, rows), :].astype(BF16)
    dv_out[...] = dv_acc[pl.ds(WINDOW, rows), :].astype(BF16)
    if chunk:
        dk_back[...] = dk_acc[pl.ds(0, WINDOW), :]
        dv_back[...] = dv_acc[pl.ds(0, WINDOW), :]


SMEM_SPEC = pl.BlockSpec(memory_space=pltpu.SMEM)
PARAMS = pltpu.CompilerParams(
    dimension_semantics=("arbitrary",), vmem_limit_bytes=VMEM_LIMIT
)


def cost(flops, moved):
    return pl.CostEstimate(flops=flops, bytes_accessed=moved, transcendentals=0)


def narrow_spec(rows, width):
    return pl.BlockSpec((rows, width), lambda h: (0, 0))


def head_spec(rows):
    return pl.BlockSpec((rows, HEAD_DIM), lambda h: (0, h))


def total_spec(rows):
    return pl.BlockSpec((1, rows, 1), lambda h: (h, 0, 0))


def linear_forward(chunk, lengths, query, keys, values):
    rows, width = query.shape
    heads = width // FEATURE_SIZE
    tile = min(256, rows)
    count = chunk + 1
    wide = heads * HEAD_DIM
    return pl.pallas_call(
        functools.partial(linear_forward_kernel, chunk, rows, tile),
        grid=(heads,),
        in_specs=[SMEM_SPEC, narrow_spec(rows, width)]
        + [narrow_spec(rows, width)] * count
        + [head_spec(rows)] * count,
        out_specs=[head_spec(rows), head_spec(rows), total_spec(rows)],
        out_shape=[
            jax.ShapeDtypeStruct((rows, wide), BF16),
            jax.ShapeDtypeStruct((rows, wide), F32),
            jax.ShapeDtypeStruct((heads, rows, 1), F32),
        ],
        compiler_params=PARAMS,
        cost_estimate=cost(4 * heads * rows * rows * count * HEAD_DIM, 8 * rows * wide),
        name="linear_forward",
    )(lengths, query, *keys, *values)


def linear_backward(chunk, lengths, query, keys, values, grad, mixed, total, carry):
    rows, width = query.shape
    heads = width // FEATURE_SIZE
    tile = min(512, rows)
    count = chunk + 1
    wide = heads * HEAD_DIM
    carry = list(carry)
    outs = pl.pallas_call(
        functools.partial(linear_backward_kernel, chunk, rows, tile, bool(carry)),
        grid=(heads,),
        in_specs=[SMEM_SPEC, narrow_spec(rows, width)]
        + [narrow_spec(rows, width)] * count
        + [head_spec(rows)] * count
        + [head_spec(rows), head_spec(rows), total_spec(rows)]
        + ([narrow_spec(rows, width), head_spec(rows)] if carry else []),
        out_specs=[narrow_spec(rows, width), narrow_spec(rows, width), head_spec(rows)]
        + [narrow_spec(rows, width)] * chunk
        + [head_spec(rows)] * chunk,
        out_shape=[
            jax.ShapeDtypeStruct((rows, width), BF16),
            jax.ShapeDtypeStruct((rows, width), BF16),
            jax.ShapeDtypeStruct((rows, wide), BF16),
        ]
        + [jax.ShapeDtypeStruct((rows, width), F32)] * chunk
        + [jax.ShapeDtypeStruct((rows, wide), F32)] * chunk,
        scratch_shapes=[
            pltpu.VMEM((rows, width), F32),
            pltpu.VMEM((count * rows, width), F32),
            pltpu.VMEM((count * rows, HEAD_DIM), F32),
        ],
        compiler_params=PARAMS,
        cost_estimate=cost(10 * heads * rows * rows * count * HEAD_DIM, 16 * rows * wide),
        name="linear_backward",
    )(lengths, query, *keys, *values, grad, mixed, total, *carry)
    return outs[:3], list(zip(outs[3 : 3 + chunk], outs[3 + chunk :]))


def prev_spec(rows):
    return pl.BlockSpec((WINDOW, HEAD_DIM), lambda h: (rows // WINDOW - 1, h))


def edge_spec():
    return pl.BlockSpec((WINDOW, HEAD_DIM), lambda h: (0, h))


def window_forward(chunk, lengths, query, key, value, before):
    rows, wide = query.shape
    heads = wide // HEAD_DIM
    tile = min(256, rows)
    return pl.pallas_call(
        functools.partial(window_forward_kernel, chunk, rows, tile),
        grid=(heads,),
        in_specs=[SMEM_SPEC] + [head_spec(rows)] * 3 + [prev_spec(rows)] * len(before),
        out_specs=head_spec(rows),
        out_shape=jax.ShapeDtypeStruct((rows, wide), BF16),
        compiler_params=PARAMS,
        cost_estimate=cost(4 * rows * 4 * HEAD_DIM * wide, 8 * rows * wide),
        name="window_forward",
    )(lengths, query, key, value, *before)


def window_backward(chunk, lengths, query, key, value, before, grad, carry):
    rows, wide = query.shape
    heads = wide // HEAD_DIM
    tile = min(256, rows)
    carry = list(carry)
    edges = 2 if chunk else 0
    outs = pl.pallas_call(
        functools.partial(window_backward_kernel, chunk, rows, tile, bool(carry)),
        grid=(heads,),
        in_specs=[SMEM_SPEC]
        + [head_spec(rows)] * 3
        + [prev_spec(rows)] * len(before)
        + [head_spec(rows)]
        + [edge_spec()] * len(carry),
        out_specs=[head_spec(rows)] * 3 + [edge_spec()] * edges,
        out_shape=[jax.ShapeDtypeStruct((rows, wide), BF16)] * 3
        + [jax.ShapeDtypeStruct((WINDOW, wide), F32)] * edges,
        scratch_shapes=[pltpu.VMEM((WINDOW + rows, HEAD_DIM), F32)] * 2,
        compiler_params=PARAMS,
        cost_estimate=cost(10 * rows * 4 * HEAD_DIM * wide, 16 * rows * wide),
        name="window_backward",
    )(lengths, query, key, value, *before, grad, *carry)
    return outs[:3], outs[3:]


def gather_norm_kernel(count, width, place_ref, own_ref, *refs):
    right, left = refs[: count - 1], refs[count - 1 : 2 * count - 2]
    gain_ref, normed_ref, inverse_ref, held = refs[2 * count - 2 :]
    place = place_ref[0]
    squares = jnp.zeros((own_ref.shape[0], 1), F32)
    for k in range(count):
        if k == 0:
            piece = own_ref[...].astype(F32)
        else:
            piece = jnp.where(place >= k, right[k - 1][...], left[count - k - 1][...]).astype(F32)
        held[k] = piece
        squares += jnp.sum(piece * piece, axis=1, keepdims=True)
    inverse = lax.rsqrt(squares * (1.0 / (count * width)) + EPSILON)
    inverse_ref[...] = inverse
    for k in range(count):
        block = lax.rem(place - k + count, count)
        columns = pl.ds(pl.multiple_of(block * width, width), width)
        gain = gain_ref[:, columns].astype(F32)
        normed_ref[:, columns] = (held[k] * inverse * gain).astype(BF16)


def gather_norm(pieces, gain_vector):
    own, right, left = pieces
    rows, width = own.shape
    count = len(right) + 1
    tile = min(256, rows)
    place = lax.axis_index("mp").astype(jnp.int32).reshape(1)
    piece_spec = pl.BlockSpec((tile, width), lambda t: (t, 0))
    return pl.pallas_call(
        functools.partial(gather_norm_kernel, count, width),
        grid=(rows // tile,),
        in_specs=[SMEM_SPEC]
        + [piece_spec] * (2 * count - 1)
        + [pl.BlockSpec((1, count * width), lambda t: (0, 0))],
        out_specs=[
            pl.BlockSpec((tile, count * width), lambda t: (t, 0)),
            pl.BlockSpec((tile, 1), lambda t: (t, 0)),
        ],
        out_shape=[
            jax.ShapeDtypeStruct((rows, count * width), BF16),
            jax.ShapeDtypeStruct((rows, 1), F32),
        ],
        scratch_shapes=[pltpu.VMEM((count, tile, width), F32)],
        compiler_params=PARAMS,
        cost_estimate=cost(8 * rows * width * count, 6 * rows * width * count),
        name="gather_norm",
    )(place, own, *right, *left, gain_vector.reshape(1, -1))


def gather_join_kernel(count, width, place_ref, own_ref, *refs):
    right, left = refs[: count - 1], refs[count - 1 : 2 * count - 2]
    out_ref = refs[-1]
    place = place_ref[0]
    for k in range(count):
        if k == 0:
            piece = own_ref[...]
        else:
            piece = jnp.where(place >= k, right[k - 1][...], left[count - k - 1][...])
        block = lax.rem(place - k + count, count)
        out_ref[:, pl.ds(pl.multiple_of(block * width, width), width)] = piece


def gather_join(pieces):
    own, right, left = pieces
    rows, width = own.shape
    count = len(right) + 1
    tile = min(256, rows)
    place = lax.axis_index("mp").astype(jnp.int32).reshape(1)
    piece_spec = pl.BlockSpec((tile, width), lambda t: (t, 0))
    return pl.pallas_call(
        functools.partial(gather_join_kernel, count, width),
        grid=(rows // tile,),
        in_specs=[SMEM_SPEC] + [piece_spec] * (2 * count - 1),
        out_specs=pl.BlockSpec((tile, count * width), lambda t: (t, 0)),
        out_shape=jax.ShapeDtypeStruct((rows, count * width), BF16),
        compiler_params=PARAMS,
        cost_estimate=cost(rows * width * count, 6 * rows * width * count),
        name="gather_join",
    )(place, own, *right, *left)


def hidden_kernel(gate_ref, upper_ref, after_ref, hidden_ref):
    gate = gate_ref[...]
    hidden_ref[...] = (gate * jax.nn.sigmoid(gate) * upper_ref[...]).astype(BF16)


def hidden_backward_kernel(gate_ref, upper_ref, grad_ref, dg_ref, du_ref, row_ref):
    gate, upper, grad = gate_ref[...], upper_ref[...], grad_ref[...]
    sigma = jax.nn.sigmoid(gate)
    gate_grad = (grad * upper * sigma * (1.0 + gate * (1.0 - sigma))).astype(BF16)
    upper_grad = (grad * gate * sigma).astype(BF16)
    dg_ref[...] = gate_grad
    du_ref[...] = upper_grad
    row_ref[...] = jnp.sum(
        gate_grad.astype(F32) * gate + upper_grad.astype(F32) * upper, axis=1, keepdims=True
    )


def row_tiles(rows, most):
    return max(t for t in range(16, most + 1, 16) if rows % t == 0)


def hidden_forward(gate, upper, after):
    rows, width = gate.shape
    tile = row_tiles(rows, 256)
    spec = pl.BlockSpec((tile, width), lambda t: (t, 0))
    return pl.pallas_call(
        hidden_kernel,
        grid=(rows // tile,),
        in_specs=[spec, spec, pl.BlockSpec(memory_space=pl.ANY)],
        out_specs=spec,
        out_shape=jax.ShapeDtypeStruct((rows, width), BF16),
        compiler_params=PARAMS,
        cost_estimate=cost(8 * rows * width, 10 * rows * width),
        name="hidden_forward",
    )(gate, upper, after)


def hidden_backward(gate, upper, grad):
    rows, width = gate.shape
    tile = row_tiles(rows, 256)
    spec = pl.BlockSpec((tile, width), lambda t: (t, 0))
    return pl.pallas_call(
        hidden_backward_kernel,
        grid=(rows // tile,),
        in_specs=[spec] * 3,
        out_specs=[spec, spec, pl.BlockSpec((tile, 1), lambda t: (t, 0))],
        out_shape=[jax.ShapeDtypeStruct((rows, width), BF16)] * 2
        + [jax.ShapeDtypeStruct((rows, 1), F32)],
        compiler_params=PARAMS,
        cost_estimate=cost(20 * rows * width, 16 * rows * width),
        name="hidden_backward",
    )(gate, upper, grad)


def pack_kernel(count, tile, grad_ref, normed_ref, extra_ref, out_ref, sum_ref):
    step = pl.program_id(0)
    rows = out_ref.shape[1] - PAD_ROWS
    width = out_ref.shape[2]
    grad = grad_ref[...]

    @pl.when(step == 0)
    def _():
        sum_ref[...] = jnp.zeros_like(sum_ref)

    sum_ref[...] += jnp.sum(grad * normed_ref[...].astype(F32), axis=0, keepdims=True)
    own = pl.ds(pl.multiple_of(step * tile, tile), tile)
    for j in range(count):
        out_ref[j, own, :] = grad[:, j * width : (j + 1) * width].astype(BF16)

    @pl.when(step == pl.num_programs(0) - 1)
    def _():
        line = lax.broadcasted_iota(jnp.int32, extra_ref.shape, 0)
        last = jnp.where(line == PAD_ROWS - 1, sum_ref[...], extra_ref[...]).astype(BF16)
        for j in range(count):
            out_ref[j, pl.ds(rows, PAD_ROWS), :] = last[:, j * width : (j + 1) * width]


def pack_rows(grad, normed, extra, count):
    rows, width = grad.shape
    tile = row_tiles(rows, 256)
    shape = (count, rows + PAD_ROWS, width // count)
    return pl.pallas_call(
        functools.partial(pack_kernel, count, tile),
        grid=(rows // tile,),
        in_specs=[
            pl.BlockSpec((tile, width), lambda t: (t, 0)),
            pl.BlockSpec((tile, width), lambda t: (t, 0)),
            pl.BlockSpec((PAD_ROWS, width), lambda t: (0, 0)),
        ],
        out_specs=pl.BlockSpec(shape, lambda t: (0, 0, 0)),
        out_shape=jax.ShapeDtypeStruct(shape, BF16),
        scratch_shapes=[pltpu.VMEM((1, width), F32)],
        compiler_params=PARAMS,
        cost_estimate=cost(4 * rows * width, 8 * rows * width),
        name="pack_rows",
    )(grad, normed, extra)


def block_product_kernel(left_ref, right_ref, out_ref):
    out_ref[0] = nn(left_ref[...], right_ref[...]).astype(BF16)


def block_product(left, right, count):
    rows, depth = left.shape
    width = right.shape[1] // count
    return pl.pallas_call(
        block_product_kernel,
        grid=(count,),
        in_specs=[
            pl.BlockSpec((rows, depth), lambda j: (0, 0)),
            pl.BlockSpec((depth, width), lambda j: (0, j)),
        ],
        out_specs=pl.BlockSpec((1, rows, width), lambda j: (j, 0, 0)),
        out_shape=jax.ShapeDtypeStruct((count, rows, width), BF16),
        compiler_params=PARAMS,
        cost_estimate=cost(2 * rows * depth * width * count, 2 * depth * width * count),
        name="block_product",
    )(left, right)


def residual_kernel(place_ref, resid_ref, own_ref, right_ref, left_ref, *outs):
    next_ref, low_ref, branch_ref, square_ref = outs
    branch = own_ref[0].astype(F32) + right_ref[...].astype(F32) + left_ref[...].astype(F32)
    total = resid_ref[...] + branch
    next_ref[...] = total
    low_ref[...] = total.astype(BF16)
    branch_ref[...] = jnp.sum(branch * branch, axis=1, keepdims=True)
    square_ref[...] = jnp.sum(total * total, axis=1, keepdims=True)


def residual_add(place, resid, pieces):
    blocks, right, left = pieces
    rows, width = resid.shape
    tile = row_tiles(rows, 256)
    spec = pl.BlockSpec((tile, width), lambda t, p: (t, 0))
    column = pl.BlockSpec((tile, 1), lambda t, p: (t, 0))
    return pl.pallas_call(
        residual_kernel,
        grid_spec=pltpu.PrefetchScalarGridSpec(
            num_scalar_prefetch=1,
            grid=(rows // tile,),
            in_specs=[
                spec,
                pl.BlockSpec((1, tile, width), lambda t, p: (p[0], t, 0)),
                spec,
                spec,
            ],
            out_specs=[spec, spec, column, column],
        ),
        out_shape=[
            jax.ShapeDtypeStruct((rows, width), F32),
            jax.ShapeDtypeStruct((rows, width), BF16),
            jax.ShapeDtypeStruct((rows, 1), F32),
            jax.ShapeDtypeStruct((rows, 1), F32),
        ],
        compiler_params=PARAMS,
        cost_estimate=cost(8 * rows * width, 16 * rows * width),
        name="residual_add",
    )(place, resid, blocks, right, left)


def gradient_kernel(rows, model_width, place_ref, *refs):
    own_ref, right_ref, left_ref, carried_ref, resid_ref, inverse_ref, gain_ref = refs[:7]
    next_ref, low_ref = refs[7:]
    width = gain_ref.shape[1]
    tile = row_tiles(rows, 128)
    extra = pl.ds(rows, PAD_ROWS)
    dots = own_ref[0, extra, :].astype(F32)
    dots = dots + right_ref[extra, :].astype(F32) + left_ref[extra, :].astype(F32)
    square = lax.broadcasted_iota(jnp.int32, (tile, tile), 0) == lax.broadcasted_iota(
        jnp.int32, (tile, tile), 1
    )
    for step in range(rows // tile):
        span = pl.ds(step * tile, tile)
        line, begin = divmod(step * tile, width)
        row = dots[line : line + 1, begin : begin + tile]
        dot = jnp.sum(jnp.where(square, row, 0.0), axis=1, keepdims=True)
        shard = own_ref[0, span, :].astype(F32)
        shard = shard + right_ref[span, :].astype(F32) + left_ref[span, :].astype(F32)
        inverse = inverse_ref[span, :]
        normed = resid_ref[span, :] * inverse
        grad = carried_ref[span, :] + inverse * (
            shard * gain_ref[...] - normed * (dot * (1.0 / model_width))
        )
        next_ref[span, :] = grad
        low_ref[span, :] = grad.astype(BF16)


def gradient_step(place, pieces, carried, resid, inverse, gain_part, model_width):
    blocks, right, left = pieces
    rows, width = resid.shape
    whole = lambda shape: pl.BlockSpec(shape, lambda t, p: (0,) * len(shape))
    return pl.pallas_call(
        functools.partial(gradient_kernel, rows, model_width),
        grid_spec=pltpu.PrefetchScalarGridSpec(
            num_scalar_prefetch=1,
            grid=(1,),
            in_specs=[
                pl.BlockSpec((1, rows + PAD_ROWS, width), lambda t, p: (p[0], 0, 0)),
                whole(right.shape),
                whole(left.shape),
                whole(carried.shape),
                whole(resid.shape),
                whole(inverse.shape),
                whole((1, width)),
            ],
            out_specs=[whole(resid.shape), whole(resid.shape)],
        ),
        out_shape=[
            jax.ShapeDtypeStruct((rows, width), F32),
            jax.ShapeDtypeStruct((rows, width), BF16),
        ],
        compiler_params=PARAMS,
        cost_estimate=cost(10 * rows * width, 20 * rows * width),
        name="gradient_step",
    )(place, blocks, right, left, carried, resid, inverse, gain_part.reshape(1, width))


def split_kernel(widths, own_ref, *refs):
    count = len(widths)
    kept_ref, away_ref = refs[2 * count :]
    begin = 0
    for j, width in enumerate(widths):
        kept_ref[:, begin : begin + width] = refs[j][...]
        away_ref[:, begin : begin + width] = refs[count + j][...]
        begin += width


def split_rows(own, arrays):
    rows = arrays[0].shape[0] // 2
    widths = [a.shape[1] for a in arrays]
    tile = row_tiles(rows, 256)
    steps = rows // tile
    kept = [pl.BlockSpec((tile, w), lambda t, o: (o[0] * steps + t, 0)) for w in widths]
    away = [pl.BlockSpec((tile, w), lambda t, o: ((1 - o[0]) * steps + t, 0)) for w in widths]
    spec = pl.BlockSpec((tile, sum(widths)), lambda t, o: (t, 0))
    return pl.pallas_call(
        functools.partial(split_kernel, widths),
        grid_spec=pltpu.PrefetchScalarGridSpec(
            num_scalar_prefetch=1,
            grid=(steps,),
            in_specs=kept + away,
            out_specs=[spec, spec],
        ),
        out_shape=[jax.ShapeDtypeStruct((rows, sum(widths)), BF16)] * 2,
        compiler_params=PARAMS,
        cost_estimate=cost(rows * sum(widths), 8 * rows * sum(widths)),
        name="split_rows",
    )(own.reshape(1), *arrays, *arrays)


def finish_kernel(widths, steps, own_ref, *refs):
    sources, outs = refs[:4], refs[4:]
    step = pl.program_id(0)
    for kind in range(2):
        for part in range(2):
            half = own_ref[0] if kind == 0 else 1 - own_ref[0]
            begin = (half * 2 + part) * steps

            @pl.when((step >= begin) & (step < begin + steps))
            def _(source=sources[2 * kind + part]):
                first = 0
                for out, width in zip(outs, widths):
                    out[...] = source[:, first : first + width].astype(F32)
                    first += width


def finish_rows(own, held, arrived, widths):
    rows = held[0].shape[0]
    tile = row_tiles(rows, 128)
    steps = rows // tile

    def place(kind, part):
        def index(t, o):
            half = o[0] if kind == 0 else 1 - o[0]
            return (jnp.clip(t - (half * 2 + part) * steps, 0, steps - 1), 0)

        return index

    specs = [
        pl.BlockSpec((tile, sum(widths)), place(kind, part))
        for kind in range(2)
        for part in range(2)
    ]
    return pl.pallas_call(
        functools.partial(finish_kernel, widths, steps),
        grid_spec=pltpu.PrefetchScalarGridSpec(
            num_scalar_prefetch=1,
            grid=(4 * steps,),
            in_specs=specs,
            out_specs=[pl.BlockSpec((tile, w), lambda t, o: (t, 0)) for w in widths],
        ),
        out_shape=[jax.ShapeDtypeStruct((4 * rows, w), F32) for w in widths],
        compiler_params=PARAMS,
        cost_estimate=cost(rows * sum(widths), 24 * rows * sum(widths)),
        name="finish_rows",
    )(own.reshape(1), *held, *arrived)


def line_gather(part):
    count = lax.axis_size("mp")
    right, left = [part], [part]
    for k in range(1, count):
        right.append(
            lax.ppermute(right[-1], "mp", [(j, j + 1) for j in range(k - 1, count - 1)])
        )
        left.append(lax.ppermute(left[-1], "mp", [(j, j - 1) for j in range(1, count - k + 1)]))
    return part, right[1:], left[1:]


def tie(value, *others):
    if not others:
        return value
    zero = sum(other[(0,) * other.ndim].astype(F32) * 0.0 for other in others)
    return value + zero.astype(value.dtype)


def block_at(blocks, index):
    count = blocks.shape[0]
    return lax.dynamic_index_in_dim(blocks, lax.rem(index + count, count), 0, keepdims=False)


def scatter_sum(blocks):
    count = lax.axis_size("mp")
    place = lax.axis_index("mp")
    right = left = None
    for k in range(1, count):
        to_right, to_left = block_at(blocks, place - k), block_at(blocks, place + k)
        if right is not None:
            to_right, to_left = to_right + right, to_left + left
        right = lax.ppermute(to_right, "mp", [(j, j + 1) for j in range(k)])
        left = lax.ppermute(to_left, "mp", [(j, j - 1) for j in range(count - k, count)])
    return blocks, right, left


def scatter_sum_rows(partial_value, normed, row_values, *lines):
    rows, model_width = partial_value.shape
    count = lax.axis_size("mp")
    width = model_width // count
    places = rows // width
    extra = jnp.tile(row_values.reshape(places, width), (1, count))
    extra = jnp.concatenate([extra] + [line[None] for line in lines], axis=0)
    extra = jnp.pad(extra, ((0, PAD_ROWS - extra.shape[0]), (0, 0)))
    pieces = scatter_sum(pack_rows(partial_value, normed, extra, count))
    tails = [block_at(pieces[0], lax.axis_index("mp"))] + list(pieces[1:])
    tail = sum(part[rows:].astype(F32) for part in tails)
    sums = [tail[-1]] + [tail[places + j] for j in range(len(lines))]
    return pieces, sums


def sum_groups(values, turn):
    count = lax.axis_size("dp")
    listed = [(j + turn) % count for j in range(count)]
    return lax.psum(tuple(values), "dp", axis_index_groups=[listed])


class GroupSum:
    def __init__(self, arrays):
        self.arrays = [array.astype(BF16) for array in arrays]
        count = lax.axis_size("dp")
        self.bits = count.bit_length() - 1
        place = lax.axis_index("dp")
        self.own = [lax.rem(place // 2**bit, 2) for bit in range(self.bits)]
        self.orders = [list(range(1, self.bits)), list(range(1, self.bits))[::-1]]
        self.plan = [self.first]
        self.plan += [lambda *t, k=k: self.reduce(k, *t) for k in range(self.bits - 1)]
        self.plan += [lambda *t, k=k: self.spread(k, *t) for k in reversed(range(self.bits - 1))]
        self.plan += [self.last]

    def swap(self, values, bit):
        count = lax.axis_size("dp")
        return lax.ppermute(values, "dp", [(j, j ^ (1 << bit)) for j in range(count)])

    def half(self, values, which):
        rows = values.shape[0] // 2
        return lax.dynamic_slice_in_dim(values, which * rows, rows, 0)

    def first(self, *after):
        kept, away = split_rows(self.own[0], self.arrays)
        total = kept + self.swap(tie(away, *after), 0)
        rows = total.shape[0] // 2
        self.parts = [total[:rows], total[rows:]]

    def reduce(self, k, *after):
        for p in range(2):
            bit = self.orders[p][k]
            own = self.own[bit]
            arrived = self.swap(tie(self.half(self.parts[p], 1 - own), *after), bit)
            self.parts[p] = self.half(self.parts[p], own) + arrived

    def both(self, values, arrived, own):
        low = jnp.where(own == 0, values, arrived)
        high = jnp.where(own == 0, arrived, values)
        return jnp.concatenate([low, high], axis=0)

    def spread(self, k, *after):
        for p in range(2):
            bit = self.orders[p][k]
            arrived = self.swap(tie(self.parts[p], *after), bit)
            self.parts[p] = self.both(self.parts[p], arrived, self.own[bit])

    def last(self, *after):
        arrived = [self.swap(tie(part, *after), 0) for part in self.parts]
        widths = [a.shape[1] for a in self.arrays]
        self.parts = finish_rows(self.own[0], self.parts, arrived, widths)

    def step(self, *after):
        self.plan.pop(0)(*after)
        return tuple(self.parts)

    def result(self):
        while self.plan:
            self.step()
        return self.parts


def norm_backward(
    normed_grad, normed, row_values, lines, resid, inverse, gain_part, model_width, carried
):
    place = lax.axis_index("mp").astype(jnp.int32).reshape(1)
    pieces, sums = scatter_sum_rows(normed_grad, normed, row_values, *lines)
    grads = gradient_step(place, pieces, carried, resid, inverse, gain_part, model_width)
    return grads, sums


def row_product(*pairs):
    total = 0.0
    for left, right in pairs:
        total = total + jnp.sum(left.astype(F32) * right.astype(F32), axis=1)
    return total


def per_device(
    tokens,
    seq_lengths,
    gain_first,
    lin_query,
    lin_key,
    lin_value,
    lin_out,
    gain_second,
    win_query,
    win_key,
    win_value,
    win_out,
    gain_third,
    gate_weight,
    up_weight,
    down_weight,
    out_cotangent,
):
    row_count, width = tokens.shape
    count = lax.axis_size("mp")
    model_width = width * count
    rows = row_count // CHUNKS
    order = list(range(CHUNKS))
    offset = lax.axis_index("mp") * width
    places = jnp.arange(row_count, dtype=jnp.int32)
    validity = (places < seq_lengths[0, 0] + seq_lengths[0, 1]).astype(F32)
    valid = [validity[c * rows : (c + 1) * rows, None] for c in order]

    def cut(values):
        return [values[c * rows : (c + 1) * rows] for c in order]

    def join(values):
        return jnp.concatenate(values, axis=0) if len(values) > 1 else values[0]

    def part_of(gain):
        return lax.dynamic_slice_in_dim(gain, offset, width).astype(F32)

    blank = [None] * CHUNKS
    low_one, low_two, low_three = list(blank), list(blank), list(blank)
    low_two_grad, low_one_grad = list(blank), list(blank)
    place = lax.axis_index("mp").astype(jnp.int32).reshape(1)
    token_parts = cut(tokens)
    resid_zero = [t.astype(F32) for t in token_parts]
    cot_shard = [c.astype(F32) * v for c, v in zip(cut(out_cotangent), valid)]

    cot_low = join([c.astype(BF16) for c in cot_shard])
    cot_joined = lax.all_gather(cot_low, "mp", axis=1, tiled=True)
    cot_full = cut(cot_joined)
    n1, r1, lq, lk, lv, lo, lo32, lden, b1, resid_one = [list(blank) for _ in range(10)]
    for c in order:
        part = tie(token_parts[c], r1[c - 1]) if c else token_parts[c]
        n1[c], r1[c] = gather_norm(line_gather(part), gain_first)
        lq[c] = nn(n1[c], lin_query).astype(BF16)
        lk[c] = nn(n1[c], lin_key).astype(BF16)
        lv[c] = nn(n1[c], lin_value).astype(BF16)
        lo[c], lo32[c], lden[c] = linear_forward(
            c,
            seq_lengths,
            lq[c],
            lk[: c + 1],
            lv[: c + 1],
        )
        pieces = scatter_sum(block_product(lo[c], lin_out, count))
        resid_one[c], low_one[c], b1[c], _ = residual_add(place, resid_zero[c], pieces)
    n2, r2, wq, wk, wv, wo, b2, resid_two = [list(blank) for _ in range(8)]
    for c in order:
        n2[c], r2[c] = gather_norm(line_gather(low_one[c]), gain_second)
        wq[c] = nn(n2[c], win_query).astype(BF16)
        wk[c] = nn(n2[c], win_key).astype(BF16)
        wv[c] = nn(n2[c], win_value).astype(BF16)
        before = [wk[c - 1], wv[c - 1]] if c else []
        spans = seq_lengths if c else tie(seq_lengths, cot_joined)
        wo[c] = window_forward(c, spans, wq[c], wk[c], wv[c], before)
        pieces = scatter_sum(block_product(wo[c], win_out, count))
        resid_two[c], low_two[c], b2[c], _ = residual_add(place, resid_one[c], pieces)
    n3, r3, hid, dg, du, b3, resid_three, dn3, resid_two_grad = [list(blank) for _ in range(9)]
    gates, uppers = list(blank), list(blank)
    for c in order:
        n3[c], r3[c] = gather_norm(line_gather(low_two[c]), gain_third)
        gates[c] = nn(n3[c], gate_weight)
        uppers[c] = nn(n3[c], up_weight)
    def masked(values):
        return sum(jnp.sum(v * p) for v, p in zip(valid, values))

    def stat_line(*values):
        block = jnp.pad(jnp.stack(values), (0, width - len(values)))
        return jnp.tile(block, count)

    stats = stat_line(
        masked([jnp.sum(x * x, axis=1, keepdims=True) for x in resid_zero]), masked(b1), masked(b2)
    )
    sums_three, sums_two, sums_one = list(blank), list(blank), list(blank)
    for c in order:
        hid[c] = hidden_forward(gates[c], uppers[c], cot_joined if c else seq_lengths)
    for c in reversed(order):
        hid_grad = nt(cot_full[c], down_weight)
        dg[c], du[c], row_values = hidden_backward(gates[c], uppers[c], hid_grad)
        dn3[c] = nt(dg[c], gate_weight) + nt(du[c], up_weight)
        (resid_two_grad[c], low_two_grad[c]), sums_three[c] = norm_backward(
            dn3[c],
            n3[c],
            row_values[:, 0],
            (stats,),
            resid_two[c],
            r3[c],
            part_of(gain_third),
            model_width,
            cot_shard[c],
        )
    for c in order:
        partial_sum = nn(hid[c], down_weight).astype(BF16)
        branch = lax.psum_scatter(partial_sum, "mp", scatter_dimension=1, tiled=True)
        branch = branch.astype(F32)
        total = resid_two[c] + branch
        low_three[c] = total.astype(BF16)
        b3[c] = jnp.sum(branch * branch, axis=1, keepdims=True)
        resid_three[c] = jnp.sum(total * total, axis=1, keepdims=True)
    ffn_normed, ffn_hid = join(n3), join(hid)
    down_grad = tn(ffn_hid, cot_joined).astype(BF16)
    down_sums = sum_groups([down_grad], 3)
    ffn_grads = [
        tn(ffn_normed, join(dg)).astype(BF16),
        tn(ffn_normed, join(du)).astype(BF16),
    ]
    ffn_sums = sum_groups(ffn_grads, 0)
    cot_two, wdq, wdk, wdv, dn2, resid_one_grad = [list(blank) for _ in range(6)]
    carry = []
    for c in reversed(order):
        shard = tie(low_two_grad[c], *(ffn_grads if c == 0 else [down_grad]))
        cot_two[c] = gather_join(line_gather(shard))
        mixed_grad = nt(cot_two[c], win_out).astype(BF16)
        before = [wk[c - 1], wv[c - 1]] if c else []
        (wdq[c], wdk[c], wdv[c]), carry = window_backward(
            c, seq_lengths, wq[c], wk[c], wv[c], before, mixed_grad, carry
        )
        dn2[c] = nt(wdq[c], win_query) + nt(wdk[c], win_key) + nt(wdv[c], win_value)
        (resid_one_grad[c], low_one_grad[c]), sums_two[c] = norm_backward(
            dn2[c],
            n2[c],
            row_product((wdq[c], wq[c]), (wdk[c], wk[c]), (wdv[c], wv[c])),
            (),
            resid_one[c],
            r2[c],
            part_of(gain_second),
            model_width,
            resid_two_grad[c],
        )
    win_normed = join(n2)
    win_grads = [
        tn(win_normed, join(wdq)).astype(BF16),
        tn(win_normed, join(wdk)).astype(BF16),
        tn(win_normed, join(wdv)).astype(BF16),
        tn(join(wo), join(cot_two)).astype(BF16),
    ]
    win_sums = sum_groups(win_grads, 1)
    cot_one, ldq, ldk, ldv, dn1, tokens_grad = [list(blank) for _ in range(6)]
    pending = [[] for _ in order]
    for c in reversed(order):
        shard = low_one_grad[c] if c else tie(low_one_grad[c], *win_grads)
        cot_one[c] = gather_join(line_gather(shard))
        mixed_grad = nt(cot_one[c], lin_out)
        carry = []
        if pending[c]:
            carry = [functools.reduce(jnp.add, [p[s] for p in pending[c]]) for s in (0, 1)]
        (ldq[c], ldk[c], ldv[c]), back = linear_backward(
            c,
            seq_lengths,
            lq[c],
            lk[: c + 1],
            lv[: c + 1],
            mixed_grad,
            lo32[c],
            lden[c],
            carry,
        )
        for earlier, pair in enumerate(back):
            pending[earlier].append(pair)
        dn1[c] = nt(ldq[c], lin_query) + nt(ldk[c], lin_key) + nt(ldv[c], lin_value)
        stats = stat_line(masked(b3), masked(resid_three))
        (tokens_grad[c], _), sums_one[c] = norm_backward(
            dn1[c],
            n1[c],
            row_product((ldq[c], lq[c]), (ldk[c], lk[c]), (ldv[c], lv[c])),
            () if c else (stats,),
            resid_zero[c],
            r1[c],
            part_of(gain_first),
            model_width,
            resid_one_grad[c],
        )
    lin_normed = join(n1)
    lin_grads = [
        tn(lin_normed, join(ldq)).astype(BF16),
        tn(lin_normed, join(ldk)).astype(BF16),
        tn(lin_normed, join(ldv)).astype(BF16),
        tn(join(lo), join(cot_one)).astype(BF16),
    ]
    lin_sums = sum_groups(lin_grads, 2)
    small = lax.psum(
        jnp.concatenate(
            [sum(part[0] for part in sums) for sums in (sums_one, sums_two, sums_three)]
            + [sums_three[0][1][:3], sums_one[0][1][:2], jnp.sum(validity)[None]]
        ),
        "dp",
    )
    gain_grads = [
        small[s * width : (s + 1) * width] / part_of(gain)
        for s, gain in enumerate((gain_first, gain_second, gain_third))
    ]
    rms_values = jnp.sqrt(small[3 * width : -1] / (small[-1] * model_width))
    down_sums = [tie(v.astype(F32), wdq[0]) for v in down_sums]
    ffn_sums = [tie(v.astype(F32), ldq[1]) for v in ffn_sums]
    win_sums = [tie(v.astype(F32), tokens_grad[0]) for v in win_sums]
    lin_sums = [v.astype(F32) for v in lin_sums]
    return (
        join(low_three),
        join(tokens_grad),
        gain_grads[0],
        lin_sums[0],
        lin_sums[1],
        lin_sums[2],
        lin_sums[3],
        gain_grads[1],
        win_sums[0],
        win_sums[1],
        win_sums[2],
        win_sums[3],
        gain_grads[2],
        ffn_sums[0],
        ffn_sums[1],
        down_sums[0],
        rms_values,
    )


def solution(mesh):
    in_specs = (
        P("dp", "mp"),
        P("dp", None),
        P(),
        P(None, "mp"),
        P(None, "mp"),
        P(None, "mp"),
        P("mp", None),
        P(),
        P(None, "mp"),
        P(None, "mp"),
        P(None, "mp"),
        P("mp", None),
        P(),
        P(None, "mp"),
        P(None, "mp"),
        P("mp", None),
        P("dp", "mp"),
    )
    out_specs = (
        P("dp", "mp"),
        P("dp", "mp"),
        P("mp"),
        P(None, "mp"),
        P(None, "mp"),
        P(None, "mp"),
        P("mp", None),
        P("mp"),
        P(None, "mp"),
        P(None, "mp"),
        P(None, "mp"),
        P("mp", None),
        P("mp"),
        P(None, "mp"),
        P(None, "mp"),
        P("mp", None),
        P(),
    )
    return jax.shard_map(
        per_device, mesh=mesh, in_specs=in_specs, out_specs=out_specs, check_vma=False
    )
```
